128 devices in a mesh: az: 16 (over x_hi, y, core), rg: 8 (over z, x_lo).
Axes of the slice: x: 4 (x_hi: 2, x_lo: 2; x = x_hi * 2 + x_lo), y: 4, z: 4, core: 2. Of those that a mesh axis runs over, the one named last changes fastest.
Arguments:
- reference_slc: bfloat16 [2, 1536, 24576], P(None, 'az', 'rg'), may hold values from -6 to 6
- secondary_slc: bfloat16 [2, 1536, 24576], P(None, 'az', 'rg'), may hold values from -6 to 6
- chip_offsets: int32 [2, 16, 768], P(None, 'az', 'rg'), may hold values from -80 to 80, as said below
- src_row: int32 [1536], replicated, may hold values from 0 to 1535, as said below
- line_owner: int32 [1536], replicated, may hold values from 0 to 127, as said below
- band_start: int32 [24576], replicated, may hold values from -64 to 24631, as said below
- band_taps: bfloat16 [8, 24576], replicated, may hold values from -2.09375 to 2.09375
Outputs:
- est_offsets: float32 [2, 16, 768], P(None, 'az', 'rg')
- resampled: bfloat16 [2, 4096, 24576], P(None, ('az', 'rg'))
The draws below stay inside these ranges and needn't reach their ends.
Inputs may be any that keep to these rules, and one draw needn't show every extreme that they name: chip_offsets[0] lies within -80 and 80, chip_offsets[1] within -48 and 48. `src_row`: the source row of line i lies within 8 rows of i. `line_owner`: for every owner and every azimuth tile, at most 2 lines of that owner take their source rows from that tile, and an owner holds at most 32 lines; both bounds are met in every draw. band_start[j] lies within j - 64 and j + 56.
All inputs are finite; a program needn't handle non-finite values.
Results may differ from the reference program's by a relative error of at most 0.008.
Values may be sent and summed in bfloat16 or wider, within the bound.
No kernel may reach another device: no remote copies, remote signals or barrier semaphores. Data moves between devices by JAX's collectives and lax.ppermute only.
A program may use at most 128 MiB of HBM per device.

```python
import math
import jax
import jax.numpy as jnp
from jax import lax

CHIP_LEN = 64
OVERSAMPLE = 16
LAG_COUNT = 48
TAP_COUNT = 8
SPACING = 32
MARGIN = 64
MAX_SHIFT = 8
LINES_DEV = 96
TILES_AZ = 16
ALL_LINES = 1536
ALL_COLUMNS = 24576
CHIPS_ALL = 768
REF_RIM = 16
AZ_REACH = 80
RG_REACH = 48
OWNERS = 128
BUSY_OWNERS = 16
CALM_OWNERS = 112
PAIR_CAP = 2
OWNER_CAP = 32


def plan_lines(key):
    base = jax.random.fold_in(key, 71)
    shift_key = jax.random.fold_in(base, 1)
    order_key = jax.random.fold_in(base, 2)
    turn_key = jax.random.fold_in(base, 3)
    line_ids = jnp.arange(ALL_LINES, dtype=jnp.int32)
    line_moves = jax.random.randint(shift_key, (ALL_LINES,), -MAX_SHIFT, MAX_SHIFT + 1)
    line_moves = line_moves.at[0].set(-MAX_SHIFT).at[ALL_LINES - 1].set(MAX_SHIFT)
    source = jnp.clip(line_ids + line_moves, 0, ALL_LINES - 1)
    tile_of = source // LINES_DEV
    tile_hot = (tile_of[:, None] == jnp.arange(TILES_AZ, dtype=jnp.int32)[None, :]).astype(jnp.int32)
    tile_rank = jnp.sum(jnp.cumsum(tile_hot, axis=0) * tile_hot, axis=1) - 1
    shuffled = jax.random.permutation(order_key, OWNERS)
    heavy_set = shuffled[:BUSY_OWNERS]
    light_set = shuffled[BUSY_OWNERS:]
    light_turn = jax.random.randint(turn_key, (TILES_AZ,), 0, CALM_OWNERS)
    heavy_pick = heavy_set[jnp.minimum(tile_rank // PAIR_CAP, BUSY_OWNERS - 1)]
    light_pick = light_set[(tile_rank - PAIR_CAP * BUSY_OWNERS + light_turn[tile_of]) % CALM_OWNERS]
    owners = jnp.where(tile_rank < PAIR_CAP * BUSY_OWNERS, heavy_pick, light_pick)
    return (source.astype(jnp.int32), owners.astype(jnp.int32))


def draw_src_row(key, part):
    return plan_lines(key)[0]


def draw_line_owner(key, part):
    return plan_lines(key)[1]


def draw_chip_offsets(key, part):
    az_key = jax.random.fold_in(key, 5)
    rg_key = jax.random.fold_in(key, 6)
    az_part = jax.random.randint(az_key, (TILES_AZ, CHIPS_ALL), -AZ_REACH, AZ_REACH + 1)
    az_part = az_part.at[0, 0].set(-AZ_REACH).at[TILES_AZ - 1, CHIPS_ALL - 1].set(AZ_REACH)
    rg_part = jax.random.randint(rg_key, (TILES_AZ, CHIPS_ALL), -RG_REACH, RG_REACH + 1)
    rg_part = rg_part.at[0, 1].set(-RG_REACH).at[TILES_AZ - 1, 0].set(RG_REACH)
    return jnp.stack([az_part, rg_part]).astype(jnp.int32)


def draw_band_start(key, part):
    jitter = jax.random.randint(jax.random.fold_in(key, 9), (ALL_COLUMNS,), -MARGIN, MARGIN - TAP_COUNT + 1)
    jitter = jitter.at[0].set(-MARGIN).at[ALL_COLUMNS - 1].set(MARGIN - TAP_COUNT)
    return (jnp.arange(ALL_COLUMNS, dtype=jnp.int32) + jitter).astype(jnp.int32)


def levels(rng, shape, shards, smallest, top_value):
    def one(axis_at, parts):
        steps = jax.random.uniform(jax.random.fold_in(jax.random.fold_in(rng, 6), axis_at), (parts,), jnp.float32, smallest / len(shards), top_value / len(shards))
        return jnp.repeat(jnp.exp(steps), shape[axis_at] // parts).reshape((-1,) + (1,) * (len(shape) - axis_at - 1))

    gain = one(*shards[0])
    for cut in shards[1:]:
        gain = gain * one(*cut)
    return gain


def centred(own_key, shape, spread, bound, shards=(), held_as=jnp.bfloat16):
    result = spread * jax.random.normal(own_key, shape, jnp.float32)
    if shards:
        result = result * levels(own_key, shape, shards, -0.22, 0.18)
    return jnp.clip(result, -bound, bound).astype(held_as)


def setup_inputs(seed: int = 0) -> dict:
    arg_keys = jax.random.split(jax.random.key(seed), 8)
    return {
        "reference_slc": centred(arg_keys[0], (2, ALL_LINES, ALL_COLUMNS), 1.0, 6.0, ((1, 16), (2, 8))),
        "secondary_slc": centred(arg_keys[1], (2, ALL_LINES, ALL_COLUMNS), 1.0, 6.0, ((1, 16), (2, 8))),
        "chip_offsets": draw_chip_offsets(jax.random.fold_in(arg_keys[7], 71), 0),
        "src_row": draw_src_row(jax.random.fold_in(arg_keys[7], 71), 0),
        "line_owner": draw_line_owner(jax.random.fold_in(arg_keys[7], 71), 0),
        "band_start": draw_band_start(jax.random.fold_in(arg_keys[7], 71), 0),
        "band_taps": centred(arg_keys[6], (TAP_COUNT, ALL_COLUMNS), 0.35, 2.09375),
    }


PHASE_RATE = 2.0
EPS = 1e-06

def make_tables():
    indices = jnp.arange(CHIP_LEN, dtype=jnp.int32)
    product = indices[:, None] * indices[None, :] % CHIP_LEN
    angles = -2.0 * math.pi / CHIP_LEN * product.astype(jnp.float32)
    scaling = 1.0 / math.sqrt(CHIP_LEN)
    four_re = (jnp.cos(angles) * scaling).astype(jnp.bfloat16)
    four_im = (jnp.sin(angles) * scaling).astype(jnp.bfloat16)
    lag_steps = jnp.arange(LAG_COUNT, dtype=jnp.int32) - LAG_COUNT // 2
    frequency = jnp.where(indices < CHIP_LEN // 2, indices, indices - CHIP_LEN)
    phase_turns = lag_steps[:, None] * frequency[None, :] % (OVERSAMPLE * CHIP_LEN)
    lifted = 2.0 * math.pi / (OVERSAMPLE * CHIP_LEN) * phase_turns.astype(jnp.float32)
    lift_re = (jnp.cos(lifted) * scaling).astype(jnp.bfloat16)
    lift_im = (jnp.sin(lifted) * scaling).astype(jnp.bfloat16)
    lag_values = lag_steps.astype(jnp.float32) / OVERSAMPLE
    return (four_re, four_im, lift_re, lift_im, lag_values)

def rounded(values):
    return lax.optimization_barrier(values.astype(jnp.bfloat16)).astype(jnp.float32)

def spectrum(chip_re, chip_im, four_re, four_im):
    half_re = rounded(jnp.einsum('px,xgy->pgy', four_re, chip_re) - jnp.einsum('px,xgy->pgy', four_im, chip_im))
    half_im = rounded(jnp.einsum('px,xgy->pgy', four_re, chip_im) + jnp.einsum('px,xgy->pgy', four_im, chip_re))
    spec_re = jnp.einsum('pgy,qy->pgq', half_re, four_re) - jnp.einsum('pgy,qy->pgq', half_im, four_im)
    spec_im = jnp.einsum('pgy,qy->pgq', half_re, four_im) + jnp.einsum('pgy,qy->pgq', half_im, four_re)
    return (spec_re, spec_im)

def reference(reference_slc, secondary_slc, chip_offsets, src_row, line_owner, band_start, band_taps):
    four_re, four_im, lift_re, lift_im, lag_values = make_tables()
    four_re = four_re.astype(jnp.float32)
    four_im = four_im.astype(jnp.float32)
    lift_re = lift_re.astype(jnp.float32)
    lift_im = lift_im.astype(jnp.float32)
    sec_pad = jnp.pad(secondary_slc, ((0, 0), (MARGIN, MARGIN), (MARGIN, MARGIN)))
    first_row = LINES_DEV // 2 - CHIP_LEN // 2
    block_total = CHIPS_ALL + CHIP_LEN // SPACING - 1

    def per_tile(tile_index):
        row_first = (tile_index * LINES_DEV + first_row).astype(jnp.int32)
        ref_rows = lax.dynamic_slice(reference_slc, (jnp.int32(0), row_first, jnp.int32(0)), (2, CHIP_LEN, ALL_COLUMNS))
        offsets = lax.dynamic_index_in_dim(chip_offsets, tile_index, axis=1, keepdims=False)
        padded = jnp.pad(ref_rows, ((0, 0), (0, 0), (REF_RIM, REF_RIM)))
        blocks = padded.reshape(2, CHIP_LEN, block_total, SPACING)
        ref_chips = jnp.concatenate([blocks[:, :, start_block:start_block + CHIPS_ALL] for start_block in range(CHIP_LEN // SPACING)], axis=3)
        row_start = (row_first + offsets[0] + MARGIN).astype(jnp.int32)
        col_start = (SPACING * jnp.arange(CHIPS_ALL, dtype=jnp.int32) - REF_RIM + offsets[1] + MARGIN).astype(jnp.int32)

        def cut_chip(row_first_one, col_first_one):
            return lax.dynamic_slice(sec_pad, (jnp.int32(0), row_first_one, col_first_one), (2, CHIP_LEN, CHIP_LEN))
        sec_chips = jax.vmap(cut_chip)(row_start, col_start).transpose(1, 2, 0, 3)
        ref_re, ref_im = spectrum(ref_chips[0].astype(jnp.float32), ref_chips[1].astype(jnp.float32), four_re, four_im)
        sec_re, sec_im = spectrum(sec_chips[0].astype(jnp.float32), sec_chips[1].astype(jnp.float32), four_re, four_im)
        cross_re = rounded(ref_re * sec_re + ref_im * sec_im)
        cross_im = rounded(ref_im * sec_re - ref_re * sec_im)
        mid_re = rounded(jnp.einsum('pgq,vq->pgv', cross_re, lift_re) - jnp.einsum('pgq,vq->pgv', cross_im, lift_im))
        mid_im = rounded(jnp.einsum('pgq,vq->pgv', cross_re, lift_im) + jnp.einsum('pgq,vq->pgv', cross_im, lift_re))
        corr_re = jnp.einsum('up,pgv->ugv', lift_re, mid_re) - jnp.einsum('up,pgv->ugv', lift_im, mid_im)
        corr_im = jnp.einsum('up,pgv->ugv', lift_re, mid_im) + jnp.einsum('up,pgv->ugv', lift_im, mid_re)
        energy = corr_re * corr_re + corr_im * corr_im
        weight_map = energy * energy
        totals = lax.optimization_barrier(jnp.sum(weight_map, axis=(0, 2))) + EPS
        cent_az = jnp.einsum('u,ugv->g', lag_values, weight_map) / totals
        cent_rg = jnp.einsum('v,ugv->g', lag_values, weight_map) / totals
        return jnp.stack([offsets[0].astype(jnp.float32) + cent_az, offsets[1].astype(jnp.float32) + cent_rg])
    est_tiles = lax.map(per_tile, jnp.arange(TILES_AZ, dtype=jnp.int32))
    est_offsets = jnp.transpose(est_tiles, (1, 0, 2))
    line_data = jnp.take(secondary_slc, src_row, axis=1)
    padded_lines = jnp.pad(line_data, ((0, 0), (0, 0), (MARGIN, MARGIN)))
    summed = jnp.zeros((2, ALL_LINES, ALL_COLUMNS), jnp.float32)
    for tap_index in range(TAP_COUNT):
        picked = jnp.take(padded_lines, (band_start + tap_index + MARGIN).astype(jnp.int32), axis=2).astype(jnp.float32)
        summed = summed + picked * band_taps[tap_index].astype(jnp.float32)[None, None, :]
    field_rows = jnp.take(est_offsets[0], (src_row // LINES_DEV).astype(jnp.int32), axis=0)
    phase_angle = PHASE_RATE * jnp.repeat(field_rows, SPACING, axis=1)
    cosine = jnp.cos(phase_angle)
    sine_part = jnp.sin(phase_angle)
    line_re = summed[0] * cosine + summed[1] * sine_part
    line_im = summed[1] * cosine - summed[0] * sine_part
    lines_done = jnp.stack([line_re, line_im]).astype(jnp.bfloat16)
    line_ids = jnp.arange(ALL_LINES, dtype=jnp.int32)
    same_owner = line_owner[:, None] == line_owner[None, :]
    earlier = line_ids[:, None] > line_ids[None, :]
    own_rank = lax.optimization_barrier(jnp.sum((same_owner & earlier).astype(jnp.int32), axis=1))
    position = (line_owner * OWNER_CAP + own_rank).astype(jnp.int32)
    resampled = jnp.zeros((2, OWNERS * OWNER_CAP, ALL_COLUMNS), jnp.bfloat16).at[:, position, :].set(lines_done)
    return (est_offsets, resampled)
```

```python
import functools
import math

import jax
import jax.numpy as jnp
import ml_dtypes
import numpy as np
from jax import lax
from jax.experimental import pallas as pl
from jax.experimental.pallas import tpu as pltpu
from jax.sharding import PartitionSpec as P

CHIP_LEN = 64
OVERSAMPLE = 16
LAG_COUNT = 48
TAP_COUNT = 8
SPACING = 32
MARGIN = 64
PHASE_RATE = 2.0
EPS = 1e-06

TILES = 16
PIECES = 8
OWNERS = 128
LINES = 96
COLS = 3072
ALL_LINES = 1536
CHIPS = 96
PAIRS = CHIPS // 2
OWNER_CAP = 32
FIRST_ROW = 16
ROWS = LINES + 2 * MARGIN
WINDOWS = COLS // 128 + 2
HALF = WINDOWS // 2
WIDTH = HALF * 128
LINE_SPAN = 256
SCRATCH_BLOCKS = 27
GROUP = 4
BOTH = ("az", "rg")
BF = jnp.bfloat16
F32 = jnp.float32


def numpy_tables():
    ids = np.arange(CHIP_LEN)
    angles = -2.0 * math.pi / CHIP_LEN * (ids[:, None] * ids[None, :] % CHIP_LEN)
    scale = 1.0 / math.sqrt(CHIP_LEN)

    def low(values):
        return values.astype(np.float32).astype(ml_dtypes.bfloat16).astype(np.float32)

    four = (low(np.cos(angles) * scale), low(np.sin(angles) * scale))
    steps = np.arange(LAG_COUNT) - LAG_COUNT // 2
    freq = np.where(ids < CHIP_LEN // 2, ids, ids - CHIP_LEN)
    turns = steps[:, None] * freq[None, :] % (OVERSAMPLE * CHIP_LEN)
    lifted = 2.0 * math.pi / (OVERSAMPLE * CHIP_LEN) * turns
    lift = (low(np.cos(lifted) * scale), low(np.sin(lifted) * scale))
    return four, lift


def kernel_tables():
    four, lift = numpy_tables()

    def stacked(re, im):
        return np.block([[re, -im], [im, re]])

    def paired(re, im, starts):
        out = np.zeros((2, 128, 2, 2, 64), np.float32)
        count = re.shape[0]
        for chip, first in enumerate(starts):
            rows = slice(first, first + CHIP_LEN)
            out[0, rows, 0, chip, :count] = re.T
            out[0, rows, 1, chip, :count] = im.T
            out[1, rows, 0, chip, :count] = -im.T
            out[1, rows, 1, chip, :count] = re.T
        return out.reshape(256, 256)

    return tuple(
        jnp.asarray(t.astype(ml_dtypes.bfloat16))
        for t in (
            stacked(*four),
            paired(*four, (0, 32)),
            paired(*four, (0, 64)),
            paired(*lift, (0, 64)),
            stacked(*lift),
        )
    )


def iota(shape, dim):
    return lax.broadcasted_iota(jnp.int32, shape, dim)


def pack_kernel(
    place_ref, sec_ref, start_ref, taps_ref, src_ref, own_ref, out_ref, shift_ref, res_ref, pick_ref
):
    az = place_ref[0]
    rg = place_ref[1]

    line_first = jnp.minimum(jnp.maximum(az * LINES - 8, 0) // 128 * 128, ALL_LINES - LINE_SPAN)
    span = pl.ds(pl.multiple_of(line_first, 128), LINE_SPAN)
    local = src_ref[:, span] - az * LINES
    owner = own_ref[:, span]
    here = (local >= 0) & (local < LINES)
    tagged = jnp.where(here, owner, -1).astype(F32)
    tagged_col = jnp.transpose(jnp.broadcast_to(tagged, (128, LINE_SPAN)))
    tagged_col = jnp.concatenate([tagged_col, tagged_col], axis=1)
    square = (LINE_SPAN, LINE_SPAN)
    earlier = iota(square, 0) < iota(square, 1)
    same = (tagged_col == tagged) & earlier
    rank = jnp.sum(jnp.where(same, 1.0, 0.0), axis=0, keepdims=True)
    slot = jnp.where(here, tagged * 2.0 + rank, -1.0)
    marked = jnp.where(here, local + 1, 0).astype(F32)
    marked_col = jnp.transpose(jnp.broadcast_to(marked, (128, LINE_SPAN))).astype(BF)
    for first in range(0, 1024, 256):
        ids = iota((256, LINE_SPAN), 0) + first
        wanted = ((ids >> 3) * 2 + ((ids >> 1) & 1)).astype(F32)
        hot = jnp.where(slot == wanted, 1.0, 0.0).astype(BF)
        found = jnp.dot(hot, marked_col, preferred_element_type=F32).astype(jnp.int32)
        ids = iota((256, 128), 0) + first
        base = ((ids >> 2) & 1) * (2 * LINES) + (ids & 1) * LINES - 1
        target = jnp.where(found > 0, found + base, -1)
        for block in range(3):
            lanes = iota((256, 128), 1) + block * 128
            pick_ref[first : first + 256, block * 128 : (block + 1) * 128] = jnp.where(
                lanes == target, 1.0, 0.0
            ).astype(BF)

    lane = iota((2 * LINES, 128), 1)
    none = jnp.zeros((2 * LINES, 128), F32)
    shift_ref[:, 0:128] = none.astype(BF)
    shift_ref[:, 26 * 128 : 27 * 128] = none.astype(BF)

    def moved(left, right):
        return pltpu.roll(jnp.where(lane >= 64, left, right), 64, 1).astype(BF)

    shift_ref[:, 128:256] = moved(none, sec_ref[:, 0:128].astype(F32))
    shift_ref[:, 25 * 128 : 26 * 128] = moved(sec_ref[:, COLS - 128 : COLS].astype(F32), none)

    def move(block, carry):
        at = pl.multiple_of(block * 128, 128)
        left = sec_ref[:, pl.ds(pl.multiple_of(at - 128, 128), 128)].astype(F32)
        right = sec_ref[:, pl.ds(at, 128)].astype(F32)
        shift_ref[:, pl.ds(pl.multiple_of(at + 128, 128), 128)] = moved(left, right)
        return carry

    lax.fori_loop(1, COLS // 128, move, 0)

    tap_row = iota((256, 128), 0)
    for half in range(2):

        def window(step, carry):
            at = step + half * HALF
            block = jnp.clip(rg * (COLS // 128) + at - 1, 0, PIECES * (COLS // 128) - 1)
            start = start_ref[pl.ds(block, 1), :] - block * 128 + MARGIN
            taps = taps_ref[:, pl.ds(pl.multiple_of(block * 128, 128), 128)].astype(F32)
            offset = tap_row - start
            band = jnp.zeros((256, 128), F32)
            for tap in range(TAP_COUNT):
                band = jnp.where(offset == tap, taps[tap : tap + 1, :], band)
            lines = shift_ref[:, pl.ds(pl.multiple_of(at * 128, 128), 256)]
            summed = jnp.dot(lines, band.astype(BF), preferred_element_type=F32)
            res_ref[
                half * 2 * LINES : (half + 1) * 2 * LINES,
                pl.ds(pl.multiple_of(step * 128, 128), 128),
            ] = summed.astype(BF)
            return carry

        lax.fori_loop(0, HALF, window, 0)

    def send(step, carry):
        at = pl.ds(pl.multiple_of(step * 128, 128), 128)
        out_ref[:, at] = jnp.dot(
            pick_ref[...], res_ref[:, at], preferred_element_type=F32
        ).astype(BF)
        return carry

    lax.fori_loop(0, HALF, send, 0)


def pack_lines(place, sec, starts, taps, src, own):
    smem = pl.BlockSpec(memory_space=pltpu.SMEM)
    vmem = pl.BlockSpec(memory_space=pltpu.VMEM)
    return pl.pallas_call(
        pack_kernel,
        out_shape=jax.ShapeDtypeStruct((OWNERS * 8, WIDTH), BF),
        in_specs=[smem] + [vmem] * 5,
        out_specs=vmem,
        scratch_shapes=[
            pltpu.VMEM((2 * LINES, SCRATCH_BLOCKS * 128), BF),
            pltpu.VMEM((4 * LINES, WIDTH), BF),
            pltpu.VMEM((OWNERS * 8, 4 * LINES), BF),
        ],
        compiler_params=pltpu.CompilerParams(vmem_limit_bytes=40 * 2**20),
        cost_estimate=pl.CostEstimate(
            flops=2 * 10**9, bytes_accessed=6 * 10**6, transcendentals=0
        ),
        name="pack_lines",
    )(place, sec, starts, taps, src, own)


def estimate_kernel(
    off_ref,
    offv_ref,
    ref_ref,
    sec_ref,
    up_ref,
    down_ref,
    left_ref,
    right_ref,
    fwd_ref,
    wref_ref,
    wsec_ref,
    wlift_ref,
    lift_ref,
    est_ref,
    msg_ref,
    rcols_ref,
    scols_ref,
    chips_ref,
    half_ref,
    tot_ref,
    mom_ref,
):
    for part in range(2):
        rows = slice(part * CHIP_LEN, (part + 1) * CHIP_LEN)
        rcols_ref[rows, 0:128] = left_ref[part, 0:CHIP_LEN, :]
        rcols_ref[rows, 128 : 128 + COLS] = ref_ref[part, FIRST_ROW : FIRST_ROW + CHIP_LEN, :]
        rcols_ref[rows, 128 + COLS : 256 + COLS] = right_ref[part, 0:CHIP_LEN, :]
        rows = slice(part * ROWS, (part + 1) * ROWS)
        scols_ref[0, rows, :] = left_ref[part, CHIP_LEN:, :].astype(F32)
        scols_ref[SCRATCH_BLOCKS - 2, rows, :] = right_ref[part, CHIP_LEN:, :].astype(F32)
        scols_ref[SCRATCH_BLOCKS - 1, rows, :] = jnp.zeros((ROWS, 128), F32)

    def widen(block, carry):
        at = pl.ds(pl.multiple_of(block * 128, 128), 128)
        to = block + 1
        for part in range(2):
            base = part * ROWS
            own = base + MARGIN
            scols_ref[to, base:own, :] = up_ref[part, :, at].astype(F32)
            scols_ref[to, own : own + LINES, :] = sec_ref[part, :, at].astype(F32)
            scols_ref[to, own + LINES : base + ROWS, :] = down_ref[part, :, at].astype(F32)
        return carry

    lax.fori_loop(0, COLS // 128, widen, 0)

    lane = iota((CHIP_LEN, 128), 1)
    lane_all = iota((2 * CHIP_LEN, 128), 1)

    def cut(pair, carry):
        col = pair * 64 + 112
        at = pl.multiple_of((col >> 7) * 128, 128)
        turn = col & 127
        near = rcols_ref[:, pl.ds(at, 128)].astype(F32)
        far = rcols_ref[:, pl.ds(pl.multiple_of(at + 128, 128), 128)].astype(F32)
        both = pltpu.roll(jnp.where(lane_all >= turn, near, far), (128 - turn) & 127, 1)
        to = pl.multiple_of(pair * 128, 128)
        chips_ref[:, pl.ds(to, 128)] = both.astype(BF)
        for part in range(2):
            found = []
            for side in range(2):
                chip = pair * 2 + side
                row = off_ref[0, chip] + (FIRST_ROW + MARGIN + part * ROWS)
                col = chip * SPACING + off_ref[1, chip] + 112
                block = col >> 7
                turn = col & 127
                near = scols_ref[block, pl.ds(row, CHIP_LEN), :]
                far = scols_ref[block + 1, pl.ds(row, CHIP_LEN), :]
                found.append(
                    pltpu.roll(
                        jnp.where(lane >= turn, near, far), (128 + side * 64 - turn) & 127, 1
                    )
                )
            chips_ref[
                part * CHIP_LEN : (part + 1) * CHIP_LEN,
                pl.ds(pl.multiple_of(to + CHIPS * 64, 128), 128),
            ] = jnp.where(lane < 64, found[0], found[1]).astype(BF)
        return carry

    lax.fori_loop(0, PAIRS, cut, 0)

    def first_pass(step, carry):
        at = pl.ds(pl.multiple_of(step * 512, 512), 512)
        half_ref[:, at] = jnp.dot(
            fwd_ref[...], chips_ref[:, at], preferred_element_type=F32
        ).astype(BF)
        return carry

    lax.fori_loop(0, CHIPS * 128 // 512, first_pass, 0)

    lag_row = (iota((LAG_COUNT, 128), 0) - LAG_COUNT // 2).astype(F32) / OVERSAMPLE

    def correlate(step, carry):
        def gathered(base):
            rows = []
            for member in range(GROUP):
                at = pl.ds(pl.multiple_of(base + (step * GROUP + member) * 128, 128), 128)
                rows.append(
                    jnp.concatenate(
                        [half_ref[0:CHIP_LEN, at], half_ref[CHIP_LEN : 2 * CHIP_LEN, at]], axis=1
                    )
                )
            return jnp.concatenate(rows, axis=0)

        spec_ref = jnp.dot(gathered(0), wref_ref[...], preferred_element_type=F32)
        spec_sec = jnp.dot(gathered(CHIPS * 64), wsec_ref[...], preferred_element_type=F32)
        rr, ri = spec_ref[:, :128], spec_ref[:, 128:]
        sr, si = spec_sec[:, :128], spec_sec[:, 128:]
        cross = jnp.concatenate([rr * sr + ri * si, ri * sr - rr * si], axis=1).astype(BF)
        middle = jnp.dot(cross, wlift_ref[...], preferred_element_type=F32).astype(BF)
        columns = [
            jnp.concatenate(
                [
                    middle[m * CHIP_LEN : (m + 1) * CHIP_LEN, :128],
                    middle[m * CHIP_LEN : (m + 1) * CHIP_LEN, 128:],
                ],
                axis=0,
            )
            for m in range(GROUP)
        ]
        corr = jnp.dot(
            lift_ref[...], jnp.concatenate(columns, axis=1), preferred_element_type=F32
        )
        for m in range(GROUP):
            re = corr[:LAG_COUNT, m * 128 : (m + 1) * 128]
            im = corr[LAG_COUNT:, m * 128 : (m + 1) * 128]
            energy = re * re + im * im
            weight = energy * energy
            row = pl.ds(step * GROUP + m, 1)
            tot_ref[row, :] = jnp.sum(weight, axis=0, keepdims=True)
            mom_ref[row, :] = jnp.sum(weight * lag_row, axis=0, keepdims=True)
        return carry

    lax.fori_loop(0, PAIRS // GROUP, correlate, 0)

    wide = (PAIRS, 128)
    lanes = iota(wide, 1)
    total = tot_ref[...]
    moment = mom_ref[...]
    lag_lane = ((lanes & 63) - LAG_COUNT // 2).astype(F32) / OVERSAMPLE
    sides = []
    for side in range(2):
        mask = (lanes < 64) if side == 0 else (lanes >= 64)

        def over(values):
            return jnp.sum(jnp.where(mask, values, 0.0), axis=1, keepdims=True)

        whole = over(total) + EPS
        sides.append((over(moment) / whole, over(total * lag_lane) / whole))
    own = (lanes >> 1) == iota(wide, 0)
    even = (lanes & 1) == 0

    def spread(which):
        values = jnp.where(even, sides[0][which], sides[1][which])
        return jnp.sum(jnp.where(own, values, 0.0), axis=0, keepdims=True)

    offsets = offv_ref[...].astype(F32)
    est_az = offsets[0:1, :] + spread(0)
    est_rg = offsets[1:2, :] + spread(1)
    est_ref[0:1, :] = est_az
    est_ref[1:2, :] = est_rg
    angle = PHASE_RATE * est_az
    cosine = jnp.cos(angle)
    sine = jnp.sin(angle)
    cos_hi = cosine.astype(BF).astype(F32)
    sin_hi = sine.astype(BF).astype(F32)
    kind = iota((8, 128), 0)
    message = jnp.where(
        kind == 0,
        cos_hi,
        jnp.where(
            kind == 1,
            cosine - cos_hi,
            jnp.where(kind == 2, sin_hi, jnp.where(kind == 3, sine - sin_hi, 0.0)),
        ),
    ).astype(BF)
    for owner in range(OWNERS):
        msg_ref[owner] = message


def estimate(off, offv, ref, sec, up, down, left, right):
    smem = pl.BlockSpec(memory_space=pltpu.SMEM)
    vmem = pl.BlockSpec(memory_space=pltpu.VMEM)
    return pl.pallas_call(
        estimate_kernel,
        out_shape=(
            jax.ShapeDtypeStruct((2, 128), F32),
            jax.ShapeDtypeStruct((OWNERS, 8, 128), BF),
        ),
        in_specs=[smem] + [vmem] * 12,
        out_specs=(vmem, vmem),
        scratch_shapes=[
            pltpu.VMEM((2 * CHIP_LEN, SCRATCH_BLOCKS * 128), BF),
            pltpu.VMEM((SCRATCH_BLOCKS, 2 * ROWS, 128), F32),
            pltpu.VMEM((2 * CHIP_LEN, CHIPS * 128), BF),
            pltpu.VMEM((2 * CHIP_LEN, CHIPS * 128), BF),
            pltpu.VMEM((PAIRS, 128), F32),
            pltpu.VMEM((PAIRS, 128), F32),
        ],
        compiler_params=pltpu.CompilerParams(vmem_limit_bytes=48 * 2**20),
        cost_estimate=pl.CostEstimate(
            flops=6 * 10**9, bytes_accessed=20 * 10**6, transcendentals=0
        ),
        name="estimate",
    )(off, offv, ref, sec, up, down, left, right, *kernel_tables())


def place_kernel(pick_ref, sel_ref, msg_ref, arr_ref, prev_ref, next_ref, out_ref):
    piece = pl.program_id(0)
    pick = pick_ref[...]
    turned = jnp.dot(sel_ref[...], msg_ref[...].reshape(128, 128), preferred_element_type=F32)
    cos_all = turned[0:32] + turned[32:64]
    sin_all = turned[64:96] + turned[96:128]
    lane = iota((OWNER_CAP, 128), 1)

    def moved(block_ref, first, last):
        return jnp.dot(
            pick, block_ref[:, 0, :, first:last].reshape(128, last - first),
            preferred_element_type=F32,
        )

    def write(block, lines):
        chip = block * 4 + (lane >> 5)
        cosine = jnp.take_along_axis(cos_all, chip, axis=1)
        sine = jnp.take_along_axis(sin_all, chip, axis=1)
        re, im = lines[:OWNER_CAP], lines[OWNER_CAP:]
        at = slice(block * 128, (block + 1) * 128)
        out_ref[0, :, at] = (re * cosine + im * sine).astype(BF)
        out_ref[1, :, at] = (im * cosine - re * sine).astype(BF)

    before = jnp.where(piece > 0, moved(prev_ref, 0, 128)[64:], 0.0)
    after = jnp.where(piece < PIECES - 1, moved(next_ref, 0, 128)[:64], 0.0)
    for first in range(0, HALF, 2):
        last = min(first + 2, HALF)
        lines = moved(arr_ref, first * 128, last * 128)
        for at in range(first, last):
            cols = slice((at - first) * 128, (at - first + 1) * 128)
            if at >= 1:
                low = lines[:64, cols]
                write(at - 1, low + before if at == 1 else low)
            if at < HALF - 1:
                high = lines[64:, cols]
                write(HALF - 1 + at, high + after if at == HALF - 2 else high)


def place_lines(pick, sel, message, arrived):
    same = pl.BlockSpec((128, 128), lambda r: (0, 0))
    block = (TILES, 1, 8, 128)
    return pl.pallas_call(
        place_kernel,
        grid=(PIECES,),
        out_shape=jax.ShapeDtypeStruct((2, OWNER_CAP, COLS * PIECES), BF),
        in_specs=[
            same,
            same,
            pl.BlockSpec(block, lambda r: (0, r, 0, 0)),
            pl.BlockSpec((TILES, 1, 8, WIDTH), lambda r: (0, r, 0, 0)),
            pl.BlockSpec(block, lambda r: (0, jnp.maximum(r - 1, 0), 0, HALF - 1)),
            pl.BlockSpec(block, lambda r: (0, jnp.minimum(r + 1, PIECES - 1), 0, 0)),
        ],
        out_specs=pl.BlockSpec((2, OWNER_CAP, COLS), lambda r: (0, 0, r)),
        compiler_params=pltpu.CompilerParams(vmem_limit_bytes=40 * 2**20),
        cost_estimate=pl.CostEstimate(
            flops=10**9, bytes_accessed=8 * 10**6, transcendentals=0
        ),
        name="place_lines",
    )(pick, sel, message, arrived, arrived, arrived)


def owner_tables(src_row, line_owner, me):
    tile = src_row // LINES
    owned = line_owner == me
    ids = jnp.arange(ALL_LINES, dtype=jnp.int32)
    before = owned[None, :] & (ids[None, :] < ids[:, None])
    rank = jnp.sum(before.astype(jnp.int32), axis=1)
    rank_tile = jnp.sum((before & (tile[None, :] == tile[:, None])).astype(jnp.int32), axis=1)
    outs = jnp.arange(OWNER_CAP, dtype=jnp.int32)
    hit = owned[None, :] & (rank[None, :] == outs[:, None])
    code = jnp.sum(jnp.where(hit, (tile * 2 + rank_tile + 1)[None, :], 0), axis=1) - 1
    rows = jnp.arange(128, dtype=jnp.int32)[:, None]
    cols = jnp.arange(128, dtype=jnp.int32)[None, :]
    slot = jnp.tile(code, 4)[:, None]
    pick = (
        (slot == (cols >> 3) * 2 + ((cols >> 1) & 1))
        & ((rows >> 6) == ((cols >> 2) & 1))
        & (((rows >> 5) & 1) == (cols & 1))
    )
    sel = (slot >= 0) & ((slot >> 1) == (cols >> 3)) & ((rows >> 5) == (cols & 7))
    return pick.astype(BF), sel.astype(BF)


def neighbours(axis, first, last):
    count = lax.axis_size(axis)
    up = [(i, i + 1) for i in range(count - 1)]
    down = [(i + 1, i) for i in range(count - 1)]
    return lax.ppermute(last, axis, up), lax.ppermute(first, axis, down)


def per_device(
    reference_slc, secondary_slc, chip_offsets, src_row, line_owner, band_start, band_taps
):
    az = lax.axis_index("az")
    rg = lax.axis_index("rg")
    place = jnp.stack([az, rg]).astype(jnp.int32)
    packed = pack_lines(
        place,
        secondary_slc.reshape(2 * LINES, COLS),
        band_start.reshape(PIECES * COLS // 128, 128),
        band_taps,
        src_row.reshape(1, ALL_LINES),
        line_owner.reshape(1, ALL_LINES),
    )
    arrived = lax.all_to_all(packed, BOTH, 0, 0, tiled=True)

    up, down = neighbours(
        "az", secondary_slc[:, :MARGIN, :], secondary_slc[:, LINES - MARGIN :, :]
    )

    def edge(cols):
        return jnp.concatenate(
            [
                reference_slc[:, FIRST_ROW : FIRST_ROW + CHIP_LEN, cols],
                up[:, :, cols],
                secondary_slc[:, :, cols],
                down[:, :, cols],
            ],
            axis=1,
        )

    left, right = neighbours("rg", edge(slice(0, 128)), edge(slice(COLS - 128, COLS)))
    off = chip_offsets[:, 0, :]
    offv = jnp.pad(off, ((0, 0), (0, 128 - CHIPS)))
    est, message = estimate(off, offv, reference_slc, secondary_slc, up, down, left, right)
    told = lax.all_to_all(message.reshape(OWNERS * 8, 128), BOTH, 0, 0, tiled=True)
    pick, sel = owner_tables(src_row, line_owner, az * PIECES + rg)
    resampled = place_lines(
        pick,
        sel,
        told.reshape(TILES, PIECES, 8, 128),
        arrived.reshape(TILES, PIECES, 8, WIDTH),
    )
    return est[:, None, :CHIPS], resampled


def solution(mesh):
    return jax.shard_map(
        per_device,
        mesh=mesh,
        in_specs=(
            P(None, "az", "rg"),
            P(None, "az", "rg"),
            P(None, "az", "rg"),
            P(),
            P(),
            P(),
            P(),
        ),
        out_specs=(P(None, "az", "rg"), P(None, BOTH, None)),
        check_vma=False,
    )
```

```python
import functools
import math

import jax
import jax.numpy as jnp
import ml_dtypes
import numpy as np
from jax import lax
from jax.experimental import pallas as pl
from jax.experimental.pallas import tpu as pltpu
from jax.sharding import PartitionSpec as P

CHIP_LEN = 64
OVERSAMPLE = 16
LAG_COUNT = 48
TAP_COUNT = 8
SPACING = 32
MARGIN = 64
PHASE_RATE = 2.0
EPS = 1e-06

TILES = 16
PIECES = 8
OWNERS = 128
LINES = 96
COLS = 3072
ALL_LINES = 1536
CHIPS = 96
PAIRS = CHIPS // 2
OWNER_CAP = 32
FIRST_ROW = 16
ROWS = LINES + 2 * MARGIN
WINDOWS = COLS // 128 + 2
HALF = WINDOWS // 2
WIDTH = HALF * 128
LINE_SPAN = 256
SCRATCH_BLOCKS = 27
GROUP = 4
BOTH = ("az", "rg")
BF = jnp.bfloat16
F32 = jnp.float32


def numpy_tables():
    ids = np.arange(CHIP_LEN)
    angles = -2.0 * math.pi / CHIP_LEN * (ids[:, None] * ids[None, :] % CHIP_LEN)
    scale = 1.0 / math.sqrt(CHIP_LEN)

    def low(values):
        return values.astype(np.float32).astype(ml_dtypes.bfloat16).astype(np.float32)

    four = (low(np.cos(angles) * scale), low(np.sin(angles) * scale))
    steps = np.arange(LAG_COUNT) - LAG_COUNT // 2
    freq = np.where(ids < CHIP_LEN // 2, ids, ids - CHIP_LEN)
    turns = steps[:, None] * freq[None, :] % (OVERSAMPLE * CHIP_LEN)
    lifted = 2.0 * math.pi / (OVERSAMPLE * CHIP_LEN) * turns
    lift = (low(np.cos(lifted) * scale), low(np.sin(lifted) * scale))
    return four, lift


def kernel_tables():
    four, lift = numpy_tables()

    def stacked(re, im):
        return np.block([[re, -im], [im, re]])

    def paired(re, im, starts):
        out = np.zeros((2, 128, 2, 2, 64), np.float32)
        count = re.shape[0]
        for chip, first in enumerate(starts):
            rows = slice(first, first + CHIP_LEN)
            out[0, rows, 0, chip, :count] = re.T
            out[0, rows, 1, chip, :count] = im.T
            out[1, rows, 0, chip, :count] = -im.T
            out[1, rows, 1, chip, :count] = re.T
        return out.reshape(256, 256)

    return tuple(
        jnp.asarray(t.astype(ml_dtypes.bfloat16))
        for t in (
            stacked(*four),
            paired(*four, (0, 32)),
            paired(*four, (0, 64)),
            paired(*lift, (0, 64)),
            stacked(*lift),
        )
    )


def iota(shape, dim):
    return lax.broadcasted_iota(jnp.int32, shape, dim)


def pack_kernel(
    place_ref, sec_ref, start_ref, taps_ref, src_ref, own_ref, out_ref, shift_ref, res_ref, pick_ref
):
    az = place_ref[0]
    rg = place_ref[1]

    line_first = jnp.minimum(jnp.maximum(az * LINES - 8, 0) // 128 * 128, ALL_LINES - LINE_SPAN)
    span = pl.ds(pl.multiple_of(line_first, 128), LINE_SPAN)
    local = src_ref[:, span] - az * LINES
    owner = own_ref[:, span]
    here = (local >= 0) & (local < LINES)
    tagged = jnp.where(here, owner, -1).astype(F32)
    tagged_col = jnp.transpose(jnp.broadcast_to(tagged, (128, LINE_SPAN)))
    tagged_col = jnp.concatenate([tagged_col, tagged_col], axis=1)
    square = (LINE_SPAN, LINE_SPAN)
    earlier = iota(square, 0) < iota(square, 1)
    same = (tagged_col == tagged) & earlier
    rank = jnp.sum(jnp.where(same, 1.0, 0.0), axis=0, keepdims=True)
    slot = jnp.where(here, tagged * 2.0 + rank, -1.0)
    marked = jnp.where(here, local + 1, 0).astype(F32)
    marked_col = jnp.transpose(jnp.broadcast_to(marked, (128, LINE_SPAN))).astype(BF)
    for first in range(0, 1024, 256):
        ids = iota((256, LINE_SPAN), 0) + first
        wanted = ((ids >> 3) * 2 + ((ids >> 1) & 1)).astype(F32)
        hot = jnp.where(slot == wanted, 1.0, 0.0).astype(BF)
        found = jnp.dot(hot, marked_col, preferred_element_type=F32).astype(jnp.int32)
        ids = iota((256, 128), 0) + first
        base = ((ids >> 2) & 1) * (2 * LINES) + (ids & 1) * LINES - 1
        target = jnp.where(found > 0, found + base, -1)
        for block in range(3):
            lanes = iota((256, 128), 1) + block * 128
            pick_ref[first : first + 256, block * 128 : (block + 1) * 128] = jnp.where(
                lanes == target, 1.0, 0.0
            ).astype(BF)

    lane = iota((2 * LINES, 128), 1)
    none = jnp.zeros((2 * LINES, 128), F32)
    shift_ref[:, 0:128] = none.astype(BF)
    shift_ref[:, 26 * 128 : 27 * 128] = none.astype(BF)

    def moved(left, right):
        return pltpu.roll(jnp.where(lane >= 64, left, right), 64, 1).astype(BF)

    shift_ref[:, 128:256] = moved(none, sec_ref[:, 0:128].astype(F32))
    shift_ref[:, 25 * 128 : 26 * 128] = moved(sec_ref[:, COLS - 128 : COLS].astype(F32), none)

    def move(block, carry):
        at = pl.multiple_of(block * 128, 128)
        left = sec_ref[:, pl.ds(pl.multiple_of(at - 128, 128), 128)].astype(F32)
        right = sec_ref[:, pl.ds(at, 128)].astype(F32)
        shift_ref[:, pl.ds(pl.multiple_of(at + 128, 128), 128)] = moved(left, right)
        return carry

    lax.fori_loop(1, COLS // 128, move, 0)

    tap_row = iota((256, 128), 0)
    for half in range(2):

        def window(step, carry):
            at = step + half * HALF
            block = jnp.clip(rg * (COLS // 128) + at - 1, 0, PIECES * (COLS // 128) - 1)
            start = start_ref[pl.ds(block, 1), :] - block * 128 + MARGIN
            taps = taps_ref[:, pl.ds(pl.multiple_of(block * 128, 128), 128)].astype(F32)
            offset = tap_row - start
            band = jnp.zeros((256, 128), F32)
            for tap in range(TAP_COUNT):
                band = jnp.where(offset == tap, taps[tap : tap + 1, :], band)
            lines = shift_ref[:, pl.ds(pl.multiple_of(at * 128, 128), 256)]
            summed = jnp.dot(lines, band.astype(BF), preferred_element_type=F32)
            res_ref[
                half * 2 * LINES : (half + 1) * 2 * LINES,
                pl.ds(pl.multiple_of(step * 128, 128), 128),
            ] = summed.astype(BF)
            return carry

        lax.fori_loop(0, HALF, window, 0)

    def send(step, carry):
        at = pl.ds(pl.multiple_of(step * 128, 128), 128)
        out_ref[:, at] = jnp.dot(
            pick_ref[...], res_ref[:, at], preferred_element_type=F32
        ).astype(BF)
        return carry

    lax.fori_loop(0, HALF, send, 0)


def pack_lines(place, sec, starts, taps, src, own):
    smem = pl.BlockSpec(memory_space=pltpu.SMEM)
    vmem = pl.BlockSpec(memory_space=pltpu.VMEM)
    return pl.pallas_call(
        pack_kernel,
        out_shape=jax.ShapeDtypeStruct((OWNERS * 8, WIDTH), BF),
        in_specs=[smem] + [vmem] * 5,
        out_specs=vmem,
        scratch_shapes=[
            pltpu.VMEM((2 * LINES, SCRATCH_BLOCKS * 128), BF),
            pltpu.VMEM((4 * LINES, WIDTH), BF),
            pltpu.VMEM((OWNERS * 8, 4 * LINES), BF),
        ],
        compiler_params=pltpu.CompilerParams(vmem_limit_bytes=20 * 2**20),
        cost_estimate=pl.CostEstimate(
            flops=2 * 10**9, bytes_accessed=6 * 10**6, transcendentals=0
        ),
        name="pack_lines",
    )(place, sec, starts, taps, src, own)


def estimate_kernel(
    off_ref,
    offv_ref,
    ref_ref,
    sec_ref,
    up_ref,
    down_ref,
    left_ref,
    right_ref,
    fwd_ref,
    wref_ref,
    wsec_ref,
    wlift_ref,
    lift_ref,
    est_ref,
    msg_ref,
    rcols_ref,
    scols_ref,
    chips_ref,
    half_ref,
    tot_ref,
    mom_ref,
):
    for part in range(2):
        rows = slice(part * CHIP_LEN, (part + 1) * CHIP_LEN)
        rcols_ref[rows, 0:128] = left_ref[part, 0:CHIP_LEN, :]
        rcols_ref[rows, 128 : 128 + COLS] = ref_ref[part, FIRST_ROW : FIRST_ROW + CHIP_LEN, :]
        rcols_ref[rows, 128 + COLS : 256 + COLS] = right_ref[part, 0:CHIP_LEN, :]
        rows = slice(part * ROWS, (part + 1) * ROWS)
        scols_ref[0, rows, :] = left_ref[part, CHIP_LEN:, :].astype(F32)
        scols_ref[SCRATCH_BLOCKS - 2, rows, :] = right_ref[part, CHIP_LEN:, :].astype(F32)
        scols_ref[SCRATCH_BLOCKS - 1, rows, :] = jnp.zeros((ROWS, 128), F32)

    def widen(block, carry):
        at = pl.ds(pl.multiple_of(block * 128, 128), 128)
        to = block + 1
        for part in range(2):
            base = part * ROWS
            own = base + MARGIN
            scols_ref[to, base:own, :] = up_ref[part, :, at].astype(F32)
            scols_ref[to, own : own + LINES, :] = sec_ref[part, :, at].astype(F32)
            scols_ref[to, own + LINES : base + ROWS, :] = down_ref[part, :, at].astype(F32)
        return carry

    lax.fori_loop(0, COLS // 128, widen, 0)

    lane = iota((CHIP_LEN, 128), 1)
    lane_all = iota((2 * CHIP_LEN, 128), 1)

    def cut(pair, carry):
        col = pair * 64 + 112
        at = pl.multiple_of((col >> 7) * 128, 128)
        turn = col & 127
        near = rcols_ref[:, pl.ds(at, 128)].astype(F32)
        far = rcols_ref[:, pl.ds(pl.multiple_of(at + 128, 128), 128)].astype(F32)
        both = pltpu.roll(jnp.where(lane_all >= turn, near, far), (128 - turn) & 127, 1)
        to = pl.multiple_of(pair * 128, 128)
        chips_ref[:, pl.ds(to, 128)] = both.astype(BF)
        for part in range(2):
            found = []
            for side in range(2):
                chip = pair * 2 + side
                row = off_ref[0, chip] + (FIRST_ROW + MARGIN + part * ROWS)
                col = chip * SPACING + off_ref[1, chip] + 112
                block = col >> 7
                turn = col & 127
                near = scols_ref[block, pl.ds(row, CHIP_LEN), :]
                far = scols_ref[block + 1, pl.ds(row, CHIP_LEN), :]
                found.append(
                    pltpu.roll(
                        jnp.where(lane >= turn, near, far), (128 + side * 64 - turn) & 127, 1
                    )
                )
            chips_ref[
                part * CHIP_LEN : (part + 1) * CHIP_LEN,
                pl.ds(pl.multiple_of(to + CHIPS * 64, 128), 128),
            ] = jnp.where(lane < 64, found[0], found[1]).astype(BF)
        return carry

    lax.fori_loop(0, PAIRS, cut, 0)

    def first_pass(step, carry):
        at = pl.ds(pl.multiple_of(step * 512, 512), 512)
        half_ref[:, at] = jnp.dot(
            fwd_ref[...], chips_ref[:, at], preferred_element_type=F32
        ).astype(BF)
        return carry

    lax.fori_loop(0, CHIPS * 128 // 512, first_pass, 0)

    lag_row = (iota((LAG_COUNT, 128), 0) - LAG_COUNT // 2).astype(F32) / OVERSAMPLE

    def correlate(step, carry):
        def gathered(base):
            rows = []
            for member in range(GROUP):
                at = pl.ds(pl.multiple_of(base + (step * GROUP + member) * 128, 128), 128)
                rows.append(
                    jnp.concatenate(
                        [half_ref[0:CHIP_LEN, at], half_ref[CHIP_LEN : 2 * CHIP_LEN, at]], axis=1
                    )
                )
            return jnp.concatenate(rows, axis=0)

        spec_ref = jnp.dot(gathered(0), wref_ref[...], preferred_element_type=F32)
        spec_sec = jnp.dot(gathered(CHIPS * 64), wsec_ref[...], preferred_element_type=F32)
        rr, ri = spec_ref[:, :128], spec_ref[:, 128:]
        sr, si = spec_sec[:, :128], spec_sec[:, 128:]
        cross = jnp.concatenate([rr * sr + ri * si, ri * sr - rr * si], axis=1).astype(BF)
        middle = jnp.dot(cross, wlift_ref[...], preferred_element_type=F32).astype(BF)
        columns = [
            jnp.concatenate(
                [
                    middle[m * CHIP_LEN : (m + 1) * CHIP_LEN, :128],
                    middle[m * CHIP_LEN : (m + 1) * CHIP_LEN, 128:],
                ],
                axis=0,
            )
            for m in range(GROUP)
        ]
        corr = jnp.dot(
            lift_ref[...], jnp.concatenate(columns, axis=1), preferred_element_type=F32
        )
        for m in range(GROUP):
            re = corr[:LAG_COUNT, m * 128 : (m + 1) * 128]
            im = corr[LAG_COUNT:, m * 128 : (m + 1) * 128]
            energy = re * re + im * im
            weight = energy * energy
            row = pl.ds(step * GROUP + m, 1)
            tot_ref[row, :] = jnp.sum(weight, axis=0, keepdims=True)
            mom_ref[row, :] = jnp.sum(weight * lag_row, axis=0, keepdims=True)
        return carry

    lax.fori_loop(0, PAIRS // GROUP, correlate, 0)

    wide = (PAIRS, 128)
    lanes = iota(wide, 1)
    total = tot_ref[...]
    moment = mom_ref[...]
    lag_lane = ((lanes & 63) - LAG_COUNT // 2).astype(F32) / OVERSAMPLE
    sides = []
    for side in range(2):
        mask = (lanes < 64) if side == 0 else (lanes >= 64)

        def over(values):
            return jnp.sum(jnp.where(mask, values, 0.0), axis=1, keepdims=True)

        whole = over(total) + EPS
        sides.append((over(moment) / whole, over(total * lag_lane) / whole))
    own = (lanes >> 1) == iota(wide, 0)
    even = (lanes & 1) == 0

    def spread(which):
        values = jnp.where(even, sides[0][which], sides[1][which])
        return jnp.sum(jnp.where(own, values, 0.0), axis=0, keepdims=True)

    offsets = offv_ref[...].astype(F32)
    est_az = offsets[0:1, :] + spread(0)
    est_rg = offsets[1:2, :] + spread(1)
    est_ref[0:1, :] = est_az
    est_ref[1:2, :] = est_rg
    angle = PHASE_RATE * est_az
    cosine = jnp.cos(angle)
    sine = jnp.sin(angle)
    cos_hi = cosine.astype(BF).astype(F32)
    sin_hi = sine.astype(BF).astype(F32)
    kind = iota((8, 128), 0)
    message = jnp.where(
        kind == 0,
        cos_hi,
        jnp.where(
            kind == 1,
            cosine - cos_hi,
            jnp.where(kind == 2, sin_hi, jnp.where(kind == 3, sine - sin_hi, 0.0)),
        ),
    ).astype(BF)
    msg_ref[...] = message


def estimate(off, offv, ref, sec, up, down, left, right):
    smem = pl.BlockSpec(memory_space=pltpu.SMEM)
    vmem = pl.BlockSpec(memory_space=pltpu.VMEM)
    return pl.pallas_call(
        estimate_kernel,
        out_shape=(
            jax.ShapeDtypeStruct((2, 128), F32),
            jax.ShapeDtypeStruct((8, 128), BF),
        ),
        in_specs=[smem] + [vmem] * 12,
        out_specs=(vmem, vmem),
        scratch_shapes=[
            pltpu.VMEM((2 * CHIP_LEN, SCRATCH_BLOCKS * 128), BF),
            pltpu.VMEM((SCRATCH_BLOCKS, 2 * ROWS, 128), F32),
            pltpu.VMEM((2 * CHIP_LEN, CHIPS * 128), BF),
            pltpu.VMEM((2 * CHIP_LEN, CHIPS * 128), BF),
            pltpu.VMEM((PAIRS, 128), F32),
            pltpu.VMEM((PAIRS, 128), F32),
        ],
        compiler_params=pltpu.CompilerParams(vmem_limit_bytes=26 * 2**20),
        cost_estimate=pl.CostEstimate(
            flops=6 * 10**9, bytes_accessed=20 * 10**6, transcendentals=0
        ),
        name="estimate",
    )(off, offv, ref, sec, up, down, left, right, *kernel_tables())


def place_kernel(at_ref, pick_ref, sel_ref, msg_ref, arr_ref, prev_ref, next_ref, out_ref):
    piece = pl.program_id(0)
    pick = pick_ref[...]
    turned = jnp.dot(sel_ref[...], msg_ref[...].reshape(128, 128), preferred_element_type=F32)
    cos_all = turned[0:32] + turned[32:64]
    sin_all = turned[64:96] + turned[96:128]
    lane = iota((OWNER_CAP, 128), 1)

    def moved(block_ref, first, last):
        return jnp.dot(
            pick, block_ref[:, 0, :, first:last].reshape(128, last - first),
            preferred_element_type=F32,
        )

    def write(block, lines):
        chip = block * 4 + (lane >> 5)
        cosine = jnp.take_along_axis(cos_all, chip, axis=1)
        sine = jnp.take_along_axis(sin_all, chip, axis=1)
        re, im = lines[:OWNER_CAP], lines[OWNER_CAP:]
        at = slice(block * 128, (block + 1) * 128)
        out_ref[0, :, at] = (re * cosine + im * sine).astype(BF)
        out_ref[1, :, at] = (im * cosine - re * sine).astype(BF)

    before = jnp.where(piece > 0, moved(prev_ref, 0, 128)[64:], 0.0)
    after = jnp.where(piece < PIECES - 1, moved(next_ref, 0, 128)[:64], 0.0)
    for first in range(0, HALF, 2):
        last = min(first + 2, HALF)
        lines = moved(arr_ref, first * 128, last * 128)
        for at in range(first, last):
            cols = slice((at - first) * 128, (at - first + 1) * 128)
            if at >= 1:
                low = lines[:64, cols]
                write(at - 1, low + before if at == 1 else low)
            if at < HALF - 1:
                high = lines[64:, cols]
                write(HALF - 1 + at, high + after if at == HALF - 2 else high)


def place_lines(place, pick, sel, message, arrived):
    same = pl.BlockSpec((128, 128), lambda r, at: (0, 0))
    block = (TILES, 1, 8, 128)
    return pl.pallas_call(
        place_kernel,
        grid_spec=pltpu.PrefetchScalarGridSpec(
            num_scalar_prefetch=1,
            grid=(PIECES,),
            in_specs=[
                same,
                same,
                pl.BlockSpec(block, lambda r, at: (0, r ^ at[1], 0, 0)),
                pl.BlockSpec((TILES, 1, 8, WIDTH), lambda r, at: (0, r, 0, 0)),
                pl.BlockSpec(block, lambda r, at: (0, jnp.maximum(r - 1, 0), 0, HALF - 1)),
                pl.BlockSpec(block, lambda r, at: (0, jnp.minimum(r + 1, PIECES - 1), 0, 0)),
            ],
            out_specs=pl.BlockSpec((2, OWNER_CAP, COLS), lambda r, at: (0, 0, r)),
        ),
        out_shape=jax.ShapeDtypeStruct((2, OWNER_CAP, COLS * PIECES), BF),
        compiler_params=pltpu.CompilerParams(vmem_limit_bytes=20 * 2**20),
        cost_estimate=pl.CostEstimate(
            flops=10**9, bytes_accessed=8 * 10**6, transcendentals=0
        ),
        name="place_lines",
    )(place, pick, sel, message, arrived, arrived, arrived)


def owner_tables(src_row, line_owner, az, me):
    tile = src_row // LINES
    owned = line_owner == me
    ids = jnp.arange(ALL_LINES, dtype=jnp.int32)
    before = owned[None, :] & (ids[None, :] < ids[:, None])
    rank = jnp.sum(before.astype(jnp.int32), axis=1)
    rank_tile = jnp.sum((before & (tile[None, :] == tile[:, None])).astype(jnp.int32), axis=1)
    outs = jnp.arange(OWNER_CAP, dtype=jnp.int32)
    hit = owned[None, :] & (rank[None, :] == outs[:, None])
    code = jnp.sum(jnp.where(hit, (tile * 2 + rank_tile + 1)[None, :], 0), axis=1) - 1
    rows = jnp.arange(128, dtype=jnp.int32)[:, None]
    cols = jnp.arange(128, dtype=jnp.int32)[None, :]
    slot = jnp.tile(code, 4)[:, None]
    pick = (
        (slot == (cols >> 3) * 2 + ((cols >> 1) & 1))
        & ((rows >> 6) == ((cols >> 2) & 1))
        & (((rows >> 5) & 1) == (cols & 1))
    )
    sel = (slot >= 0) & ((slot >> 1) == ((cols >> 3) ^ az)) & ((rows >> 5) == (cols & 7))
    return pick.astype(BF), sel.astype(BF)


def neighbours(axis, first, last):
    count = lax.axis_size(axis)
    up = [(i, i + 1) for i in range(count - 1)]
    down = [(i + 1, i) for i in range(count - 1)]
    return lax.ppermute(last, axis, up), lax.ppermute(first, axis, down)


def exchanged(block):
    block = block[None]
    held = 1
    while held < OWNERS:
        radix = min(4, OWNERS // held)
        block = jnp.concatenate(
            [block]
            + [
                lax.ppermute(block, BOTH, [(d, d ^ (held * k)) for d in range(OWNERS)])
                for k in range(1, radix)
            ],
            axis=0,
        )
        held *= radix
    return block


def per_device(
    reference_slc, secondary_slc, chip_offsets, src_row, line_owner, band_start, band_taps
):
    az = lax.axis_index("az")
    rg = lax.axis_index("rg")
    place = jnp.stack([az, rg]).astype(jnp.int32)
    packed = pack_lines(
        place,
        secondary_slc.reshape(2 * LINES, COLS),
        band_start.reshape(PIECES * COLS // 128, 128),
        band_taps,
        src_row.reshape(1, ALL_LINES),
        line_owner.reshape(1, ALL_LINES),
    )
    arrived = lax.all_to_all(packed, BOTH, 0, 0, tiled=True)
    chip_offsets, _ = lax.optimization_barrier((chip_offsets, packed))

    up, down = neighbours(
        "az", secondary_slc[:, :MARGIN, :], secondary_slc[:, LINES - MARGIN :, :]
    )

    def edge(cols):
        return jnp.concatenate(
            [
                reference_slc[:, FIRST_ROW : FIRST_ROW + CHIP_LEN, cols],
                up[:, :, cols],
                secondary_slc[:, :, cols],
                down[:, :, cols],
            ],
            axis=1,
        )

    left, right = neighbours("rg", edge(slice(0, 128)), edge(slice(COLS - 128, COLS)))
    off = chip_offsets[:, 0, :]
    offv = jnp.pad(off, ((0, 0), (0, 128 - CHIPS)))
    est, message = estimate(off, offv, reference_slc, secondary_slc, up, down, left, right)
    told = exchanged(message)
    pick, sel = owner_tables(src_row, line_owner, az, az * PIECES + rg)
    resampled = place_lines(
        place,
        pick,
        sel,
        told.reshape(TILES, PIECES, 8, 128),
        arrived.reshape(TILES, PIECES, 8, WIDTH),
    )
    return est[:, None, :CHIPS], resampled


def solution(mesh):
    return jax.shard_map(
        per_device,
        mesh=mesh,
        in_specs=(
            P(None, "az", "rg"),
            P(None, "az", "rg"),
            P(None, "az", "rg"),
            P(),
            P(),
            P(),
            P(),
        ),
        out_specs=(P(None, "az", "rg"), P(None, BOTH, None)),
        check_vma=False,
    )
```

```python
import math

import jax
import jax.numpy as jnp
import ml_dtypes
import numpy as np
from jax import lax
from jax.experimental import pallas as pl
from jax.experimental.pallas import tpu as pltpu
from jax.sharding import PartitionSpec as P

CHIP_LEN = 64
OVERSAMPLE = 16
LAG_COUNT = 48
TAP_COUNT = 8
SPACING = 32
MARGIN = 64
PHASE_RATE = 2.0
EPS = 1e-06

TILES = 16
PIECES = 8
OWNERS = 128
LINES = 96
COLS = 3072
BLOCKS = COLS // 128
ALL_LINES = 1536
CHIPS = 96
PAIRS = CHIPS // 2
OWNER_CAP = 32
FIRST_ROW = 16
ROWS = LINES + 2 * MARGIN
HALF = BLOCKS // 2
WIDTH = HALF * 128
LINE_SPAN = 256
SCRATCH_BLOCKS = BLOCKS + 3
GROUP = 8
BOTH = ("az", "rg")
BF = jnp.bfloat16
F32 = jnp.float32


def numpy_tables():
    ids = np.arange(CHIP_LEN)
    angles = -2.0 * math.pi / CHIP_LEN * (ids[:, None] * ids[None, :] % CHIP_LEN)
    scale = 1.0 / math.sqrt(CHIP_LEN)

    def low(values):
        return values.astype(np.float32).astype(ml_dtypes.bfloat16).astype(np.float32)

    four = (low(np.cos(angles) * scale), low(np.sin(angles) * scale))
    steps = np.arange(LAG_COUNT) - LAG_COUNT // 2
    freq = np.where(ids < CHIP_LEN // 2, ids, ids - CHIP_LEN)
    turns = steps[:, None] * freq[None, :] % (OVERSAMPLE * CHIP_LEN)
    lifted = 2.0 * math.pi / (OVERSAMPLE * CHIP_LEN) * turns
    lift = (low(np.cos(lifted) * scale), low(np.sin(lifted) * scale))
    return four, lift


def kernel_table():
    four, lift = numpy_tables()

    def stacked(re, im):
        out = np.zeros((2 * re.shape[0], 256), np.float32)
        out[:, :128] = np.block([[re, -im], [im, re]])
        return out

    def paired(re, im, starts):
        out = np.zeros((2, 128, 2, 2, 64), np.float32)
        count = re.shape[0]
        for chip, first in enumerate(starts):
            rows = slice(first, first + CHIP_LEN)
            out[0, rows, 0, chip, :count] = re.T
            out[0, rows, 1, chip, :count] = im.T
            out[1, rows, 0, chip, :count] = -im.T
            out[1, rows, 1, chip, :count] = re.T
        return out.reshape(256, 256)

    whole = np.concatenate(
        [
            paired(*four, (0, 32)),
            paired(*four, (0, 64)),
            paired(*lift, (0, 64)),
            stacked(*lift),
            stacked(*four),
        ]
    )
    return jnp.asarray(whole.astype(ml_dtypes.bfloat16))


def iota(shape, dim):
    return lax.broadcasted_iota(jnp.int32, shape, dim)


def half_turned(left, right):
    lane = iota(left.shape, 1)
    return pltpu.roll(jnp.where(lane >= 64, left.astype(F32), right.astype(F32)), 64, 1).astype(BF)


def sinc_band(start_ref, taps_ref, block):
    start = start_ref[pl.ds(block, 1), :] - block * 128 + MARGIN
    taps = taps_ref[:, pl.ds(pl.multiple_of(block * 128, 128), 128)].astype(F32)
    offset = iota((256, 128), 0) - start
    band = jnp.zeros((256, 128), F32)
    for tap in range(TAP_COUNT):
        band = jnp.where(offset == tap, taps[tap : tap + 1, :], band)
    return band.astype(BF)


def resample_kernel(
    place_ref, sec_ref, start_ref, taps_ref, src_ref, own_ref, sum_ref, pick_ref, shift_ref
):
    az = place_ref[0]
    rg = place_ref[1]

    line_first = jnp.minimum(jnp.maximum(az * LINES - 8, 0) // 128 * 128, ALL_LINES - LINE_SPAN)
    span = pl.ds(pl.multiple_of(line_first, 128), LINE_SPAN)
    local = src_ref[:, span] - az * LINES
    owner = own_ref[:, span]
    here = (local >= 0) & (local < LINES)
    tagged = jnp.where(here, owner, -1).astype(F32)
    tagged_col = jnp.transpose(jnp.broadcast_to(tagged, (128, LINE_SPAN)))
    tagged_col = jnp.concatenate([tagged_col, tagged_col], axis=1)
    square = (LINE_SPAN, LINE_SPAN)
    earlier = iota(square, 0) < iota(square, 1)
    same = (tagged_col == tagged) & earlier
    rank = jnp.sum(jnp.where(same, 1.0, 0.0), axis=0, keepdims=True)
    slot = jnp.where(here, tagged * 2.0 + rank, -1.0)
    marked = jnp.where(here, local + 1, 0).astype(F32)
    marked_col = jnp.transpose(jnp.broadcast_to(marked, (128, LINE_SPAN))).astype(BF)
    for first in range(0, 1024, 256):
        ids = iota((256, LINE_SPAN), 0) + first
        wanted = ((ids >> 3) * 2 + ((ids >> 1) & 1)).astype(F32)
        hot = jnp.where(slot == wanted, 1.0, 0.0).astype(BF)
        found = jnp.dot(hot, marked_col, preferred_element_type=F32).astype(jnp.int32)
        ids = iota((256, 128), 0) + first
        base = ((ids >> 2) & 1) * (2 * LINES) + (ids & 1) * LINES - 1
        target = jnp.where(found > 0, found + base, -1)
        for block in range(3):
            lanes = iota((256, 128), 1) + block * 128
            pick_ref[first : first + 256, block * 128 : (block + 1) * 128] = jnp.where(
                lanes == target, 1.0, 0.0
            ).astype(BF)

    def move(step, carry):
        at = pl.multiple_of(step * 128, 128)
        shift_ref[:, pl.ds(at, 128)] = half_turned(
            sec_ref[:, pl.ds(pl.multiple_of(at - 128, 128), 128)], sec_ref[:, pl.ds(at, 128)]
        )
        return carry

    lax.fori_loop(1, BLOCKS, move, 0)

    def window(step, carry):
        for member in range(2):
            block = step * 2 + member + 1
            at = pl.multiple_of(block * 128, 128)
            sum_ref[:, pl.ds(at, 128)] = jnp.dot(
                shift_ref[:, pl.ds(at, 256)],
                sinc_band(start_ref, taps_ref, rg * BLOCKS + block),
                preferred_element_type=F32,
            )
        return carry

    lax.fori_loop(0, (BLOCKS - 2) // 2, window, 0)


def resample_inner(place, sec, starts, taps, src, own):
    smem = pl.BlockSpec(memory_space=pltpu.SMEM)
    vmem = pl.BlockSpec(memory_space=pltpu.VMEM)
    return pl.pallas_call(
        resample_kernel,
        out_shape=(
            jax.ShapeDtypeStruct((2 * LINES, COLS), F32),
            jax.ShapeDtypeStruct((OWNERS * 8, 4 * LINES), BF),
        ),
        in_specs=[smem] + [vmem] * 5,
        out_specs=(vmem, vmem),
        scratch_shapes=[pltpu.VMEM((2 * LINES, COLS), BF)],
        compiler_params=pltpu.CompilerParams(vmem_limit_bytes=14 * 2**20),
        cost_estimate=pl.CostEstimate(
            flops=2 * 10**9, bytes_accessed=6 * 10**6, transcendentals=0
        ),
        name="resample_inner",
    )(place, sec, starts, taps, src, own)


def estimate_kernel(
    place_ref,
    off_ref,
    offv_ref,
    ref_ref,
    sec_ref,
    up_ref,
    down_ref,
    left_ref,
    right_ref,
    table_ref,
    start_ref,
    taps_ref,
    sum_ref,
    pick_ref,
    est_ref,
    out_ref,
    rcols_ref,
    scols_ref,
    chips_ref,
    half_ref,
    tot_ref,
    mom_ref,
    lines_ref,
):
    for part in range(2):
        rows = slice(part * CHIP_LEN, (part + 1) * CHIP_LEN)
        rcols_ref[rows, 0:128] = left_ref[part, 0:CHIP_LEN, :]
        rcols_ref[rows, 128 : 128 + COLS] = ref_ref[part, FIRST_ROW : FIRST_ROW + CHIP_LEN, :]
        rcols_ref[rows, 128 + COLS : 256 + COLS] = right_ref[part, 0:CHIP_LEN, :]
        rows = slice(part * ROWS, (part + 1) * ROWS)
        scols_ref[0, rows, :] = left_ref[part, CHIP_LEN:, :].astype(F32)
        scols_ref[SCRATCH_BLOCKS - 2, rows, :] = right_ref[part, CHIP_LEN:, :].astype(F32)
        scols_ref[SCRATCH_BLOCKS - 1, rows, :] = jnp.zeros((ROWS, 128), F32)

    def widen(step, carry):
        for member in range(2):
            block = step * 2 + member
            at = pl.ds(pl.multiple_of(block * 128, 128), 128)
            to = block + 1
            for part in range(2):
                base = part * ROWS
                own = base + MARGIN
                scols_ref[to, base:own, :] = up_ref[part, :, at].astype(F32)
                scols_ref[to, own : own + LINES, :] = sec_ref[part, :, at].astype(F32)
                scols_ref[to, own + LINES : base + ROWS, :] = down_ref[part, :, at].astype(F32)
        return carry

    lax.fori_loop(0, BLOCKS // 2, widen, 0)

    lane = iota((CHIP_LEN, 128), 1)
    lane_all = iota((2 * CHIP_LEN, 128), 1)

    def cut_pair(pair):
        col = pair * 64 + 112
        at = pl.multiple_of((col >> 7) * 128, 128)
        turn = col & 127
        near = rcols_ref[:, pl.ds(at, 128)].astype(F32)
        far = rcols_ref[:, pl.ds(pl.multiple_of(at + 128, 128), 128)].astype(F32)
        both = pltpu.roll(jnp.where(lane_all >= turn, near, far), (128 - turn) & 127, 1)
        to = pl.multiple_of(pair * 128, 128)
        chips_ref[:, pl.ds(to, 128)] = both.astype(BF)
        for part in range(2):
            found = []
            for side in range(2):
                chip = pair * 2 + side
                row = off_ref[0, chip] + (FIRST_ROW + MARGIN + part * ROWS)
                col = chip * SPACING + off_ref[1, chip] + 112
                block = col >> 7
                turn = col & 127
                near = scols_ref[block, pl.ds(row, CHIP_LEN), :]
                far = scols_ref[block + 1, pl.ds(row, CHIP_LEN), :]
                found.append(
                    pltpu.roll(
                        jnp.where(lane >= turn, near, far), (128 + side * 64 - turn) & 127, 1
                    )
                )
            chips_ref[
                part * CHIP_LEN : (part + 1) * CHIP_LEN,
                pl.ds(pl.multiple_of(to + CHIPS * 64, 128), 128),
            ] = jnp.where(lane < 64, found[0], found[1]).astype(BF)

    def cut(step, carry):
        for member in range(2):
            cut_pair(step * 2 + member)
        return carry

    lax.fori_loop(0, PAIRS // 2, cut, 0)

    fwd = table_ref[864:992, 0:128]
    for first in range(0, CHIPS * 128, 1024):
        half_ref[:, first : first + 1024] = jnp.dot(
            fwd, chips_ref[:, first : first + 1024], preferred_element_type=F32
        ).astype(BF)

    lag_row = (iota((LAG_COUNT, 128), 0) - LAG_COUNT // 2).astype(F32) / OVERSAMPLE

    def correlate(step, carry):
        def gathered(base):
            rows = []
            for member in range(GROUP):
                at = pl.ds(pl.multiple_of(base + (step * GROUP + member) * 128, 128), 128)
                rows.append(
                    jnp.concatenate(
                        [half_ref[0:CHIP_LEN, at], half_ref[CHIP_LEN : 2 * CHIP_LEN, at]], axis=1
                    )
                )
            return jnp.concatenate(rows, axis=0)

        spec_ref = jnp.dot(gathered(0), table_ref[0:256, :], preferred_element_type=F32)
        spec_sec = jnp.dot(gathered(CHIPS * 64), table_ref[256:512, :], preferred_element_type=F32)
        rr, ri = spec_ref[:, :128], spec_ref[:, 128:]
        sr, si = spec_sec[:, :128], spec_sec[:, 128:]
        cross = jnp.concatenate([rr * sr + ri * si, ri * sr - rr * si], axis=1).astype(BF)
        middle = jnp.dot(cross, table_ref[512:768, :], preferred_element_type=F32).astype(BF)
        columns = [
            jnp.concatenate(
                [
                    middle[m * CHIP_LEN : (m + 1) * CHIP_LEN, :128],
                    middle[m * CHIP_LEN : (m + 1) * CHIP_LEN, 128:],
                ],
                axis=0,
            )
            for m in range(GROUP)
        ]
        corr = jnp.dot(
            table_ref[768:864, 0:128],
            jnp.concatenate(columns, axis=1),
            preferred_element_type=F32,
        )
        for m in range(GROUP):
            re = corr[:LAG_COUNT, m * 128 : (m + 1) * 128]
            im = corr[LAG_COUNT:, m * 128 : (m + 1) * 128]
            energy = re * re + im * im
            weight = energy * energy
            row = pl.ds(step * GROUP + m, 1)
            tot_ref[row, :] = jnp.sum(weight, axis=0, keepdims=True)
            mom_ref[row, :] = jnp.sum(weight * lag_row, axis=0, keepdims=True)
        return carry

    lax.fori_loop(0, PAIRS // GROUP, correlate, 0)

    wide = (PAIRS, 128)
    lanes = iota(wide, 1)
    total = tot_ref[...]
    moment = mom_ref[...]
    lag_lane = ((lanes & 63) - LAG_COUNT // 2).astype(F32) / OVERSAMPLE
    sides = []
    for side in range(2):
        mask = (lanes < 64) if side == 0 else (lanes >= 64)

        def over(values):
            return jnp.sum(jnp.where(mask, values, 0.0), axis=1, keepdims=True)

        whole = over(total) + EPS
        sides.append((over(moment) / whole, over(total * lag_lane) / whole))
    own = (lanes >> 1) == iota(wide, 0)
    even = (lanes & 1) == 0

    def spread(which):
        values = jnp.where(even, sides[0][which], sides[1][which])
        return jnp.sum(jnp.where(own, values, 0.0), axis=0, keepdims=True)

    offsets = offv_ref[...].astype(F32)
    est_az = offsets[0:1, :] + spread(0)
    est_rg = offsets[1:2, :] + spread(1)
    est_ref[0:1, :] = est_az
    est_ref[1:2, :] = est_rg
    angle = PHASE_RATE * est_az
    cos_all = jnp.broadcast_to(jnp.cos(angle), (8, 128))
    sin_all = jnp.broadcast_to(jnp.sin(angle), (8, 128))

    def turned(block, summed):
        chip = block * 4 + (iota((8, 128), 1) >> 5)
        cosine = jnp.take_along_axis(cos_all, chip, axis=1)[0:1, :]
        sine = jnp.take_along_axis(sin_all, chip, axis=1)[0:1, :]
        re, im = summed[:LINES], summed[LINES:]
        half = block // HALF
        at = slice((block - half * HALF) * 128, (block - half * HALF + 1) * 128)
        base = half * 2 * LINES
        lines_ref[base : base + LINES, at] = (re * cosine + im * sine).astype(BF)
        lines_ref[base + LINES : base + 2 * LINES, at] = (im * cosine - re * sine).astype(BF)

    first_own = CHIP_LEN + MARGIN
    rg = place_ref[1]

    def joined(ref, rows, cols):
        return jnp.concatenate([ref[0, rows, cols], ref[1, rows, cols]], axis=0)

    every = slice(0, LINES)
    rim = slice(first_own, first_own + LINES)
    for block in (0, BLOCKS - 1):
        cols = []
        for at in range(block - 1, block + 2):
            if at < 0:
                cols.append(joined(left_ref, rim, slice(0, 128)))
            elif at >= BLOCKS:
                cols.append(joined(right_ref, rim, slice(0, 128)))
            else:
                cols.append(joined(sec_ref, every, slice(at * 128, (at + 1) * 128)))
        near = jnp.concatenate(
            [half_turned(cols[0], cols[1]), half_turned(cols[1], cols[2])], axis=1
        )
        turned(
            block,
            jnp.dot(
                near,
                sinc_band(start_ref, taps_ref, rg * BLOCKS + block),
                preferred_element_type=F32,
            ),
        )
    for block in range(1, BLOCKS - 1):
        turned(block, sum_ref[:, block * 128 : (block + 1) * 128])
    for first in range(0, WIDTH, 256):
        out_ref[:, first : first + 256] = jnp.dot(
            pick_ref[...], lines_ref[:, first : first + 256], preferred_element_type=F32
        ).astype(BF)


def estimate(place, off, offv, *arrays):
    smem = pl.BlockSpec(memory_space=pltpu.SMEM)
    vmem = pl.BlockSpec(memory_space=pltpu.VMEM)
    return pl.pallas_call(
        estimate_kernel,
        out_shape=(
            jax.ShapeDtypeStruct((2, 128), F32),
            jax.ShapeDtypeStruct((OWNERS * 8, WIDTH), BF),
        ),
        in_specs=[smem] * 2 + [vmem] * 12,
        out_specs=(vmem, vmem),
        scratch_shapes=[
            pltpu.VMEM((2 * CHIP_LEN, SCRATCH_BLOCKS * 128), BF),
            pltpu.VMEM((SCRATCH_BLOCKS, 2 * ROWS, 128), F32),
            pltpu.VMEM((2 * CHIP_LEN, CHIPS * 128), BF),
            pltpu.VMEM((2 * CHIP_LEN, CHIPS * 128), BF),
            pltpu.VMEM((PAIRS, 128), F32),
            pltpu.VMEM((PAIRS, 128), F32),
            pltpu.VMEM((4 * LINES, WIDTH), BF),
        ],
        compiler_params=pltpu.CompilerParams(vmem_limit_bytes=36 * 2**20),
        cost_estimate=pl.CostEstimate(
            flops=6 * 10**9, bytes_accessed=20 * 10**6, transcendentals=0
        ),
        name="estimate",
    )(place, off, offv, *arrays)


def place_kernel(pick_ref, arr_ref, out_ref):
    pick = pick_ref[...]
    for first in range(0, WIDTH, 256):
        lines = jnp.dot(
            pick,
            arr_ref[:, 0, :, first : first + 256].reshape(128, 256),
            preferred_element_type=F32,
        ).astype(BF)
        for half in range(2):
            at = slice(half * WIDTH + first, half * WIDTH + first + 256)
            for part in range(2):
                base = half * 64 + part * OWNER_CAP
                out_ref[part, :, at] = lines[base : base + OWNER_CAP, :]


def place_lines(pick, arrived):
    return pl.pallas_call(
        place_kernel,
        grid=(PIECES,),
        out_shape=jax.ShapeDtypeStruct((2, OWNER_CAP, COLS * PIECES), BF),
        in_specs=[
            pl.BlockSpec((128, 128), lambda r: (0, 0)),
            pl.BlockSpec((TILES, 1, 8, WIDTH), lambda r: (0, r, 0, 0)),
        ],
        out_specs=pl.BlockSpec((2, OWNER_CAP, COLS), lambda r: (0, 0, r)),
        compiler_params=pltpu.CompilerParams(vmem_limit_bytes=20 * 2**20),
        cost_estimate=pl.CostEstimate(
            flops=10**9, bytes_accessed=8 * 10**6, transcendentals=0
        ),
        name="place_lines",
    )(pick, arrived)


def owner_table(src_row, line_owner, me):
    tile = src_row // LINES
    owned = line_owner == me
    ids = jnp.arange(ALL_LINES, dtype=jnp.int32)
    before = owned[None, :] & (ids[None, :] < ids[:, None])
    rank = jnp.sum(before.astype(jnp.int32), axis=1)
    rank_tile = jnp.sum((before & (tile[None, :] == tile[:, None])).astype(jnp.int32), axis=1)
    outs = jnp.arange(OWNER_CAP, dtype=jnp.int32)
    hit = owned[None, :] & (rank[None, :] == outs[:, None])
    code = jnp.sum(jnp.where(hit, (tile * 2 + rank_tile + 1)[None, :], 0), axis=1) - 1
    rows = jnp.arange(128, dtype=jnp.int32)[:, None]
    cols = jnp.arange(128, dtype=jnp.int32)[None, :]
    slot = jnp.tile(code, 4)[:, None]
    pick = (
        (slot == (cols >> 3) * 2 + ((cols >> 1) & 1))
        & ((rows >> 6) == ((cols >> 2) & 1))
        & (((rows >> 5) & 1) == (cols & 1))
    )
    return pick.astype(BF)


def neighbours(axis, first, last):
    count = lax.axis_size(axis)
    up = [(i, i + 1) for i in range(count - 1)]
    down = [(i + 1, i) for i in range(count - 1)]
    return lax.ppermute(last, axis, up), lax.ppermute(first, axis, down)


def per_device(
    reference_slc, secondary_slc, chip_offsets, src_row, line_owner, band_start, band_taps
):
    az = lax.axis_index("az")
    rg = lax.axis_index("rg")
    place = jnp.stack([az, rg]).astype(jnp.int32)
    starts = band_start.reshape(PIECES * BLOCKS, 128)
    up, down = neighbours(
        "az", secondary_slc[:, :MARGIN, :], secondary_slc[:, LINES - MARGIN :, :]
    )

    def edge(cols):
        return jnp.concatenate(
            [
                reference_slc[:, FIRST_ROW : FIRST_ROW + CHIP_LEN, cols],
                up[:, :, cols],
                secondary_slc[:, :, cols],
                down[:, :, cols],
            ],
            axis=1,
        )

    left, right = neighbours("rg", edge(slice(0, 128)), edge(slice(COLS - 128, COLS)))
    summed, pick_sent = resample_inner(
        place,
        secondary_slc.reshape(2 * LINES, COLS),
        starts,
        band_taps,
        src_row.reshape(1, ALL_LINES),
        line_owner.reshape(1, ALL_LINES),
    )
    off = chip_offsets[:, 0, :]
    offv = jnp.pad(off, ((0, 0), (0, 128 - CHIPS)))
    est, packed = estimate(
        place,
        off,
        offv,
        reference_slc,
        secondary_slc,
        up,
        down,
        left,
        right,
        kernel_table(),
        starts,
        band_taps,
        summed,
        pick_sent,
    )
    arrived = lax.all_to_all(packed, BOTH, 0, 0, tiled=True)
    pick = owner_table(src_row, line_owner, az * PIECES + rg)
    resampled = place_lines(pick, arrived.reshape(TILES, PIECES, 8, WIDTH))
    return est[:, None, :CHIPS], resampled


def solution(mesh):
    return jax.shard_map(
        per_device,
        mesh=mesh,
        in_specs=(
            P(None, "az", "rg"),
            P(None, "az", "rg"),
            P(None, "az", "rg"),
            P(),
            P(),
            P(),
            P(),
        ),
        out_specs=(P(None, "az", "rg"), P(None, BOTH, None)),
        check_vma=False,
    )
```

```python
import math

import jax
import jax.numpy as jnp
import ml_dtypes
import numpy as np
from jax import lax
from jax.experimental import pallas as pl
from jax.experimental.pallas import tpu as pltpu
from jax.sharding import PartitionSpec as P

CHIP_LEN = 64
OVERSAMPLE = 16
LAG_COUNT = 48
TAP_COUNT = 8
SPACING = 32
MARGIN = 64
PHASE_RATE = 2.0
EPS = 1e-06

TILES = 16
PIECES = 8
OWNERS = 128
LINES = 96
COLS = 3072
BLOCKS = COLS // 128
ALL_LINES = 1536
CHIPS = 96
PAIRS = CHIPS // 2
OWNER_CAP = 32
FIRST_ROW = 16
ROWS = LINES + 2 * MARGIN
HALF = BLOCKS // 2
WIDTH = HALF * 128
LINE_SPAN = 256
SCRATCH_BLOCKS = BLOCKS + 3
GROUP = 8
BOTH = ("az", "rg")
BF = jnp.bfloat16
F32 = jnp.float32


def numpy_tables():
    ids = np.arange(CHIP_LEN)
    angles = -2.0 * math.pi / CHIP_LEN * (ids[:, None] * ids[None, :] % CHIP_LEN)
    scale = 1.0 / math.sqrt(CHIP_LEN)

    def low(values):
        return values.astype(np.float32).astype(ml_dtypes.bfloat16).astype(np.float32)

    four = (low(np.cos(angles) * scale), low(np.sin(angles) * scale))
    steps = np.arange(LAG_COUNT) - LAG_COUNT // 2
    freq = np.where(ids < CHIP_LEN // 2, ids, ids - CHIP_LEN)
    turns = steps[:, None] * freq[None, :] % (OVERSAMPLE * CHIP_LEN)
    lifted = 2.0 * math.pi / (OVERSAMPLE * CHIP_LEN) * turns
    lift = (low(np.cos(lifted) * scale), low(np.sin(lifted) * scale))
    return four, lift


def kernel_table():
    four, lift = numpy_tables()

    def stacked(re, im):
        out = np.zeros((2 * re.shape[0], 256), np.float32)
        out[:, :128] = np.block([[re, -im], [im, re]])
        return out

    def paired(re, im, starts):
        out = np.zeros((2, 128, 2, 2, 64), np.float32)
        count = re.shape[0]
        for chip, first in enumerate(starts):
            rows = slice(first, first + CHIP_LEN)
            out[0, rows, 0, chip, :count] = re.T
            out[0, rows, 1, chip, :count] = im.T
            out[1, rows, 0, chip, :count] = -im.T
            out[1, rows, 1, chip, :count] = re.T
        return out.reshape(256, 256)

    whole = np.concatenate(
        [
            paired(*four, (0, 32)),
            paired(*four, (0, 64)),
            paired(*lift, (0, 64)),
            stacked(*lift),
            stacked(*four),
        ]
    )
    return jnp.asarray(whole.astype(ml_dtypes.bfloat16))


def iota(shape, dim):
    return lax.broadcasted_iota(jnp.int32, shape, dim)


def half_turned(left, right):
    lane = iota(left.shape, 1)
    return pltpu.roll(jnp.where(lane >= 64, left.astype(F32), right.astype(F32)), 64, 1).astype(BF)


def sinc_band(start_ref, taps_ref, block):
    start = start_ref[pl.ds(block, 1), :] - block * 128 + MARGIN
    taps = taps_ref[:, pl.ds(pl.multiple_of(block * 128, 128), 128)].astype(F32)
    offset = iota((256, 128), 0) - start
    band = jnp.zeros((256, 128), F32)
    for tap in range(TAP_COUNT):
        band = jnp.where(offset == tap, taps[tap : tap + 1, :], band)
    return band.astype(BF)


def resample_kernel(
    place_ref, sec_ref, start_ref, taps_ref, src_ref, own_ref, sum_ref, pick_ref, shift_ref
):
    az = place_ref[0]
    rg = place_ref[1]

    line_first = jnp.minimum(jnp.maximum(az * LINES - 8, 0) // 128 * 128, ALL_LINES - LINE_SPAN)
    span = pl.ds(pl.multiple_of(line_first, 128), LINE_SPAN)
    local = src_ref[:, span] - az * LINES
    owner = own_ref[:, span]
    here = (local >= 0) & (local < LINES)
    tagged = jnp.where(here, owner, -1).astype(F32)
    tagged_col = jnp.transpose(jnp.broadcast_to(tagged, (128, LINE_SPAN)))
    tagged_col = jnp.concatenate([tagged_col, tagged_col], axis=1)
    square = (LINE_SPAN, LINE_SPAN)
    earlier = iota(square, 0) < iota(square, 1)
    same = (tagged_col == tagged) & earlier
    rank = jnp.sum(jnp.where(same, 1.0, 0.0), axis=0, keepdims=True)
    slot = jnp.where(here, tagged * 2.0 + rank, -1.0)
    marked = jnp.where(here, local + 1, 0).astype(F32)
    marked_col = jnp.transpose(jnp.broadcast_to(marked, (128, LINE_SPAN))).astype(BF)
    for first in range(0, 1024, 256):
        ids = iota((256, LINE_SPAN), 0) + first
        wanted = ((ids >> 3) * 2 + ((ids >> 1) & 1)).astype(F32)
        hot = jnp.where(slot == wanted, 1.0, 0.0).astype(BF)
        found = jnp.dot(hot, marked_col, preferred_element_type=F32).astype(jnp.int32)
        ids = iota((256, 128), 0) + first
        base = ((ids >> 2) & 1) * (2 * LINES) + (ids & 1) * LINES - 1
        target = jnp.where(found > 0, found + base, -1)
        for block in range(3):
            lanes = iota((256, 128), 1) + block * 128
            pick_ref[first : first + 256, block * 128 : (block + 1) * 128] = jnp.where(
                lanes == target, 1.0, 0.0
            ).astype(BF)

    def move(step, carry):
        at = pl.multiple_of(step * 128, 128)
        shift_ref[:, pl.ds(at, 128)] = half_turned(
            sec_ref[:, pl.ds(pl.multiple_of(at - 128, 128), 128)], sec_ref[:, pl.ds(at, 128)]
        )
        return carry

    lax.fori_loop(1, BLOCKS, move, 0)

    def window(step, carry):
        for member in range(2):
            block = step * 2 + member + 1
            at = pl.multiple_of(block * 128, 128)
            sum_ref[:, pl.ds(at, 128)] = jnp.dot(
                shift_ref[:, pl.ds(at, 256)],
                sinc_band(start_ref, taps_ref, rg * BLOCKS + block),
                preferred_element_type=F32,
            )
        return carry

    lax.fori_loop(0, (BLOCKS - 2) // 2, window, 0)


def resample_inner(place, sec, starts, taps, src, own):
    smem = pl.BlockSpec(memory_space=pltpu.SMEM)
    vmem = pl.BlockSpec(memory_space=pltpu.VMEM)
    return pl.pallas_call(
        resample_kernel,
        out_shape=(
            jax.ShapeDtypeStruct((2 * LINES, COLS), F32),
            jax.ShapeDtypeStruct((OWNERS * 8, 4 * LINES), BF),
        ),
        in_specs=[smem] + [vmem] * 5,
        out_specs=(vmem, vmem),
        scratch_shapes=[pltpu.VMEM((2 * LINES, COLS), BF)],
        compiler_params=pltpu.CompilerParams(vmem_limit_bytes=14 * 2**20),
        cost_estimate=pl.CostEstimate(
            flops=2 * 10**9, bytes_accessed=6 * 10**6, transcendentals=0
        ),
        name="resample_inner",
    )(place, sec, starts, taps, src, own)


def rims_kernel(ref_ref, sec_ref, head_ref, tail_ref, first_ref, last_ref, sems):
    copies = []
    for part in range(2):
        pairs = (
            (sec_ref.at[part, 0:MARGIN, :], head_ref.at[part]),
            (sec_ref.at[part, LINES - MARGIN : LINES, :], tail_ref.at[part]),
        )
        for to_ref, cols in ((first_ref, slice(0, 128)), (last_ref, slice(COLS - 128, COLS))):
            pairs += (
                (
                    ref_ref.at[part, FIRST_ROW : FIRST_ROW + CHIP_LEN, cols],
                    to_ref.at[part, 0:CHIP_LEN, :],
                ),
                (sec_ref.at[part, :, cols], to_ref.at[part, CHIP_LEN : CHIP_LEN + LINES, :]),
            )
        copies += pairs
    started = [
        pltpu.make_async_copy(src, dst, sems.at[n]) for n, (src, dst) in enumerate(copies)
    ]
    for copy in started:
        copy.start()
    for copy in started:
        copy.wait()


def rims(ref, sec):
    hbm = pl.BlockSpec(memory_space=pltpu.HBM)
    vmem = pl.BlockSpec(memory_space=pltpu.VMEM)
    rows = jax.ShapeDtypeStruct((2, MARGIN, COLS), BF)
    cols = jax.ShapeDtypeStruct((2, CHIP_LEN + LINES, 128), BF)
    return pl.pallas_call(
        rims_kernel,
        out_shape=(rows, rows, cols, cols),
        in_specs=[hbm] * 2,
        out_specs=(vmem,) * 4,
        scratch_shapes=[pltpu.SemaphoreType.DMA((12,))],
        compiler_params=pltpu.CompilerParams(vmem_limit_bytes=4 * 2**20),
        cost_estimate=pl.CostEstimate(flops=0, bytes_accessed=4 * 10**6, transcendentals=0),
        name="rims",
    )(ref, sec)


def side_by_side(half_ref, pairs):
    rows = []
    for pair in pairs:
        at = pl.ds(pl.multiple_of(pair * 128, 128), 128)
        rows.append(
            jnp.concatenate(
                [half_ref[0:CHIP_LEN, at], half_ref[CHIP_LEN : 2 * CHIP_LEN, at]], axis=1
            )
        )
    return jnp.concatenate(rows, axis=0)


def first_pass(table_ref, chips_ref, half_ref):
    fwd = table_ref[864:992, 0:128]
    for first in range(0, CHIPS * 64, 1024):
        half_ref[:, first : first + 1024] = jnp.dot(
            fwd, chips_ref[:, first : first + 1024], preferred_element_type=F32
        ).astype(BF)


def reference_kernel(
    place_ref,
    ref_ref,
    sec_ref,
    left_ref,
    right_ref,
    table_ref,
    start_ref,
    taps_ref,
    spec_ref,
    edge_ref,
    rcols_ref,
    chips_ref,
    half_ref,
):
    for part in range(2):
        rows = slice(part * CHIP_LEN, (part + 1) * CHIP_LEN)
        rcols_ref[rows, 0:128] = left_ref[part, 0:CHIP_LEN, :]
        rcols_ref[rows, 128 : 128 + COLS] = ref_ref[part, FIRST_ROW : FIRST_ROW + CHIP_LEN, :]
        rcols_ref[rows, 128 + COLS : 256 + COLS] = right_ref[part, 0:CHIP_LEN, :]

    lane = iota((2 * CHIP_LEN, 128), 1)

    def cut(step, carry):
        near = rcols_ref[:, pl.ds(pl.multiple_of(step * 128, 128), 128)].astype(F32)
        here = rcols_ref[:, pl.ds(pl.multiple_of(step * 128 + 128, 128), 128)].astype(F32)
        far = rcols_ref[:, pl.ds(pl.multiple_of(step * 128 + 256, 128), 128)].astype(F32)
        to = pl.multiple_of(step * 256, 256)
        even = pltpu.roll(jnp.where(lane >= 112, near, here), 16, 1)
        odd = pltpu.roll(jnp.where(lane >= 48, here, far), 80, 1)
        chips_ref[:, pl.ds(to, 128)] = even.astype(BF)
        chips_ref[:, pl.ds(pl.multiple_of(to + 128, 128), 128)] = odd.astype(BF)
        return carry

    lax.fori_loop(0, PAIRS // 2, cut, 0)
    first_pass(table_ref, chips_ref, half_ref)

    def second_pass(step, carry):
        spec_ref[pl.ds(pl.multiple_of(step * GROUP * CHIP_LEN, 512), GROUP * CHIP_LEN), :] = jnp.dot(
            side_by_side(half_ref, [step * GROUP + m for m in range(GROUP)]),
            table_ref[0:256, :],
            preferred_element_type=F32,
        )
        return carry

    lax.fori_loop(0, PAIRS // GROUP, second_pass, 0)

    def joined(ref, rows, cols):
        return jnp.concatenate([ref[0, rows, cols], ref[1, rows, cols]], axis=0)

    every = slice(0, LINES)
    rim = slice(CHIP_LEN, CHIP_LEN + LINES)
    one = slice(0, 128)
    lefts = (joined(left_ref, rim, one), joined(sec_ref, every, one))
    rights = (joined(sec_ref, every, slice(COLS - 128, COLS)), joined(right_ref, rim, one))
    after = joined(sec_ref, every, slice(128, 256))
    before = joined(sec_ref, every, slice(COLS - 256, COLS - 128))
    windows = ((0, *lefts, after), (BLOCKS - 1, before, *rights))
    for place, (block, *cols) in enumerate(windows):
        near = jnp.concatenate(
            [half_turned(cols[0], cols[1]), half_turned(cols[1], cols[2])], axis=1
        )
        edge_ref[:, place * 128 : (place + 1) * 128] = jnp.dot(
            near,
            sinc_band(start_ref, taps_ref, place_ref[1] * BLOCKS + block),
            preferred_element_type=F32,
        )


def reference_side(*arrays):
    smem = pl.BlockSpec(memory_space=pltpu.SMEM)
    vmem = pl.BlockSpec(memory_space=pltpu.VMEM)
    return pl.pallas_call(
        reference_kernel,
        out_shape=(
            jax.ShapeDtypeStruct((PAIRS * CHIP_LEN, 256), F32),
            jax.ShapeDtypeStruct((2 * LINES, 256), F32),
        ),
        in_specs=[smem] + [vmem] * 7,
        out_specs=(vmem, vmem),
        scratch_shapes=[
            pltpu.VMEM((2 * CHIP_LEN, SCRATCH_BLOCKS * 128), BF),
            pltpu.VMEM((2 * CHIP_LEN, CHIPS * 64), BF),
            pltpu.VMEM((2 * CHIP_LEN, CHIPS * 64), BF),
        ],
        compiler_params=pltpu.CompilerParams(vmem_limit_bytes=16 * 2**20),
        cost_estimate=pl.CostEstimate(
            flops=2 * 10**9, bytes_accessed=6 * 10**6, transcendentals=0
        ),
        name="reference_side",
    )(*arrays)


def estimate_kernel(
    off_ref,
    offv_ref,
    sec_ref,
    up_ref,
    down_ref,
    left_ref,
    right_ref,
    above_ref,
    below_ref,
    table_ref,
    spec_ref,
    sum_ref,
    edge_ref,
    pick_ref,
    est_ref,
    out_ref,
    scols_ref,
    chips_ref,
    half_ref,
    tot_ref,
    mom_ref,
    lines_ref,
    packed_ref,
    sems,
):
    for part in range(2):
        base = part * ROWS
        own = base + MARGIN
        low = own + LINES
        for to, side_ref, cols in (
            (0, left_ref, slice(0, 128)),
            (SCRATCH_BLOCKS - 2, right_ref, slice(128, 256)),
        ):
            scols_ref[to, base:own, :] = above_ref[part, :, cols].astype(F32)
            scols_ref[to, own:low, :] = side_ref[part, CHIP_LEN:, :].astype(F32)
            scols_ref[to, low : base + ROWS, :] = below_ref[part, :, cols].astype(F32)
        scols_ref[SCRATCH_BLOCKS - 1, base : base + ROWS, :] = jnp.zeros((ROWS, 128), F32)

    def widen(step, carry):
        for member in range(2):
            block = step * 2 + member
            at = pl.ds(pl.multiple_of(block * 128, 128), 128)
            to = block + 1
            for part in range(2):
                base = part * ROWS
                own = base + MARGIN
                scols_ref[to, base:own, :] = up_ref[part, :, at].astype(F32)
                scols_ref[to, own : own + LINES, :] = sec_ref[part, :, at].astype(F32)
                scols_ref[to, own + LINES : base + ROWS, :] = down_ref[part, :, at].astype(F32)
        return carry

    lax.fori_loop(0, BLOCKS // 2, widen, 0)

    lane = iota((CHIP_LEN, 128), 1)

    def cut(step, carry):
        for member in range(2):
            pair = step * 2 + member
            to = pl.multiple_of(pair * 128, 128)
            for part in range(2):
                found = []
                for side in range(2):
                    chip = pair * 2 + side
                    row = off_ref[0, chip] + (FIRST_ROW + MARGIN + part * ROWS)
                    col = chip * SPACING + off_ref[1, chip] + 112
                    block = col >> 7
                    turn = col & 127
                    near = scols_ref[block, pl.ds(row, CHIP_LEN), :]
                    far = scols_ref[block + 1, pl.ds(row, CHIP_LEN), :]
                    found.append(
                        pltpu.roll(
                            jnp.where(lane >= turn, near, far), (128 + side * 64 - turn) & 127, 1
                        )
                    )
                chips_ref[part * CHIP_LEN : (part + 1) * CHIP_LEN, pl.ds(to, 128)] = jnp.where(
                    lane < 64, found[0], found[1]
                ).astype(BF)
        return carry

    lax.fori_loop(0, PAIRS // 2, cut, 0)
    first_pass(table_ref, chips_ref, half_ref)

    lag_row = (iota((LAG_COUNT, 128), 0) - LAG_COUNT // 2).astype(F32) / OVERSAMPLE

    def correlate(step, carry):
        rows = pl.ds(pl.multiple_of(step * GROUP * CHIP_LEN, 512), GROUP * CHIP_LEN)
        spec_sec = jnp.dot(
            side_by_side(half_ref, [step * GROUP + m for m in range(GROUP)]),
            table_ref[256:512, :],
            preferred_element_type=F32,
        )
        rr, ri = spec_ref[rows, :128], spec_ref[rows, 128:]
        sr, si = spec_sec[:, :128], spec_sec[:, 128:]
        cross = jnp.concatenate([rr * sr + ri * si, ri * sr - rr * si], axis=1).astype(BF)
        middle = jnp.dot(cross, table_ref[512:768, :], preferred_element_type=F32).astype(BF)
        columns = [
            jnp.concatenate(
                [
                    middle[m * CHIP_LEN : (m + 1) * CHIP_LEN, :128],
                    middle[m * CHIP_LEN : (m + 1) * CHIP_LEN, 128:],
                ],
                axis=0,
            )
            for m in range(GROUP)
        ]
        corr = jnp.dot(
            table_ref[768:864, 0:128],
            jnp.concatenate(columns, axis=1),
            preferred_element_type=F32,
        )
        for m in range(GROUP):
            re = corr[:LAG_COUNT, m * 128 : (m + 1) * 128]
            im = corr[LAG_COUNT:, m * 128 : (m + 1) * 128]
            energy = re * re + im * im
            weight = energy * energy
            row = pl.ds(step * GROUP + m, 1)
            tot_ref[row, :] = jnp.sum(weight, axis=0, keepdims=True)
            mom_ref[row, :] = jnp.sum(weight * lag_row, axis=0, keepdims=True)
        return carry

    lax.fori_loop(0, PAIRS // GROUP, correlate, 0)

    wide = (PAIRS, 128)
    lanes = iota(wide, 1)
    total = tot_ref[...]
    moment = mom_ref[...]
    lag_lane = ((lanes & 63) - LAG_COUNT // 2).astype(F32) / OVERSAMPLE
    sides = []
    for side in range(2):
        mask = (lanes < 64) if side == 0 else (lanes >= 64)

        def over(values):
            return jnp.sum(jnp.where(mask, values, 0.0), axis=1, keepdims=True)

        whole = over(total) + EPS
        sides.append((over(moment) / whole, over(total * lag_lane) / whole))
    own_chip = (lanes >> 1) == iota(wide, 0)
    even = (lanes & 1) == 0

    def spread(which):
        values = jnp.where(even, sides[0][which], sides[1][which])
        return jnp.sum(jnp.where(own_chip, values, 0.0), axis=0, keepdims=True)

    offsets = offv_ref[...].astype(F32)
    est_az = offsets[0:1, :] + spread(0)
    est_rg = offsets[1:2, :] + spread(1)
    est_ref[0:1, :] = est_az
    est_ref[1:2, :] = est_rg
    angle = PHASE_RATE * est_az
    cos_all = jnp.broadcast_to(jnp.cos(angle), (8, 128))
    sin_all = jnp.broadcast_to(jnp.sin(angle), (8, 128))

    def turned(block):
        if block in (0, BLOCKS - 1):
            summed = edge_ref[:, 0:128] if block == 0 else edge_ref[:, 128:256]
        else:
            summed = sum_ref[:, block * 128 : (block + 1) * 128]
        chip = block * 4 + (iota((8, 128), 1) >> 5)
        cosine = jnp.take_along_axis(cos_all, chip, axis=1)[0:1, :]
        sine = jnp.take_along_axis(sin_all, chip, axis=1)[0:1, :]
        re, im = summed[:LINES], summed[LINES:]
        half = block // HALF
        at = slice((block - half * HALF) * 128, (block - half * HALF + 1) * 128)
        base = half * 2 * LINES
        lines_ref[base : base + LINES, at] = (re * cosine + im * sine).astype(BF)
        lines_ref[base + LINES : base + 2 * LINES, at] = (im * cosine - re * sine).astype(BF)

    copies = []
    for first in range(0, WIDTH, 256):
        at = slice(first, first + 256)
        for block in (first // 128, first // 128 + 1):
            turned(block)
            turned(block + HALF)
        packed_ref[:, at] = jnp.dot(
            pick_ref[...], lines_ref[:, at], preferred_element_type=F32
        ).astype(BF)
        copy = pltpu.make_async_copy(
            packed_ref.at[:, at], out_ref.at[:, at], sems.at[first // 256]
        )
        copy.start()
        copies.append(copy)
    for copy in copies:
        copy.wait()


def estimate(off, offv, *arrays):
    smem = pl.BlockSpec(memory_space=pltpu.SMEM)
    vmem = pl.BlockSpec(memory_space=pltpu.VMEM)
    hbm = pl.BlockSpec(memory_space=pltpu.HBM)
    return pl.pallas_call(
        estimate_kernel,
        out_shape=(
            jax.ShapeDtypeStruct((2, 128), F32),
            jax.ShapeDtypeStruct((OWNERS * 8, WIDTH), BF),
        ),
        in_specs=[smem] + [vmem] * 13,
        out_specs=(vmem, hbm),
        scratch_shapes=[
            pltpu.VMEM((SCRATCH_BLOCKS, 2 * ROWS, 128), F32),
            pltpu.VMEM((2 * CHIP_LEN, CHIPS * 64), BF),
            pltpu.VMEM((2 * CHIP_LEN, CHIPS * 64), BF),
            pltpu.VMEM((PAIRS, 128), F32),
            pltpu.VMEM((PAIRS, 128), F32),
            pltpu.VMEM((4 * LINES, WIDTH), BF),
            pltpu.VMEM((OWNERS * 8, WIDTH), BF),
            pltpu.SemaphoreType.DMA((WIDTH // 256,)),
        ],
        compiler_params=pltpu.CompilerParams(vmem_limit_bytes=36 * 2**20),
        cost_estimate=pl.CostEstimate(
            flops=6 * 10**9, bytes_accessed=20 * 10**6, transcendentals=0
        ),
        name="estimate",
    )(off, offv, *arrays)


def place_kernel(pick_ref, arr_ref, out_ref):
    pick = pick_ref[...]
    for first in range(0, WIDTH, 256):
        lines = jnp.dot(
            pick,
            arr_ref[:, 0, :, first : first + 256].reshape(128, 256),
            preferred_element_type=F32,
        ).astype(BF)
        for half in range(2):
            at = slice(half * WIDTH + first, half * WIDTH + first + 256)
            for part in range(2):
                base = half * 64 + part * OWNER_CAP
                out_ref[part, :, at] = lines[base : base + OWNER_CAP, :]


def place_lines(pick, arrived):
    return pl.pallas_call(
        place_kernel,
        grid=(PIECES,),
        out_shape=jax.ShapeDtypeStruct((2, OWNER_CAP, COLS * PIECES), BF),
        in_specs=[
            pl.BlockSpec((128, 128), lambda r: (0, 0)),
            pl.BlockSpec((TILES, 1, 8, WIDTH), lambda r: (0, r, 0, 0)),
        ],
        out_specs=pl.BlockSpec((2, OWNER_CAP, COLS), lambda r: (0, 0, r)),
        compiler_params=pltpu.CompilerParams(vmem_limit_bytes=20 * 2**20),
        cost_estimate=pl.CostEstimate(
            flops=10**9, bytes_accessed=8 * 10**6, transcendentals=0
        ),
        name="place_lines",
    )(pick, arrived)


def owner_table(src_row, line_owner, me):
    tile = src_row // LINES
    owned = line_owner == me
    ids = jnp.arange(ALL_LINES, dtype=jnp.int32)
    before = owned[None, :] & (ids[None, :] < ids[:, None])
    rank = jnp.sum(before.astype(jnp.int32), axis=1)
    rank_tile = jnp.sum((before & (tile[None, :] == tile[:, None])).astype(jnp.int32), axis=1)
    outs = jnp.arange(OWNER_CAP, dtype=jnp.int32)
    hit = owned[None, :] & (rank[None, :] == outs[:, None])
    code = jnp.sum(jnp.where(hit, (tile * 2 + rank_tile + 1)[None, :], 0), axis=1) - 1
    rows = jnp.arange(128, dtype=jnp.int32)[:, None]
    cols = jnp.arange(128, dtype=jnp.int32)[None, :]
    slot = jnp.tile(code, 4)[:, None]
    pick = (
        (slot == (cols >> 3) * 2 + ((cols >> 1) & 1))
        & ((rows >> 6) == ((cols >> 2) & 1))
        & (((rows >> 5) & 1) == (cols & 1))
    )
    return pick.astype(BF)


def neighbours(axis, first, last):
    count = lax.axis_size(axis)
    up = [(i, i + 1) for i in range(count - 1)]
    down = [(i + 1, i) for i in range(count - 1)]
    return lax.ppermute(last, axis, up), lax.ppermute(first, axis, down)


def per_device(
    reference_slc, secondary_slc, chip_offsets, src_row, line_owner, band_start, band_taps
):
    az = lax.axis_index("az")
    rg = lax.axis_index("rg")
    place = jnp.stack([az, rg]).astype(jnp.int32)
    starts = band_start.reshape(PIECES * BLOCKS, 128)
    table = kernel_table()
    head, tail, first, last = rims(reference_slc, secondary_slc)
    left, right = neighbours("rg", first, last)
    up, down = neighbours("az", head, tail)

    def corner(rows):
        return jnp.concatenate([left[:, rows, :], right[:, rows, :]], axis=2)

    above, below = neighbours(
        "az",
        corner(slice(CHIP_LEN, CHIP_LEN + MARGIN)),
        corner(slice(CHIP_LEN + LINES - MARGIN, CHIP_LEN + LINES)),
    )
    summed, pick_sent = resample_inner(
        place,
        secondary_slc.reshape(2 * LINES, COLS),
        starts,
        band_taps,
        src_row.reshape(1, ALL_LINES),
        line_owner.reshape(1, ALL_LINES),
    )
    spectra, edges = reference_side(
        place, reference_slc, secondary_slc, left, right, table, starts, band_taps
    )
    off = chip_offsets[:, 0, :]
    offv = jnp.pad(off, ((0, 0), (0, 128 - CHIPS)))
    est, packed = estimate(
        off,
        offv,
        secondary_slc,
        up,
        down,
        left,
        right,
        above,
        below,
        table,
        spectra,
        summed,
        edges,
        pick_sent,
    )
    arrived = lax.all_to_all(packed, BOTH, 0, 0, tiled=True)
    pick = owner_table(src_row, line_owner, az * PIECES + rg)
    resampled = place_lines(pick, arrived.reshape(TILES, PIECES, 8, WIDTH))
    return est[:, None, :CHIPS], resampled


def solution(mesh):
    return jax.shard_map(
        per_device,
        mesh=mesh,
        in_specs=(
            P(None, "az", "rg"),
            P(None, "az", "rg"),
            P(None, "az", "rg"),
            P(),
            P(),
            P(),
            P(),
        ),
        out_specs=(P(None, "az", "rg"), P(None, BOTH, None)),
        check_vma=False,
    )
```

```python
import math

import jax
import jax.numpy as jnp
import ml_dtypes
import numpy as np
from jax import lax
from jax.experimental import pallas as pl
from jax.experimental.pallas import tpu as pltpu
from jax.sharding import PartitionSpec as P

CHIP_LEN = 64
OVERSAMPLE = 16
LAG_COUNT = 48
TAP_COUNT = 8
SPACING = 32
MARGIN = 64
PHASE_RATE = 2.0
EPS = 1e-06

TILES = 16
PIECES = 8
OWNERS = 128
LINES = 96
COLS = 3072
BLOCKS = COLS // 128
ALL_LINES = 1536
CHIPS = 96
PAIRS = CHIPS // 2
OWNER_CAP = 32
FIRST_ROW = 16
ROWS = LINES + 2 * MARGIN
HALF = BLOCKS // 2
WIDTH = HALF * 128
LINE_SPAN = 256
SCRATCH_BLOCKS = BLOCKS + 3
GROUP = 8
RIM_VMEM = 61 * 2**20
BOTH = ("az", "rg")
BF = jnp.bfloat16
F32 = jnp.float32


def numpy_tables():
    ids = np.arange(CHIP_LEN)
    angles = -2.0 * math.pi / CHIP_LEN * (ids[:, None] * ids[None, :] % CHIP_LEN)
    scale = 1.0 / math.sqrt(CHIP_LEN)

    def low(values):
        return values.astype(np.float32).astype(ml_dtypes.bfloat16).astype(np.float32)

    four = (low(np.cos(angles) * scale), low(np.sin(angles) * scale))
    steps = np.arange(LAG_COUNT) - LAG_COUNT // 2
    freq = np.where(ids < CHIP_LEN // 2, ids, ids - CHIP_LEN)
    turns = steps[:, None] * freq[None, :] % (OVERSAMPLE * CHIP_LEN)
    lifted = 2.0 * math.pi / (OVERSAMPLE * CHIP_LEN) * turns
    lift = (low(np.cos(lifted) * scale), low(np.sin(lifted) * scale))
    return four, lift


def kernel_table():
    four, lift = numpy_tables()

    def stacked(re, im):
        out = np.zeros((2 * re.shape[0], 256), np.float32)
        out[:, :128] = np.block([[re, -im], [im, re]])
        return out

    def paired(re, im, starts):
        out = np.zeros((2, 128, 2, 2, 64), np.float32)
        count = re.shape[0]
        for chip, first in enumerate(starts):
            rows = slice(first, first + CHIP_LEN)
            out[0, rows, 0, chip, :count] = re.T
            out[0, rows, 1, chip, :count] = im.T
            out[1, rows, 0, chip, :count] = -im.T
            out[1, rows, 1, chip, :count] = re.T
        return out.reshape(256, 256)

    whole = np.concatenate(
        [
            paired(*four, (0, 32)),
            paired(*four, (0, 64)),
            paired(*lift, (0, 64)),
            stacked(*lift),
            stacked(*four),
        ]
    )
    return jnp.asarray(whole.astype(ml_dtypes.bfloat16))


smem = pl.BlockSpec(memory_space=pltpu.SMEM)
vmem = pl.BlockSpec(memory_space=pltpu.VMEM)
hbm = pl.BlockSpec(memory_space=pltpu.HBM)


def iota(shape, dim):
    return lax.broadcasted_iota(jnp.int32, shape, dim)


def half_turned(left, right):
    lane = iota(left.shape, 1)
    return pltpu.roll(jnp.where(lane >= 64, left.astype(F32), right.astype(F32)), 64, 1).astype(BF)


def begin(sems, *pairs):
    started = [pltpu.make_async_copy(src, dst, sems.at[n]) for n, (src, dst) in enumerate(pairs)]
    for copy in started:
        copy.start()
    return started


def band_copies(rg, start_hbm, taps_hbm, start_ref, taps_ref):
    return (
        (start_hbm.at[pl.ds(pl.multiple_of(rg * BLOCKS, 8), BLOCKS), :], start_ref),
        (taps_hbm.at[:, pl.ds(pl.multiple_of(rg * COLS, 128), COLS)], taps_ref),
    )


def sinc_band(start_ref, taps_ref, block):
    start = start_ref[pl.ds(block, 1), :] - block * 128 + MARGIN
    taps = taps_ref[:, pl.ds(pl.multiple_of(block * 128, 128), 128)].astype(F32)
    offset = iota((256, 128), 0) - start
    band = jnp.zeros((256, 128), F32)
    for tap in range(TAP_COUNT):
        band = jnp.where(offset == tap, taps[tap : tap + 1, :], band)
    return band.astype(BF)


def resample_kernel(
    place_ref,
    sec_hbm,
    start_hbm,
    taps_hbm,
    src_ref,
    own_ref,
    sum_ref,
    pick_ref,
    sec_ref,
    start_ref,
    taps_ref,
    shift_ref,
    sems,
):
    az = place_ref[0]
    rg = place_ref[1]
    fetch = begin(
        sems, (sec_hbm, sec_ref), *band_copies(rg, start_hbm, taps_hbm, start_ref, taps_ref)
    )

    line_block = jnp.minimum(jnp.maximum(az * LINES - 8, 0) // 128, ALL_LINES // 128 - 2)

    def spanned(ref):
        return jnp.concatenate(
            [ref[pl.ds(line_block, 1), :], ref[pl.ds(line_block + 1, 1), :]], axis=1
        )

    local = spanned(src_ref) - az * LINES
    owner = spanned(own_ref)
    here = (local >= 0) & (local < LINES)
    tagged = jnp.where(here, owner, -1).astype(F32)
    tagged_col = jnp.transpose(jnp.broadcast_to(tagged, (128, LINE_SPAN)))
    tagged_col = jnp.concatenate([tagged_col, tagged_col], axis=1)
    square = (LINE_SPAN, LINE_SPAN)
    earlier = iota(square, 0) < iota(square, 1)
    same = (tagged_col == tagged) & earlier
    rank = jnp.sum(jnp.where(same, 1.0, 0.0), axis=0, keepdims=True)
    slot = jnp.where(here, tagged * 2.0 + rank, -1.0)
    marked = jnp.where(here, local + 1, 0).astype(F32)
    marked_col = jnp.transpose(jnp.broadcast_to(marked, (128, LINE_SPAN))).astype(BF)
    for first in range(0, 1024, 256):
        ids = iota((256, LINE_SPAN), 0) + first
        wanted = ((ids >> 3) * 2 + ((ids >> 1) & 1)).astype(F32)
        hot = jnp.where(slot == wanted, 1.0, 0.0).astype(BF)
        found = jnp.dot(hot, marked_col, preferred_element_type=F32).astype(jnp.int32)
        ids = iota((256, 128), 0) + first
        base = ((ids >> 2) & 1) * (2 * LINES) + (ids & 1) * LINES - 1
        target = jnp.where(found > 0, found + base, -1)
        for block in range(3):
            lanes = iota((256, 128), 1) + block * 128
            pick_ref[first : first + 256, block * 128 : (block + 1) * 128] = jnp.where(
                lanes == target, 1.0, 0.0
            ).astype(BF)

    for copy in fetch:
        copy.wait()

    def move(step, carry):
        at = pl.multiple_of(step * 128, 128)
        shift_ref[:, pl.ds(at, 128)] = half_turned(
            sec_ref[:, pl.ds(pl.multiple_of(at - 128, 128), 128)], sec_ref[:, pl.ds(at, 128)]
        )
        return carry

    lax.fori_loop(1, BLOCKS, move, 0)
    start_ref[...] = start_ref[...] - rg * COLS

    def window(step, carry):
        for member in range(2):
            block = step * 2 + member + 1
            at = pl.multiple_of(block * 128, 128)
            sum_ref[:, pl.ds(at, 128)] = jnp.dot(
                shift_ref[:, pl.ds(at, 256)],
                sinc_band(start_ref, taps_ref, block),
                preferred_element_type=F32,
            )
        return carry

    lax.fori_loop(0, (BLOCKS - 2) // 2, window, 0)


def resample_inner(place, sec, starts, taps, src, own):
    return pl.pallas_call(
        resample_kernel,
        out_shape=(
            jax.ShapeDtypeStruct((2 * LINES, COLS), F32),
            jax.ShapeDtypeStruct((OWNERS * 8, 4 * LINES), BF),
        ),
        in_specs=[smem] + [hbm] * 3 + [vmem] * 2,
        out_specs=(vmem, vmem),
        scratch_shapes=[
            pltpu.VMEM((2 * LINES, COLS), BF),
            pltpu.VMEM((BLOCKS, 128), jnp.int32),
            pltpu.VMEM((TAP_COUNT, COLS), BF),
            pltpu.VMEM((2 * LINES, COLS), BF),
            pltpu.SemaphoreType.DMA((3,)),
        ],
        compiler_params=pltpu.CompilerParams(vmem_limit_bytes=16 * 2**20),
        cost_estimate=pl.CostEstimate(
            flops=2 * 10**9, bytes_accessed=6 * 10**6, transcendentals=0
        ),
        name="resample_inner",
    )(place, sec, starts, taps, src, own)


def rims_kernel(sec_hbm, head_ref, tail_ref, sems):
    for copy in begin(
        sems,
        (sec_hbm.at[:, 0:MARGIN, :], head_ref),
        (sec_hbm.at[:, LINES - MARGIN : LINES, :], tail_ref),
    ):
        copy.wait()


def rims(sec):
    rows = jax.ShapeDtypeStruct((2, MARGIN, COLS), BF)
    return pl.pallas_call(
        rims_kernel,
        out_shape=(rows, rows),
        in_specs=[hbm],
        out_specs=(vmem, vmem),
        scratch_shapes=[pltpu.SemaphoreType.DMA((2,))],
        compiler_params=pltpu.CompilerParams(vmem_limit_bytes=RIM_VMEM),
        name="rims",
    )(sec)


def edges_kernel(ref_hbm, sec_hbm, up_ref, down_ref, first_ref, last_ref, sems):
    own = CHIP_LEN + MARGIN
    pairs = []
    for to_ref, cols in ((first_ref, slice(0, 128)), (last_ref, slice(COLS - 128, COLS))):
        pairs += [
            (
                ref_hbm.at[:, FIRST_ROW : FIRST_ROW + CHIP_LEN, cols],
                to_ref.at[:, 0:CHIP_LEN, :],
            ),
            (sec_hbm.at[:, :, cols], to_ref.at[:, own : own + LINES, :]),
        ]
    fetch = begin(sems, *pairs)
    for to_ref, cols in ((first_ref, slice(0, 128)), (last_ref, slice(COLS - 128, COLS))):
        for part in range(2):
            to_ref[part, CHIP_LEN:own, :] = up_ref[part, :, cols]
            to_ref[part, own + LINES :, :] = down_ref[part, :, cols]
    for copy in fetch:
        copy.wait()


def rg_edges(ref, sec, up, down):
    cols = jax.ShapeDtypeStruct((2, CHIP_LEN + ROWS, 128), BF)
    return pl.pallas_call(
        edges_kernel,
        out_shape=(cols, cols),
        in_specs=[hbm, hbm, vmem, vmem],
        out_specs=(vmem, vmem),
        scratch_shapes=[pltpu.SemaphoreType.DMA((4,))],
        compiler_params=pltpu.CompilerParams(vmem_limit_bytes=8 * 2**20),
        name="rg_edges",
    )(ref, sec, up, down)


def side_by_side(half, pairs):
    rows = []
    for pair in pairs:
        if isinstance(pair, int):
            at = slice(pair * 128, (pair + 1) * 128)
        else:
            at = pl.ds(pl.multiple_of(pair * 128, 128), 128)
        rows.append(
            jnp.concatenate([half[0:CHIP_LEN, at], half[CHIP_LEN : 2 * CHIP_LEN, at]], axis=1)
        )
    return jnp.concatenate(rows, axis=0)


def first_pass(table_ref, chips_ref, half_ref):
    fwd = table_ref[864:992, 0:128]
    for first in range(0, CHIPS * 64, 1024):
        half_ref[:, first : first + 1024] = jnp.dot(
            fwd, chips_ref[:, first : first + 1024], preferred_element_type=F32
        ).astype(BF)


def even_pair(near, here):
    lane = iota(near.shape, 1)
    return pltpu.roll(jnp.where(lane >= 112, near, here), 16, 1).astype(BF)


def odd_pair(here, far):
    lane = iota(far.shape, 1)
    return pltpu.roll(jnp.where(lane >= 48, here, far), 80, 1).astype(BF)


def reference_kernel(ref_hbm, table_ref, spec_ref, rcols_ref, chips_ref, half_ref, sems):
    rows = slice(FIRST_ROW, FIRST_ROW + CHIP_LEN)
    fetch = begin(
        sems,
        *(
            (
                ref_hbm.at[part, rows, :],
                rcols_ref.at[part * CHIP_LEN : (part + 1) * CHIP_LEN, 128 : 128 + COLS],
            )
            for part in range(2)
        ),
    )
    none = jnp.zeros((2 * CHIP_LEN, 128), BF)
    rcols_ref[:, 0:128] = none
    rcols_ref[:, 128 + COLS : 256 + COLS] = none
    for copy in fetch:
        copy.wait()

    def cut(step, carry):
        def block(at):
            return rcols_ref[:, pl.ds(pl.multiple_of(at * 128, 128), 128)].astype(F32)

        near, here, far = block(step), block(step + 1), block(step + 2)
        to = pl.multiple_of(step * 256, 256)
        chips_ref[:, pl.ds(to, 128)] = even_pair(near, here)
        chips_ref[:, pl.ds(pl.multiple_of(to + 128, 128), 128)] = odd_pair(here, far)
        return carry

    lax.fori_loop(0, PAIRS // 2, cut, 0)
    first_pass(table_ref, chips_ref, half_ref)

    for step in range(PAIRS // GROUP):
        at = step * GROUP * CHIP_LEN
        spec_ref[at : at + GROUP * CHIP_LEN, :] = jnp.dot(
            side_by_side(half_ref, range(step * GROUP, (step + 1) * GROUP)),
            table_ref[0:256, :],
            preferred_element_type=F32,
        )


def reference_side(ref, table):
    return pl.pallas_call(
        reference_kernel,
        out_shape=jax.ShapeDtypeStruct((PAIRS * CHIP_LEN, 256), F32),
        in_specs=[hbm, vmem],
        out_specs=vmem,
        scratch_shapes=[
            pltpu.VMEM((2 * CHIP_LEN, SCRATCH_BLOCKS * 128), BF),
            pltpu.VMEM((2 * CHIP_LEN, CHIPS * 64), BF),
            pltpu.VMEM((2 * CHIP_LEN, CHIPS * 64), BF),
            pltpu.SemaphoreType.DMA((2,)),
        ],
        compiler_params=pltpu.CompilerParams(vmem_limit_bytes=12 * 2**20),
        cost_estimate=pl.CostEstimate(
            flops=2 * 10**9, bytes_accessed=6 * 10**6, transcendentals=0
        ),
        name="reference_side",
    )(ref, table)


def cut_pair(off_ref, scols_ref, pair, first_block):
    lane = iota((CHIP_LEN, 128), 1)
    parts = []
    for part in range(2):
        found = []
        for side in range(2):
            chip = pair * 2 + side
            row = off_ref[0, chip] + (FIRST_ROW + MARGIN + part * ROWS)
            col = chip * SPACING + off_ref[1, chip] + 112
            block = (col >> 7) - first_block
            turn = col & 127
            near = scols_ref[block, pl.ds(row, CHIP_LEN), :]
            far = scols_ref[block + 1, pl.ds(row, CHIP_LEN), :]
            found.append(
                pltpu.roll(jnp.where(lane >= turn, near, far), (128 + side * 64 - turn) & 127, 1)
            )
        parts.append(jnp.where(lane < 64, found[0], found[1]).astype(BF))
    return parts


def correlated(spec_ref, spec_sec, table_ref, count):
    rr, ri = spec_ref[:, :128], spec_ref[:, 128:]
    sr, si = spec_sec[:, :128], spec_sec[:, 128:]
    cross = jnp.concatenate([rr * sr + ri * si, ri * sr - rr * si], axis=1).astype(BF)
    middle = jnp.dot(cross, table_ref[512:768, :], preferred_element_type=F32).astype(BF)
    columns = []
    for m in range(count):
        rows = middle[m * CHIP_LEN : (m + 1) * CHIP_LEN]
        columns.append(jnp.concatenate([rows[:, :128], rows[:, 128:]], axis=0))
    corr = jnp.dot(
        table_ref[768:864, 0:128], jnp.concatenate(columns, axis=1), preferred_element_type=F32
    )
    lag_row = (iota((LAG_COUNT, 128), 0) - LAG_COUNT // 2).astype(F32) / OVERSAMPLE
    sums = []
    for m in range(count):
        re = corr[:LAG_COUNT, m * 128 : (m + 1) * 128]
        im = corr[LAG_COUNT:, m * 128 : (m + 1) * 128]
        energy = re * re + im * im
        weight = energy * energy
        sums.append(
            (
                jnp.sum(weight, axis=0, keepdims=True),
                jnp.sum(weight * lag_row, axis=0, keepdims=True),
            )
        )
    return sums


def inner_kernel(
    off_ref,
    sec_hbm,
    up_ref,
    down_ref,
    table_ref,
    spec_ref,
    tot_ref,
    mom_ref,
    sec_ref,
    scols_ref,
    chips_ref,
    half_ref,
    sems,
):
    fetch = begin(sems, (sec_hbm, sec_ref))
    none = jnp.zeros((2 * ROWS, 128), F32)
    for block in (0, SCRATCH_BLOCKS - 2, SCRATCH_BLOCKS - 1):
        scols_ref[block] = none

    def widen_rims(step, carry):
        for member in range(2):
            block = step * 2 + member
            at = pl.ds(pl.multiple_of(block * 128, 128), 128)
            for part in range(2):
                base = part * ROWS
                low = base + MARGIN + LINES
                scols_ref[block + 1, base : base + MARGIN, :] = up_ref[part, :, at].astype(F32)
                scols_ref[block + 1, low : base + ROWS, :] = down_ref[part, :, at].astype(F32)
        return carry

    lax.fori_loop(0, BLOCKS // 2, widen_rims, 0)
    for copy in fetch:
        copy.wait()

    def widen(step, carry):
        for member in range(2):
            block = step * 2 + member
            at = pl.ds(pl.multiple_of(block * 128, 128), 128)
            for part in range(2):
                own = part * ROWS + MARGIN
                scols_ref[block + 1, own : own + LINES, :] = sec_ref[part, :, at].astype(F32)
        return carry

    lax.fori_loop(0, BLOCKS // 2, widen, 0)

    def cut(step, carry):
        for member in range(2):
            pair = step * 2 + member
            to = pl.ds(pl.multiple_of(pair * 128, 128), 128)
            re, im = cut_pair(off_ref, scols_ref, pair, 0)
            chips_ref[0:CHIP_LEN, to] = re
            chips_ref[CHIP_LEN : 2 * CHIP_LEN, to] = im
        return carry

    lax.fori_loop(0, PAIRS // 2, cut, 0)
    first_pass(table_ref, chips_ref, half_ref)

    def correlate(step, carry):
        size = GROUP * CHIP_LEN
        spec_sec = jnp.dot(
            side_by_side(half_ref, [step * GROUP + m for m in range(GROUP)]),
            table_ref[256:512, :],
            preferred_element_type=F32,
        )
        spec = spec_ref[pl.ds(pl.multiple_of(step * size, size), size), :]
        for m, (total, moment) in enumerate(correlated(spec, spec_sec, table_ref, GROUP)):
            row = pl.ds(step * GROUP + m, 1)
            tot_ref[row, :] = total
            mom_ref[row, :] = moment
        return carry

    lax.fori_loop(0, PAIRS // GROUP, correlate, 0)


def inner_pairs(off, sec, up, down, table, spectra):
    sums = jax.ShapeDtypeStruct((PAIRS, 128), F32)
    return pl.pallas_call(
        inner_kernel,
        out_shape=(sums, sums),
        in_specs=[smem, hbm] + [vmem] * 4,
        out_specs=(vmem, vmem),
        scratch_shapes=[
            pltpu.VMEM((2, LINES, COLS), BF),
            pltpu.VMEM((SCRATCH_BLOCKS, 2 * ROWS, 128), F32),
            pltpu.VMEM((2 * CHIP_LEN, CHIPS * 64), BF),
            pltpu.VMEM((2 * CHIP_LEN, CHIPS * 64), BF),
            pltpu.SemaphoreType.DMA((1,)),
        ],
        compiler_params=pltpu.CompilerParams(vmem_limit_bytes=24 * 2**20),
        cost_estimate=pl.CostEstimate(
            flops=6 * 10**9, bytes_accessed=20 * 10**6, transcendentals=0
        ),
        name="inner_pairs",
    )(off, sec, up, down, table, spectra)


def finish_kernel(
    place_ref,
    off_ref,
    offv_ref,
    first_ref,
    last_ref,
    sec_hbm,
    start_hbm,
    taps_hbm,
    left_ref,
    right_ref,
    table_ref,
    tot_ref,
    mom_ref,
    sum_hbm,
    pick_hbm,
    est_ref,
    out_ref,
    sum_ref,
    pick_ref,
    near_ref,
    start_ref,
    taps_ref,
    scols_ref,
    lines_ref,
    packed_ref,
    sems,
    out_sems,
):
    rg = place_ref[1]
    fetch = begin(
        sems,
        *band_copies(rg, start_hbm, taps_hbm, start_ref, taps_ref),
        (sec_hbm.at[:, :, 128:256], near_ref.at[0]),
        (sec_hbm.at[:, :, COLS - 256 : COLS - 128], near_ref.at[1]),
        (sum_hbm, sum_ref),
        (pick_hbm, pick_ref),
    )
    own_rows = slice(CHIP_LEN + MARGIN, CHIP_LEN + MARGIN + LINES)
    sides = (
        (left_ref, first_ref, 0),
        (last_ref, right_ref, 3),
    )
    for near_side, far_side, at in sides:
        for part in range(2):
            base = part * ROWS
            scols_ref[at, base : base + ROWS, :] = near_side[part, CHIP_LEN:, :].astype(F32)
            scols_ref[at + 1, base : base + ROWS, :] = far_side[part, CHIP_LEN:, :].astype(F32)
        scols_ref[at + 2] = jnp.zeros((2 * ROWS, 128), F32)

    def both_parts(ref, rows):
        return jnp.concatenate([ref[0, rows, :], ref[1, rows, :]], axis=0)

    chip_rows = slice(0, CHIP_LEN)
    columns = [
        even_pair(
            both_parts(left_ref, chip_rows).astype(F32),
            both_parts(first_ref, chip_rows).astype(F32),
        ),
        odd_pair(
            both_parts(last_ref, chip_rows).astype(F32),
            both_parts(right_ref, chip_rows).astype(F32),
        ),
        jnp.concatenate(cut_pair(off_ref, scols_ref, 0, 0), axis=0),
        jnp.concatenate(cut_pair(off_ref, scols_ref, PAIRS - 1, BLOCKS - 3), axis=0),
    ]
    half = jnp.dot(
        table_ref[864:992, 0:128],
        jnp.concatenate(columns, axis=1),
        preferred_element_type=F32,
    ).astype(BF)
    spec = jnp.dot(
        side_by_side(half, (0, 1)), table_ref[0:256, :], preferred_element_type=F32
    )
    spec_sec = jnp.dot(
        side_by_side(half, (2, 3)), table_ref[256:512, :], preferred_element_type=F32
    )
    outer = correlated(spec, spec_sec, table_ref, 2)

    wide = (PAIRS, 128)
    lanes = iota(wide, 1)
    pairs = iota(wide, 0)

    def completed(ref, which):
        return jnp.where(
            pairs == 0,
            outer[0][which],
            jnp.where(pairs == PAIRS - 1, outer[1][which], ref[...]),
        )

    total = completed(tot_ref, 0)
    moment = completed(mom_ref, 1)
    lag_lane = ((lanes & 63) - LAG_COUNT // 2).astype(F32) / OVERSAMPLE
    found = []
    for side in range(2):
        mask = (lanes < 64) if side == 0 else (lanes >= 64)

        def over(values):
            return jnp.sum(jnp.where(mask, values, 0.0), axis=1, keepdims=True)

        whole = over(total) + EPS
        found.append((over(moment) / whole, over(total * lag_lane) / whole))
    own_chip = (lanes >> 1) == pairs
    even = (lanes & 1) == 0

    def spread(which):
        values = jnp.where(even, found[0][which], found[1][which])
        return jnp.sum(jnp.where(own_chip, values, 0.0), axis=0, keepdims=True)

    offsets = offv_ref[...].astype(F32)
    est_az = offsets[0:1, :] + spread(0)
    est_rg = offsets[1:2, :] + spread(1)
    est_ref[0:1, :] = est_az
    est_ref[1:2, :] = est_rg
    angle = PHASE_RATE * est_az
    cos_all = jnp.broadcast_to(jnp.cos(angle), (8, 128))
    sin_all = jnp.broadcast_to(jnp.sin(angle), (8, 128))

    for copy in fetch:
        copy.wait()
    start_ref[...] = start_ref[...] - rg * COLS
    every = slice(0, LINES)
    edge_columns = {
        0: (
            both_parts(left_ref, own_rows),
            both_parts(first_ref, own_rows),
            both_parts(near_ref.at[0], every),
        ),
        BLOCKS - 1: (
            both_parts(near_ref.at[1], every),
            both_parts(last_ref, own_rows),
            both_parts(right_ref, own_rows),
        ),
    }

    def turned(block):
        if block in edge_columns:
            cols = edge_columns[block]
            near = jnp.concatenate(
                [half_turned(cols[0], cols[1]), half_turned(cols[1], cols[2])], axis=1
            )
            summed = jnp.dot(
                near, sinc_band(start_ref, taps_ref, block), preferred_element_type=F32
            )
        else:
            summed = sum_ref[:, block * 128 : (block + 1) * 128]
        chip = block * 4 + (iota((8, 128), 1) >> 5)
        cosine = jnp.take_along_axis(cos_all, chip, axis=1)[0:1, :]
        sine = jnp.take_along_axis(sin_all, chip, axis=1)[0:1, :]
        re, im = summed[:LINES], summed[LINES:]
        half = block // HALF
        at = slice((block - half * HALF) * 128, (block - half * HALF + 1) * 128)
        base = half * 2 * LINES
        lines_ref[base : base + LINES, at] = (re * cosine + im * sine).astype(BF)
        lines_ref[base + LINES : base + 2 * LINES, at] = (im * cosine - re * sine).astype(BF)

    copies = []
    for first in range(0, WIDTH, 256):
        at = slice(first, first + 256)
        for block in (first // 128, first // 128 + 1):
            turned(block)
            turned(block + HALF)
        packed_ref[:, at] = jnp.dot(
            pick_ref[...], lines_ref[:, at], preferred_element_type=F32
        ).astype(BF)
        copy = pltpu.make_async_copy(
            packed_ref.at[:, at], out_ref.at[:, at], out_sems.at[first // 256]
        )
        copy.start()
        copies.append(copy)
    for copy in copies:
        copy.wait()


def finish(place, off, offv, first, last, *arrays):
    return pl.pallas_call(
        finish_kernel,
        out_shape=(
            jax.ShapeDtypeStruct((2, 128), F32),
            jax.ShapeDtypeStruct((OWNERS * 8, WIDTH), BF),
        ),
        in_specs=[smem] * 2 + [vmem] * 3 + [hbm] * 3 + [vmem] * 5 + [hbm] * 2,
        out_specs=(vmem, hbm),
        scratch_shapes=[
            pltpu.VMEM((2 * LINES, COLS), F32),
            pltpu.VMEM((OWNERS * 8, 4 * LINES), BF),
            pltpu.VMEM((2, 2, LINES, 128), BF),
            pltpu.VMEM((BLOCKS, 128), jnp.int32),
            pltpu.VMEM((TAP_COUNT, COLS), BF),
            pltpu.VMEM((6, 2 * ROWS, 128), F32),
            pltpu.VMEM((4 * LINES, WIDTH), BF),
            pltpu.VMEM((OWNERS * 8, WIDTH), BF),
            pltpu.SemaphoreType.DMA((6,)),
            pltpu.SemaphoreType.DMA((WIDTH // 256,)),
        ],
        compiler_params=pltpu.CompilerParams(vmem_limit_bytes=52 * 2**20),
        cost_estimate=pl.CostEstimate(
            flops=2 * 10**9, bytes_accessed=10 * 10**6, transcendentals=0
        ),
        name="finish",
    )(place, off, offv, first, last, *arrays)


def place_kernel(pick_ref, arr_ref, out_ref):
    pick = pick_ref[...]
    for first in range(0, WIDTH, 256):
        lines = jnp.dot(
            pick,
            arr_ref[:, 0, :, first : first + 256].reshape(128, 256),
            preferred_element_type=F32,
        ).astype(BF)
        for half in range(2):
            at = slice(half * WIDTH + first, half * WIDTH + first + 256)
            for part in range(2):
                base = half * 64 + part * OWNER_CAP
                out_ref[part, :, at] = lines[base : base + OWNER_CAP, :]


def place_lines(pick, arrived):
    return pl.pallas_call(
        place_kernel,
        grid=(PIECES,),
        out_shape=jax.ShapeDtypeStruct((2, OWNER_CAP, COLS * PIECES), BF),
        in_specs=[
            pl.BlockSpec((128, 128), lambda r: (0, 0)),
            pl.BlockSpec((TILES, 1, 8, WIDTH), lambda r: (0, r, 0, 0)),
        ],
        out_specs=pl.BlockSpec((2, OWNER_CAP, COLS), lambda r: (0, 0, r)),
        compiler_params=pltpu.CompilerParams(vmem_limit_bytes=20 * 2**20),
        cost_estimate=pl.CostEstimate(
            flops=10**9, bytes_accessed=8 * 10**6, transcendentals=0
        ),
        name="place_lines",
    )(pick, arrived)


def owner_table(src_row, line_owner, me):
    tile = src_row // LINES
    owned = line_owner == me
    ids = jnp.arange(ALL_LINES, dtype=jnp.int32)
    before = owned[None, :] & (ids[None, :] < ids[:, None])
    rank = jnp.sum(before.astype(jnp.int32), axis=1)
    rank_tile = jnp.sum((before & (tile[None, :] == tile[:, None])).astype(jnp.int32), axis=1)
    outs = jnp.arange(OWNER_CAP, dtype=jnp.int32)
    hit = owned[None, :] & (rank[None, :] == outs[:, None])
    code = jnp.sum(jnp.where(hit, (tile * 2 + rank_tile + 1)[None, :], 0), axis=1) - 1
    rows = jnp.arange(128, dtype=jnp.int32)[:, None]
    cols = jnp.arange(128, dtype=jnp.int32)[None, :]
    slot = jnp.tile(code, 4)[:, None]
    pick = (
        (slot == (cols >> 3) * 2 + ((cols >> 1) & 1))
        & ((rows >> 6) == ((cols >> 2) & 1))
        & (((rows >> 5) & 1) == (cols & 1))
    )
    return pick.astype(BF)


def neighbours(axis, first, last):
    count = lax.axis_size(axis)
    up = [(i, i + 1) for i in range(count - 1)]
    down = [(i + 1, i) for i in range(count - 1)]
    return lax.ppermute(last, axis, up), lax.ppermute(first, axis, down)


def per_device(
    reference_slc, secondary_slc, chip_offsets, src_row, line_owner, band_start, band_taps
):
    az = lax.axis_index("az")
    rg = lax.axis_index("rg")
    place = jnp.stack([az, rg]).astype(jnp.int32)
    starts = band_start.reshape(PIECES * BLOCKS, 128)
    table = kernel_table()
    up, down = neighbours("az", *rims(secondary_slc))
    summed, pick_sent = resample_inner(
        place,
        secondary_slc.reshape(2 * LINES, COLS),
        starts,
        band_taps,
        src_row.reshape(ALL_LINES // 128, 128),
        line_owner.reshape(ALL_LINES // 128, 128),
    )
    spectra = reference_side(reference_slc, table)
    first, last = rg_edges(reference_slc, secondary_slc, up, down)
    left, right = neighbours("rg", first, last)
    off = chip_offsets[:, 0, :]
    offv = jnp.pad(off, ((0, 0), (0, 128 - CHIPS)))
    total, moment = inner_pairs(off, secondary_slc, up, down, table, spectra)
    est, packed = finish(
        place,
        off,
        offv,
        first,
        last,
        secondary_slc,
        starts,
        band_taps,
        left,
        right,
        table,
        total,
        moment,
        summed,
        pick_sent,
    )
    arrived = lax.all_to_all(packed, BOTH, 0, 0, tiled=True)
    pick = owner_table(src_row, line_owner, az * PIECES + rg)
    resampled = place_lines(pick, arrived.reshape(TILES, PIECES, 8, WIDTH))
    return est[:, None, :CHIPS], resampled


def solution(mesh):
    return jax.shard_map(
        per_device,
        mesh=mesh,
        in_specs=(
            P(None, "az", "rg"),
            P(None, "az", "rg"),
            P(None, "az", "rg"),
            P(),
            P(),
            P(),
            P(),
        ),
        out_specs=(P(None, "az", "rg"), P(None, BOTH, None)),
        check_vma=False,
    )
```

```python
import math

import jax
import jax.numpy as jnp
import ml_dtypes
import numpy as np
from jax import lax
from jax.experimental import pallas as pl
from jax.experimental.pallas import tpu as pltpu
from jax.sharding import PartitionSpec as P

CHIP_LEN = 64
OVERSAMPLE = 16
LAG_COUNT = 48
TAP_COUNT = 8
SPACING = 32
MARGIN = 64
PHASE_RATE = 2.0
EPS = 1e-06

TILES = 16
PIECES = 8
OWNERS = 128
LINES = 96
COLS = 3072
BLOCKS = COLS // 128
ALL_LINES = 1536
CHIPS = 96
PAIRS = CHIPS // 2
OWNER_CAP = 32
FIRST_ROW = 16
ROWS = LINES + 2 * MARGIN
HALF = BLOCKS // 2
WIDTH = HALF * 128
LINE_SPAN = 256
SCRATCH_BLOCKS = BLOCKS + 3
GROUP = 8
BAND_ROWS = 32
TABLE = (992, 256)
RIM_VMEM = 16 * 2**20
OWN_VMEM = 44 * 2**20
BOTH = ("az", "rg")
BF = jnp.bfloat16
F32 = jnp.float32


def numpy_tables():
    ids = np.arange(CHIP_LEN)
    angles = -2.0 * math.pi / CHIP_LEN * (ids[:, None] * ids[None, :] % CHIP_LEN)
    scale = 1.0 / math.sqrt(CHIP_LEN)

    def low(values):
        return values.astype(np.float32).astype(ml_dtypes.bfloat16).astype(np.float32)

    four = (low(np.cos(angles) * scale), low(np.sin(angles) * scale))
    steps = np.arange(LAG_COUNT) - LAG_COUNT // 2
    freq = np.where(ids < CHIP_LEN // 2, ids, ids - CHIP_LEN)
    turns = steps[:, None] * freq[None, :] % (OVERSAMPLE * CHIP_LEN)
    lifted = 2.0 * math.pi / (OVERSAMPLE * CHIP_LEN) * turns
    lift = (low(np.cos(lifted) * scale), low(np.sin(lifted) * scale))
    return four, lift


def kernel_table():
    four, lift = numpy_tables()

    def stacked(re, im):
        out = np.zeros((2 * re.shape[0], 256), np.float32)
        out[:, :128] = np.block([[re, -im], [im, re]])
        return out

    def paired(re, im, starts):
        out = np.zeros((2, 128, 2, 2, 64), np.float32)
        count = re.shape[0]
        for chip, first in enumerate(starts):
            rows = slice(first, first + CHIP_LEN)
            out[0, rows, 0, chip, :count] = re.T
            out[0, rows, 1, chip, :count] = im.T
            out[1, rows, 0, chip, :count] = -im.T
            out[1, rows, 1, chip, :count] = re.T
        return out.reshape(256, 256)

    whole = np.concatenate(
        [
            paired(*four, (0, 32)),
            paired(*four, (0, 64)),
            paired(*lift, (0, 64)),
            stacked(*lift),
            stacked(*four),
        ]
    )
    return jnp.asarray(whole.astype(ml_dtypes.bfloat16))


smem = pl.BlockSpec(memory_space=pltpu.SMEM)
vmem = pl.BlockSpec(memory_space=pltpu.VMEM)
hbm = pl.BlockSpec(memory_space=pltpu.HBM)


def iota(shape, dim):
    return lax.broadcasted_iota(jnp.int32, shape, dim)


def half_turned(left, right):
    lane = iota(left.shape, 1)
    return pltpu.roll(jnp.where(lane >= 64, left.astype(F32), right.astype(F32)), 64, 1).astype(BF)


def begin(sems, *pairs):
    started = [pltpu.make_async_copy(src, dst, sems.at[n]) for n, (src, dst) in enumerate(pairs)]
    for copy in started:
        copy.start()
    return started


def band_copies(rg, start_hbm, taps_hbm, start_ref, taps_ref):
    return (
        (start_hbm.at[pl.ds(pl.multiple_of(rg * BLOCKS, 8), BLOCKS), :], start_ref),
        (taps_hbm.at[:, pl.ds(pl.multiple_of(rg * COLS, 128), COLS)], taps_ref),
    )


def sinc_band(start_ref, taps_ref, block):
    start = start_ref[pl.ds(block, 1), :] - block * 128 + MARGIN
    taps = taps_ref[:, pl.ds(pl.multiple_of(block * 128, 128), 128)].astype(F32)
    chunks = []
    for first in range(0, 256, BAND_ROWS):
        offset = iota((BAND_ROWS, 128), 0) - (start - first)
        band = jnp.zeros((BAND_ROWS, 128), F32)
        for tap in range(TAP_COUNT):
            band = jnp.where(offset == tap, taps[tap : tap + 1, :], band)
        chunks.append(band.astype(BF))
    return jnp.concatenate(chunks, axis=0)


def own_kernel(
    place_ref,
    sec_hbm,
    start_hbm,
    taps_hbm,
    src_ref,
    own_ref,
    ref_hbm,
    table_hbm,
    sum_ref,
    pick_ref,
    spec_ref,
    sec_ref,
    start_ref,
    taps_ref,
    shift_ref,
    table_ref,
    rcols_ref,
    chips_ref,
    half_ref,
    sems,
):
    az = place_ref[0]
    rg = place_ref[1]
    rows = slice(FIRST_ROW, FIRST_ROW + CHIP_LEN)
    fetch = begin(
        sems,
        (sec_hbm, sec_ref),
        *band_copies(rg, start_hbm, taps_hbm, start_ref, taps_ref),
        (table_hbm, table_ref),
        *(
            (
                ref_hbm.at[part, rows, :],
                rcols_ref.at[part * CHIP_LEN : (part + 1) * CHIP_LEN, 128 : 128 + COLS],
            )
            for part in range(2)
        ),
    )

    line_block = jnp.minimum(jnp.maximum(az * LINES - 8, 0) // 128, ALL_LINES // 128 - 2)

    def spanned(ref):
        return jnp.concatenate(
            [ref[pl.ds(line_block, 1), :], ref[pl.ds(line_block + 1, 1), :]], axis=1
        )

    local = spanned(src_ref) - az * LINES
    owner = spanned(own_ref)
    here = (local >= 0) & (local < LINES)
    tagged = jnp.where(here, owner, -1).astype(F32)
    tagged_col = jnp.transpose(jnp.broadcast_to(tagged, (128, LINE_SPAN)))
    tagged_col = jnp.concatenate([tagged_col, tagged_col], axis=1)
    square = (LINE_SPAN, LINE_SPAN)
    earlier = iota(square, 0) < iota(square, 1)
    same = (tagged_col == tagged) & earlier
    rank = jnp.sum(jnp.where(same, 1.0, 0.0), axis=0, keepdims=True)
    slot = jnp.where(here, tagged * 2.0 + rank, -1.0)
    marked = jnp.where(here, local + 1, 0).astype(F32)
    marked_col = jnp.transpose(jnp.broadcast_to(marked, (128, LINE_SPAN))).astype(BF)
    for first in range(0, 1024, 256):
        ids = iota((256, LINE_SPAN), 0) + first
        wanted = ((ids >> 3) * 2 + ((ids >> 1) & 1)).astype(F32)
        hot = jnp.where(slot == wanted, 1.0, 0.0).astype(BF)
        found = jnp.dot(hot, marked_col, preferred_element_type=F32).astype(jnp.int32)
        ids = iota((256, 128), 0) + first
        base = ((ids >> 2) & 1) * (2 * LINES) + (ids & 1) * LINES - 1
        target = jnp.where(found > 0, found + base, -1)
        for block in range(3):
            lanes = iota((256, 128), 1) + block * 128
            pick_ref[first : first + 256, block * 128 : (block + 1) * 128] = jnp.where(
                lanes == target, 1.0, 0.0
            ).astype(BF)

    for copy in fetch:
        copy.wait()

    def move(step, carry):
        at = pl.multiple_of(step * 128, 128)
        shift_ref[:, pl.ds(at, 128)] = half_turned(
            sec_ref[:, pl.ds(pl.multiple_of(at - 128, 128), 128)], sec_ref[:, pl.ds(at, 128)]
        )
        return carry

    lax.fori_loop(1, BLOCKS, move, 0)
    start_ref[...] = start_ref[...] - rg * COLS

    def window(step, carry):
        for member in range(2):
            block = step * 2 + member + 1
            at = pl.multiple_of(block * 128, 128)
            sum_ref[:, pl.ds(at, 128)] = jnp.dot(
                shift_ref[:, pl.ds(at, 256)],
                sinc_band(start_ref, taps_ref, block),
                preferred_element_type=F32,
            )
        return carry

    lax.fori_loop(0, (BLOCKS - 2) // 2, window, 0)
    reference_spectra(table_ref, spec_ref, rcols_ref, chips_ref, half_ref)


def own_side(place, sec, starts, taps, src, own, ref, table):
    return pl.pallas_call(
        own_kernel,
        out_shape=(
            jax.ShapeDtypeStruct((2 * LINES, COLS), F32),
            jax.ShapeDtypeStruct((OWNERS * 8, 4 * LINES), BF),
            jax.ShapeDtypeStruct((PAIRS * CHIP_LEN, 256), F32),
        ),
        in_specs=[smem] + [hbm] * 3 + [vmem] * 2 + [hbm] * 2,
        out_specs=(vmem,) * 3,
        scratch_shapes=[
            pltpu.VMEM((2 * LINES, COLS), BF),
            pltpu.VMEM((BLOCKS, 128), jnp.int32),
            pltpu.VMEM((TAP_COUNT, COLS), BF),
            pltpu.VMEM((2 * LINES, COLS), BF),
            pltpu.VMEM(TABLE, BF),
            pltpu.VMEM((2 * CHIP_LEN, SCRATCH_BLOCKS * 128), BF),
            pltpu.VMEM((2 * CHIP_LEN, CHIPS * 64), BF),
            pltpu.VMEM((2 * CHIP_LEN, CHIPS * 64), BF),
            pltpu.SemaphoreType.DMA((6,)),
        ],
        compiler_params=pltpu.CompilerParams(vmem_limit_bytes=OWN_VMEM),
        cost_estimate=pl.CostEstimate(
            flops=2 * 10**9, bytes_accessed=6 * 10**6, transcendentals=0
        ),
        name="own_side",
    )(place, sec, starts, taps, src, own, ref, table)


def rims_kernel(place_ref, sec_hbm, mate_ref, other_ref, sems):
    odd = place_ref[0] & 1
    pairs = []
    for to_ref, at in ((other_ref, odd), (mate_ref, 1 - odd)):
        first = at * (LINES - MARGIN)
        for part in range(2):
            for row in range(0, MARGIN, 32):
                pairs.append(
                    (
                        sec_hbm.at[part, pl.ds(pl.multiple_of(first + row, 16), 32), :],
                        to_ref.at[part, row : row + 32, :],
                    )
                )
    for copy in begin(sems, *pairs):
        copy.wait()


def rims(place, sec):
    rows = jax.ShapeDtypeStruct((2, MARGIN, COLS), BF)
    return pl.pallas_call(
        rims_kernel,
        out_shape=(rows, rows),
        in_specs=[smem, hbm],
        out_specs=(hbm, hbm),
        scratch_shapes=[pltpu.SemaphoreType.DMA((8,))],
        compiler_params=pltpu.CompilerParams(vmem_limit_bytes=RIM_VMEM),
        name="rims",
    )(place, sec)


def edges_kernel(place_ref, ref_hbm, sec_hbm, near_ref, far_ref, mate_ref, other_ref, sems):
    odd_rows = place_ref[0] & 1
    odd = place_ref[1] & 1
    own = CHIP_LEN + MARGIN
    pairs = []
    sides = []
    for to_ref, at in ((mate_ref, 1 - odd), (other_ref, odd)):
        cols = pl.ds(pl.multiple_of(at * (COLS - 128), 128), 128)
        sides.append((to_ref, cols))
        pairs += [
            (
                ref_hbm.at[:, FIRST_ROW : FIRST_ROW + CHIP_LEN, cols],
                to_ref.at[:, 0:CHIP_LEN, :],
            ),
            (sec_hbm.at[:, :, cols], to_ref.at[:, own : own + LINES, :]),
        ]
    fetch = begin(sems, *pairs)
    for to_ref, cols in sides:
        for rows_ref, low in ((near_ref, 1 - odd_rows), (far_ref, odd_rows)):
            at = pl.ds(pl.multiple_of(CHIP_LEN + low * (MARGIN + LINES), 16), MARGIN)
            for part in range(2):
                to_ref[part, at, :] = rows_ref[part, :, cols]
    for copy in fetch:
        copy.wait()


def rg_edges(place, ref, sec, near, far):
    cols = jax.ShapeDtypeStruct((2, CHIP_LEN + ROWS, 128), BF)
    return pl.pallas_call(
        edges_kernel,
        out_shape=(cols, cols),
        in_specs=[smem, hbm, hbm, vmem, vmem],
        out_specs=(vmem, vmem),
        scratch_shapes=[pltpu.SemaphoreType.DMA((4,))],
        compiler_params=pltpu.CompilerParams(vmem_limit_bytes=8 * 2**20),
        name="rg_edges",
    )(place, ref, sec, near, far)


def side_by_side(half, pairs):
    rows = []
    for pair in pairs:
        if isinstance(pair, int):
            at = slice(pair * 128, (pair + 1) * 128)
        else:
            at = pl.ds(pl.multiple_of(pair * 128, 128), 128)
        rows.append(
            jnp.concatenate([half[0:CHIP_LEN, at], half[CHIP_LEN : 2 * CHIP_LEN, at]], axis=1)
        )
    return jnp.concatenate(rows, axis=0)


def first_pass(table_ref, chips_ref, half_ref):
    fwd = table_ref[864:992, 0:128]
    for first in range(0, CHIPS * 64, 1024):
        half_ref[:, first : first + 1024] = jnp.dot(
            fwd, chips_ref[:, first : first + 1024], preferred_element_type=F32
        ).astype(BF)


def even_pair(near, here):
    lane = iota(near.shape, 1)
    return pltpu.roll(jnp.where(lane >= 112, near, here), 16, 1).astype(BF)


def odd_pair(here, far):
    lane = iota(far.shape, 1)
    return pltpu.roll(jnp.where(lane >= 48, here, far), 80, 1).astype(BF)


def reference_spectra(table_ref, spec_ref, rcols_ref, chips_ref, half_ref):
    none = jnp.zeros((2 * CHIP_LEN, 128), BF)
    rcols_ref[:, 0:128] = none
    rcols_ref[:, 128 + COLS : 256 + COLS] = none

    def cut(step, carry):
        def block(at):
            return rcols_ref[:, pl.ds(pl.multiple_of(at * 128, 128), 128)].astype(F32)

        near, here, far = block(step), block(step + 1), block(step + 2)
        to = pl.multiple_of(step * 256, 256)
        chips_ref[:, pl.ds(to, 128)] = even_pair(near, here)
        chips_ref[:, pl.ds(pl.multiple_of(to + 128, 128), 128)] = odd_pair(here, far)
        return carry

    lax.fori_loop(0, PAIRS // 2, cut, 0)
    first_pass(table_ref, chips_ref, half_ref)

    for step in range(PAIRS // GROUP):
        at = step * GROUP * CHIP_LEN
        spec_ref[at : at + GROUP * CHIP_LEN, :] = jnp.dot(
            side_by_side(half_ref, range(step * GROUP, (step + 1) * GROUP)),
            table_ref[0:256, :],
            preferred_element_type=F32,
        )


def cut_pair(off_ref, scols_ref, pair, first_block):
    lane = iota((CHIP_LEN, 128), 1)
    parts = []
    for part in range(2):
        found = []
        for side in range(2):
            chip = pair * 2 + side
            row = off_ref[0, chip] + (FIRST_ROW + MARGIN + part * ROWS)
            col = chip * SPACING + off_ref[1, chip] + 112
            block = (col >> 7) - first_block
            turn = col & 127
            near = scols_ref[block, pl.ds(row, CHIP_LEN), :]
            far = scols_ref[block + 1, pl.ds(row, CHIP_LEN), :]
            found.append(
                pltpu.roll(jnp.where(lane >= turn, near, far), (128 + side * 64 - turn) & 127, 1)
            )
        parts.append(jnp.where(lane < 64, found[0], found[1]).astype(BF))
    return parts


def correlated(spec_ref, spec_sec, table_ref, count):
    rr, ri = spec_ref[:, :128], spec_ref[:, 128:]
    sr, si = spec_sec[:, :128], spec_sec[:, 128:]
    cross = jnp.concatenate([rr * sr + ri * si, ri * sr - rr * si], axis=1).astype(BF)
    middle = jnp.dot(cross, table_ref[512:768, :], preferred_element_type=F32).astype(BF)
    columns = []
    for m in range(count):
        rows = middle[m * CHIP_LEN : (m + 1) * CHIP_LEN]
        columns.append(jnp.concatenate([rows[:, :128], rows[:, 128:]], axis=0))
    corr = jnp.dot(
        table_ref[768:864, 0:128], jnp.concatenate(columns, axis=1), preferred_element_type=F32
    )
    lag_row = (iota((LAG_COUNT, 128), 0) - LAG_COUNT // 2).astype(F32) / OVERSAMPLE
    sums = []
    for m in range(count):
        re = corr[:LAG_COUNT, m * 128 : (m + 1) * 128]
        im = corr[LAG_COUNT:, m * 128 : (m + 1) * 128]
        energy = re * re + im * im
        weight = energy * energy
        sums.append(
            (
                jnp.sum(weight, axis=0, keepdims=True),
                jnp.sum(weight * lag_row, axis=0, keepdims=True),
            )
        )
    return sums


def inner_kernel(
    place_ref,
    off_ref,
    sec_hbm,
    near_ref,
    far_ref,
    table_hbm,
    spec_ref,
    tot_ref,
    mom_ref,
    sec_ref,
    table_ref,
    scols_ref,
    chips_ref,
    half_ref,
    sems,
):
    fetch = begin(sems, (sec_hbm, sec_ref), (table_hbm, table_ref))
    odd = place_ref[0] & 1
    none = jnp.zeros((2 * ROWS, 128), F32)
    for block in (0, SCRATCH_BLOCKS - 2, SCRATCH_BLOCKS - 1):
        scols_ref[block] = none

    def widen_rims(step, carry):
        for member in range(2):
            block = step * 2 + member
            at = pl.ds(pl.multiple_of(block * 128, 128), 128)
            for part in range(2):
                for rows_ref, low in ((near_ref, 1 - odd), (far_ref, odd)):
                    first = pl.multiple_of(part * ROWS + low * (MARGIN + LINES), 8)
                    scols_ref[block + 1, pl.ds(first, MARGIN), :] = rows_ref[part, :, at].astype(
                        F32
                    )
        return carry

    lax.fori_loop(0, BLOCKS // 2, widen_rims, 0)
    for copy in fetch:
        copy.wait()

    def widen(step, carry):
        for member in range(2):
            block = step * 2 + member
            at = pl.ds(pl.multiple_of(block * 128, 128), 128)
            for part in range(2):
                own = part * ROWS + MARGIN
                scols_ref[block + 1, own : own + LINES, :] = sec_ref[part, :, at].astype(F32)
        return carry

    lax.fori_loop(0, BLOCKS // 2, widen, 0)

    def cut(step, carry):
        for member in range(2):
            pair = step * 2 + member
            to = pl.ds(pl.multiple_of(pair * 128, 128), 128)
            re, im = cut_pair(off_ref, scols_ref, pair, 0)
            chips_ref[0:CHIP_LEN, to] = re
            chips_ref[CHIP_LEN : 2 * CHIP_LEN, to] = im
        return carry

    lax.fori_loop(0, PAIRS // 2, cut, 0)
    first_pass(table_ref, chips_ref, half_ref)

    def correlate(step, carry):
        size = GROUP * CHIP_LEN
        spec_sec = jnp.dot(
            side_by_side(half_ref, [step * GROUP + m for m in range(GROUP)]),
            table_ref[256:512, :],
            preferred_element_type=F32,
        )
        spec = spec_ref[pl.ds(pl.multiple_of(step * size, size), size), :]
        for m, (total, moment) in enumerate(correlated(spec, spec_sec, table_ref, GROUP)):
            row = pl.ds(step * GROUP + m, 1)
            tot_ref[row, :] = total
            mom_ref[row, :] = moment
        return carry

    lax.fori_loop(0, PAIRS // GROUP, correlate, 0)


def inner_pairs(place, off, sec, near, far, table, spectra):
    sums = jax.ShapeDtypeStruct((PAIRS, 128), F32)
    return pl.pallas_call(
        inner_kernel,
        out_shape=(sums, sums),
        in_specs=[smem, smem, hbm, vmem, vmem, hbm, vmem],
        out_specs=(vmem, vmem),
        scratch_shapes=[
            pltpu.VMEM((2, LINES, COLS), BF),
            pltpu.VMEM(TABLE, BF),
            pltpu.VMEM((SCRATCH_BLOCKS, 2 * ROWS, 128), F32),
            pltpu.VMEM((2 * CHIP_LEN, CHIPS * 64), BF),
            pltpu.VMEM((2 * CHIP_LEN, CHIPS * 64), BF),
            pltpu.SemaphoreType.DMA((2,)),
        ],
        compiler_params=pltpu.CompilerParams(vmem_limit_bytes=24 * 2**20),
        cost_estimate=pl.CostEstimate(
            flops=6 * 10**9, bytes_accessed=20 * 10**6, transcendentals=0
        ),
        name="inner_pairs",
    )(place, off, sec, near, far, table, spectra)


def finish_kernel(
    place_ref,
    off_ref,
    offv_ref,
    sent_mate_ref,
    sent_other_ref,
    got_mate_ref,
    got_other_ref,
    sec_hbm,
    start_hbm,
    taps_hbm,
    table_hbm,
    tot_ref,
    mom_ref,
    sum_hbm,
    pick_hbm,
    est_ref,
    out_ref,
    sum_ref,
    pick_ref,
    near_ref,
    start_ref,
    taps_ref,
    table_ref,
    edge_ref,
    padded_ref,
    scols_ref,
    lines_ref,
    packed_ref,
    table_sem,
    sems,
    out_sems,
):
    rg = place_ref[1]
    fetch_table = begin(table_sem, (table_hbm, table_ref))
    fetch = begin(
        sems,
        *band_copies(rg, start_hbm, taps_hbm, start_ref, taps_ref),
        (sec_hbm.at[:, :, 128:256], near_ref.at[0]),
        (sec_hbm.at[:, :, COLS - 256 : COLS - 128], near_ref.at[1]),
        (sum_hbm, sum_ref),
        (pick_hbm, pick_ref),
    )
    left_ref, first_ref, last_ref, right_ref = (edge_ref.at[n] for n in range(4))

    def ordered(refs):
        for to_ref, from_ref in zip((left_ref, first_ref, last_ref, right_ref), refs):
            to_ref[...] = from_ref[...]

    @pl.when((rg & 1) == 0)
    def _():
        ordered((got_other_ref, sent_other_ref, sent_mate_ref, got_mate_ref))

    @pl.when((rg & 1) == 1)
    def _():
        ordered((got_mate_ref, sent_mate_ref, sent_other_ref, got_other_ref))

    own_rows = slice(CHIP_LEN + MARGIN, CHIP_LEN + MARGIN + LINES)
    sides = (
        (left_ref, first_ref, 0),
        (last_ref, right_ref, 3),
    )
    for near_side, far_side, at in sides:
        for part in range(2):
            base = part * ROWS
            scols_ref[at, base : base + ROWS, :] = near_side[part, CHIP_LEN:, :].astype(F32)
            scols_ref[at + 1, base : base + ROWS, :] = far_side[part, CHIP_LEN:, :].astype(F32)
        scols_ref[at + 2] = jnp.zeros((2 * ROWS, 128), F32)

    def both_parts(ref, rows):
        return jnp.concatenate([ref[0, rows, :], ref[1, rows, :]], axis=0)

    chip_rows = slice(0, CHIP_LEN)
    columns = [
        even_pair(
            both_parts(left_ref, chip_rows).astype(F32),
            both_parts(first_ref, chip_rows).astype(F32),
        ),
        odd_pair(
            both_parts(last_ref, chip_rows).astype(F32),
            both_parts(right_ref, chip_rows).astype(F32),
        ),
        jnp.concatenate(cut_pair(off_ref, scols_ref, 0, 0), axis=0),
        jnp.concatenate(cut_pair(off_ref, scols_ref, PAIRS - 1, BLOCKS - 3), axis=0),
    ]
    for copy in fetch_table:
        copy.wait()
    half = jnp.dot(
        table_ref[864:992, 0:128],
        jnp.concatenate(columns, axis=1),
        preferred_element_type=F32,
    ).astype(BF)
    spec = jnp.dot(
        side_by_side(half, (0, 1)), table_ref[0:256, :], preferred_element_type=F32
    )
    spec_sec = jnp.dot(
        side_by_side(half, (2, 3)), table_ref[256:512, :], preferred_element_type=F32
    )
    outer = correlated(spec, spec_sec, table_ref, 2)

    wide = (PAIRS, 128)
    lanes = iota(wide, 1)
    pairs = iota(wide, 0)

    def completed(ref, which):
        return jnp.where(
            pairs == 0,
            outer[0][which],
            jnp.where(pairs == PAIRS - 1, outer[1][which], ref[...]),
        )

    total = completed(tot_ref, 0)
    moment = completed(mom_ref, 1)
    lag_lane = ((lanes & 63) - LAG_COUNT // 2).astype(F32) / OVERSAMPLE
    found = []
    for side in range(2):
        mask = (lanes < 64) if side == 0 else (lanes >= 64)

        def over(values):
            return jnp.sum(jnp.where(mask, values, 0.0), axis=1, keepdims=True)

        whole = over(total) + EPS
        found.append((over(moment) / whole, over(total * lag_lane) / whole))
    own_chip = (lanes >> 1) == pairs
    even = (lanes & 1) == 0

    def spread(which):
        values = jnp.where(even, found[0][which], found[1][which])
        return jnp.sum(jnp.where(own_chip, values, 0.0), axis=0, keepdims=True)

    padded_ref[...] = jnp.zeros((8, 128), jnp.int32)
    padded_ref[0:2, 0:CHIPS] = offv_ref[...]
    offsets = padded_ref[...].astype(F32)
    est_az = offsets[0:1, :] + spread(0)
    est_rg = offsets[1:2, :] + spread(1)
    est_ref[0:1, :] = est_az
    est_ref[1:2, :] = est_rg
    angle = PHASE_RATE * est_az
    cos_all = jnp.broadcast_to(jnp.cos(angle), (8, 128))
    sin_all = jnp.broadcast_to(jnp.sin(angle), (8, 128))

    for copy in fetch:
        copy.wait()
    start_ref[...] = start_ref[...] - rg * COLS
    every = slice(0, LINES)
    edge_columns = {
        0: (
            both_parts(left_ref, own_rows),
            both_parts(first_ref, own_rows),
            both_parts(near_ref.at[0], every),
        ),
        BLOCKS - 1: (
            both_parts(near_ref.at[1], every),
            both_parts(last_ref, own_rows),
            both_parts(right_ref, own_rows),
        ),
    }

    def turned(block):
        if block in edge_columns:
            cols = edge_columns[block]
            near = jnp.concatenate(
                [half_turned(cols[0], cols[1]), half_turned(cols[1], cols[2])], axis=1
            )
            summed = jnp.dot(
                near, sinc_band(start_ref, taps_ref, block), preferred_element_type=F32
            )
        else:
            summed = sum_ref[:, block * 128 : (block + 1) * 128]
        chip = block * 4 + (iota((8, 128), 1) >> 5)
        cosine = jnp.take_along_axis(cos_all, chip, axis=1)[0:1, :]
        sine = jnp.take_along_axis(sin_all, chip, axis=1)[0:1, :]
        re, im = summed[:LINES], summed[LINES:]
        half = block // HALF
        at = slice((block - half * HALF) * 128, (block - half * HALF + 1) * 128)
        base = half * 2 * LINES
        lines_ref[base : base + LINES, at] = (re * cosine + im * sine).astype(BF)
        lines_ref[base + LINES : base + 2 * LINES, at] = (im * cosine - re * sine).astype(BF)

    copies = []
    for first in range(0, WIDTH, 256):
        at = slice(first, first + 256)
        for block in (first // 128, first // 128 + 1):
            turned(block)
            turned(block + HALF)
        packed_ref[:, at] = jnp.dot(
            pick_ref[...], lines_ref[:, at], preferred_element_type=F32
        ).astype(BF)
        copy = pltpu.make_async_copy(
            packed_ref.at[:, at], out_ref.at[:, at], out_sems.at[first // 256]
        )
        copy.start()
        copies.append(copy)
    for copy in copies:
        copy.wait()


def finish(place, off, *arrays):
    return pl.pallas_call(
        finish_kernel,
        out_shape=(
            jax.ShapeDtypeStruct((2, 128), F32),
            jax.ShapeDtypeStruct((OWNERS * 8, WIDTH), BF),
        ),
        in_specs=[smem] * 2 + [vmem] * 5 + [hbm] * 4 + [vmem] * 2 + [hbm] * 2,
        out_specs=(vmem, hbm),
        scratch_shapes=[
            pltpu.VMEM((2 * LINES, COLS), F32),
            pltpu.VMEM((OWNERS * 8, 4 * LINES), BF),
            pltpu.VMEM((2, 2, LINES, 128), BF),
            pltpu.VMEM((BLOCKS, 128), jnp.int32),
            pltpu.VMEM((TAP_COUNT, COLS), BF),
            pltpu.VMEM(TABLE, BF),
            pltpu.VMEM((4, 2, CHIP_LEN + ROWS, 128), BF),
            pltpu.VMEM((8, 128), jnp.int32),
            pltpu.VMEM((6, 2 * ROWS, 128), F32),
            pltpu.VMEM((4 * LINES, WIDTH), BF),
            pltpu.VMEM((OWNERS * 8, WIDTH), BF),
            pltpu.SemaphoreType.DMA((1,)),
            pltpu.SemaphoreType.DMA((6,)),
            pltpu.SemaphoreType.DMA((WIDTH // 256,)),
        ],
        compiler_params=pltpu.CompilerParams(vmem_limit_bytes=52 * 2**20),
        cost_estimate=pl.CostEstimate(
            flops=2 * 10**9, bytes_accessed=10 * 10**6, transcendentals=0
        ),
        name="finish",
    )(place, off, off, *arrays)


def place_kernel(pick_ref, arr_ref, out_ref):
    pick = pick_ref[...]
    for first in range(0, WIDTH, 256):
        lines = jnp.dot(
            pick,
            arr_ref[:, 0, :, first : first + 256].reshape(128, 256),
            preferred_element_type=F32,
        ).astype(BF)
        for half in range(2):
            at = slice(half * WIDTH + first, half * WIDTH + first + 256)
            for part in range(2):
                base = half * 64 + part * OWNER_CAP
                out_ref[part, :, at] = lines[base : base + OWNER_CAP, :]


def place_lines(pick, arrived):
    return pl.pallas_call(
        place_kernel,
        grid=(PIECES,),
        out_shape=jax.ShapeDtypeStruct((2, OWNER_CAP, COLS * PIECES), BF),
        in_specs=[
            pl.BlockSpec((128, 128), lambda r: (0, 0)),
            pl.BlockSpec((TILES, 1, 8, WIDTH), lambda r: (0, r, 0, 0)),
        ],
        out_specs=pl.BlockSpec((2, OWNER_CAP, COLS), lambda r: (0, 0, r)),
        compiler_params=pltpu.CompilerParams(vmem_limit_bytes=20 * 2**20),
        cost_estimate=pl.CostEstimate(
            flops=10**9, bytes_accessed=8 * 10**6, transcendentals=0
        ),
        name="place_lines",
    )(pick, arrived)


def owner_table(src_row, line_owner, me):
    tile = src_row // LINES
    owned = line_owner == me
    ids = jnp.arange(ALL_LINES, dtype=jnp.int32)
    before = owned[None, :] & (ids[None, :] < ids[:, None])
    rank = jnp.sum(before.astype(jnp.int32), axis=1)
    rank_tile = jnp.sum((before & (tile[None, :] == tile[:, None])).astype(jnp.int32), axis=1)
    outs = jnp.arange(OWNER_CAP, dtype=jnp.int32)
    hit = owned[None, :] & (rank[None, :] == outs[:, None])
    code = jnp.sum(jnp.where(hit, (tile * 2 + rank_tile + 1)[None, :], 0), axis=1) - 1
    rows = jnp.arange(128, dtype=jnp.int32)[:, None]
    cols = jnp.arange(128, dtype=jnp.int32)[None, :]
    slot = jnp.tile(code, 4)[:, None]
    pick = (
        (slot == (cols >> 3) * 2 + ((cols >> 1) & 1))
        & ((rows >> 6) == ((cols >> 2) & 1))
        & (((rows >> 5) & 1) == (cols & 1))
    )
    return pick.astype(BF)


def exchanged(axis, mate, other):
    count = lax.axis_size(axis)

    def swap(block, first):
        pairs = [(i, i + 1) for i in range(first, count - 1, 2)]
        return lax.ppermute(block, axis, pairs + [(j, i) for i, j in pairs])

    return swap(mate, 0), swap(other, 1)


def per_device(
    reference_slc, secondary_slc, chip_offsets, src_row, line_owner, band_start, band_taps
):
    az = lax.axis_index("az")
    rg = lax.axis_index("rg")
    place = jnp.stack([az, rg]).astype(jnp.int32)
    starts = band_start.reshape(PIECES * BLOCKS, 128)
    table = kernel_table()
    near, far = exchanged("az", *rims(place, secondary_slc))
    summed, pick_sent, spectra = own_side(
        place,
        secondary_slc.reshape(2 * LINES, COLS),
        starts,
        band_taps,
        src_row.reshape(ALL_LINES // 128, 128),
        line_owner.reshape(ALL_LINES // 128, 128),
        reference_slc,
        table,
    )
    sent = rg_edges(place, reference_slc, secondary_slc, near, far)
    got = exchanged("rg", *sent)
    off = chip_offsets[:, 0, :]
    total, moment = inner_pairs(place, off, secondary_slc, near, far, table, spectra)
    est, packed = finish(
        place,
        off,
        *sent,
        *got,
        secondary_slc,
        starts,
        band_taps,
        table,
        total,
        moment,
        summed,
        pick_sent,
    )
    arrived = lax.all_to_all(packed, BOTH, 0, 0, tiled=True)
    pick = owner_table(src_row, line_owner, az * PIECES + rg)
    resampled = place_lines(pick, arrived.reshape(TILES, PIECES, 8, WIDTH))
    return est[:, None, :CHIPS], resampled


def solution(mesh):
    return jax.shard_map(
        per_device,
        mesh=mesh,
        in_specs=(
            P(None, "az", "rg"),
            P(None, "az", "rg"),
            P(None, "az", "rg"),
            P(),
            P(),
            P(),
            P(),
        ),
        out_specs=(P(None, "az", "rg"), P(None, BOTH, None)),
        check_vma=False,
    )
```

```python
import math

import jax
import jax.numpy as jnp
import ml_dtypes
import numpy as np
from jax import lax
from jax.experimental import pallas as pl
from jax.experimental.pallas import tpu as pltpu
from jax.sharding import PartitionSpec as P

CHIP_LEN = 64
OVERSAMPLE = 16
LAG_COUNT = 48
TAP_COUNT = 8
SPACING = 32
MARGIN = 64
PHASE_RATE = 2.0
EPS = 1e-06

TILES = 16
PIECES = 8
OWNERS = 128
LINES = 96
COLS = 3072
BLOCKS = COLS // 128
ALL_LINES = 1536
CHIPS = 96
PAIRS = CHIPS // 2
OWNER_CAP = 32
FIRST_ROW = 16
ROWS = LINES + 2 * MARGIN
HALF = BLOCKS // 2
WIDTH = HALF * 128
LINE_SPAN = 256
SCRATCH_BLOCKS = BLOCKS + 3
GROUP = 24
BAND_ROWS = 64
PLACED = 4
TABLE = (992, 256)
RIM_VMEM = 16 * 2**20
OWN_VMEM = 44 * 2**20
BOTH = ("az", "rg")
BF = jnp.bfloat16
F32 = jnp.float32


def numpy_tables():
    ids = np.arange(CHIP_LEN)
    angles = -2.0 * math.pi / CHIP_LEN * (ids[:, None] * ids[None, :] % CHIP_LEN)
    scale = 1.0 / math.sqrt(CHIP_LEN)

    def low(values):
        return values.astype(np.float32).astype(ml_dtypes.bfloat16).astype(np.float32)

    four = (low(np.cos(angles) * scale), low(np.sin(angles) * scale))
    steps = np.arange(LAG_COUNT) - LAG_COUNT // 2
    freq = np.where(ids < CHIP_LEN // 2, ids, ids - CHIP_LEN)
    turns = steps[:, None] * freq[None, :] % (OVERSAMPLE * CHIP_LEN)
    lifted = 2.0 * math.pi / (OVERSAMPLE * CHIP_LEN) * turns
    lift = (low(np.cos(lifted) * scale), low(np.sin(lifted) * scale))
    return four, lift


def kernel_table():
    four, lift = numpy_tables()

    def stacked(re, im):
        out = np.zeros((2 * re.shape[0], 256), np.float32)
        out[:, :128] = np.block([[re, -im], [im, re]])
        return out

    def paired(re, im, starts):
        out = np.zeros((2, 128, 2, 2, 64), np.float32)
        count = re.shape[0]
        for chip, first in enumerate(starts):
            rows = slice(first, first + CHIP_LEN)
            out[0, rows, 0, chip, :count] = re.T
            out[0, rows, 1, chip, :count] = im.T
            out[1, rows, 0, chip, :count] = -im.T
            out[1, rows, 1, chip, :count] = re.T
        return out.reshape(256, 256)

    whole = np.concatenate(
        [
            paired(*four, (0, 32)),
            paired(*four, (0, 64)),
            paired(*lift, (0, 64)),
            stacked(*lift),
            stacked(*four),
        ]
    )
    return jnp.asarray(whole.astype(ml_dtypes.bfloat16))


smem = pl.BlockSpec(memory_space=pltpu.SMEM)
vmem = pl.BlockSpec(memory_space=pltpu.VMEM)
hbm = pl.BlockSpec(memory_space=pltpu.HBM)


def iota(shape, dim):
    return lax.broadcasted_iota(jnp.int32, shape, dim)


def half_turned(left, right):
    lane = iota(left.shape, 1)
    return pltpu.roll(jnp.where(lane >= 64, left.astype(F32), right.astype(F32)), 64, 1).astype(BF)


def begin(sems, *pairs):
    started = [pltpu.make_async_copy(src, dst, sems.at[n]) for n, (src, dst) in enumerate(pairs)]
    for copy in started:
        copy.start()
    return started


def band_copies(rg, start_hbm, taps_hbm, start_ref, taps_ref):
    return (
        (start_hbm.at[pl.ds(pl.multiple_of(rg * BLOCKS, 8), BLOCKS), :], start_ref),
        (taps_hbm.at[:, pl.ds(pl.multiple_of(rg * COLS, 128), COLS)], taps_ref),
    )


def sinc_band(start_ref, taps_ref, block):
    start = start_ref[pl.ds(block, 1), :] - block * 128 + MARGIN
    taps = taps_ref[:, pl.ds(pl.multiple_of(block * 128, 128), 128)].astype(F32)
    chunks = []
    for first in range(0, 256, BAND_ROWS):
        offset = iota((BAND_ROWS, 128), 0) - (start - first)
        band = jnp.zeros((BAND_ROWS, 128), F32)
        for tap in range(TAP_COUNT):
            band = jnp.where(offset == tap, taps[tap : tap + 1, :], band)
        chunks.append(band.astype(BF))
    return jnp.concatenate(chunks, axis=0)


def own_kernel(
    sec_hbm,
    start_hbm,
    taps_hbm,
    src_ref,
    own_ref,
    ref_hbm,
    table_hbm,
    sum_ref,
    pick_ref,
    spec_ref,
    sec_ref,
    start_ref,
    taps_ref,
    shift_ref,
    table_ref,
    rcols_ref,
    chips_ref,
    half_ref,
    sems,
):
    az = lax.axis_index("az")
    rg = lax.axis_index("rg")
    rows = slice(FIRST_ROW, FIRST_ROW + CHIP_LEN)
    fetch = begin(
        sems,
        (sec_hbm, sec_ref),
        *band_copies(rg, start_hbm, taps_hbm, start_ref, taps_ref),
        (table_hbm, table_ref),
        *(
            (
                ref_hbm.at[part, rows, :],
                rcols_ref.at[part * CHIP_LEN : (part + 1) * CHIP_LEN, 128 : 128 + COLS],
            )
            for part in range(2)
        ),
    )

    line_block = jnp.minimum(jnp.maximum(az * LINES - 8, 0) // 128, ALL_LINES // 128 - 2)

    def spanned(ref):
        return jnp.concatenate(
            [ref[pl.ds(line_block, 1), :], ref[pl.ds(line_block + 1, 1), :]], axis=1
        )

    local = spanned(src_ref) - az * LINES
    owner = spanned(own_ref)
    here = (local >= 0) & (local < LINES)
    tagged = jnp.where(here, owner, -1).astype(F32)
    tagged_col = jnp.transpose(jnp.broadcast_to(tagged, (128, LINE_SPAN)))
    tagged_col = jnp.concatenate([tagged_col, tagged_col], axis=1)
    square = (LINE_SPAN, LINE_SPAN)
    earlier = iota(square, 0) < iota(square, 1)
    same = (tagged_col == tagged) & earlier
    rank = jnp.sum(jnp.where(same, 1.0, 0.0), axis=0, keepdims=True)
    slot = jnp.where(here, tagged * 2.0 + rank, -1.0)
    marked = jnp.where(here, local + 1, 0).astype(F32)
    marked_col = jnp.transpose(jnp.broadcast_to(marked, (128, LINE_SPAN))).astype(BF)
    for first in range(0, 1024, 256):
        ids = iota((256, LINE_SPAN), 0) + first
        wanted = ((ids >> 3) * 2 + ((ids >> 1) & 1)).astype(F32)
        hot = jnp.where(slot == wanted, 1.0, 0.0).astype(BF)
        found = jnp.dot(hot, marked_col, preferred_element_type=F32).astype(jnp.int32)
        ids = iota((256, 128), 0) + first
        base = ((ids >> 2) & 1) * (2 * LINES) + (ids & 1) * LINES - 1
        target = jnp.where(found > 0, found + base, -1)
        for block in range(3):
            lanes = iota((256, 128), 1) + block * 128
            pick_ref[first : first + 256, block * 128 : (block + 1) * 128] = jnp.where(
                lanes == target, 1.0, 0.0
            ).astype(BF)

    for copy in fetch:
        copy.wait()

    for at in range(128, COLS, 128):
        shift_ref[:, at : at + 128] = half_turned(
            sec_ref[:, at - 128 : at], sec_ref[:, at : at + 128]
        )
    start_ref[...] = start_ref[...] - rg * COLS

    def window(step, carry):
        for member in range(22):
            block = step * 22 + member + 1
            at = pl.multiple_of(block * 128, 128)
            sum_ref[:, pl.ds(at, 128)] = jnp.dot(
                shift_ref[:, pl.ds(at, 256)],
                sinc_band(start_ref, taps_ref, block),
                preferred_element_type=F32,
            )
        return carry

    lax.fori_loop(0, (BLOCKS - 2) // 22, window, 0)
    reference_spectra(table_ref, spec_ref, rcols_ref, chips_ref, half_ref)


def own_side(sec, starts, taps, src, own, ref, table):
    return pl.pallas_call(
        own_kernel,
        out_shape=(
            jax.ShapeDtypeStruct((2 * LINES, COLS), F32),
            jax.ShapeDtypeStruct((OWNERS * 8, 4 * LINES), BF),
            jax.ShapeDtypeStruct((PAIRS * CHIP_LEN, 256), F32),
        ),
        in_specs=[hbm] * 3 + [vmem] * 2 + [hbm] * 2,
        out_specs=(vmem,) * 3,
        scratch_shapes=[
            pltpu.VMEM((2 * LINES, COLS), BF),
            pltpu.VMEM((BLOCKS, 128), jnp.int32),
            pltpu.VMEM((TAP_COUNT, COLS), BF),
            pltpu.VMEM((2 * LINES, COLS), BF),
            pltpu.VMEM(TABLE, BF),
            pltpu.VMEM((2 * CHIP_LEN, SCRATCH_BLOCKS * 128), BF),
            pltpu.VMEM((2 * CHIP_LEN, CHIPS * 64), BF),
            pltpu.VMEM((2 * CHIP_LEN, CHIPS * 64), BF),
            pltpu.SemaphoreType.DMA((6,)),
        ],
        compiler_params=pltpu.CompilerParams(vmem_limit_bytes=OWN_VMEM),
        cost_estimate=pl.CostEstimate(
            flops=2 * 10**9, bytes_accessed=6 * 10**6, transcendentals=0
        ),
        name="own_side",
    )(sec, starts, taps, src, own, ref, table)


def rims_kernel(sec_hbm, mate_ref, other_ref, sems):
    odd = lax.axis_index("az") & 1
    pairs = []
    for to_ref, at in ((other_ref, odd), (mate_ref, 1 - odd)):
        first = at * (LINES - MARGIN)
        for part in range(2):
            for row in range(0, MARGIN, 32):
                pairs.append(
                    (
                        sec_hbm.at[part, pl.ds(pl.multiple_of(first + row, 16), 32), :],
                        to_ref.at[part, row : row + 32, :],
                    )
                )
    for copy in begin(sems, *pairs):
        copy.wait()


def rims(sec):
    rows = jax.ShapeDtypeStruct((2, MARGIN, COLS), BF)
    return pl.pallas_call(
        rims_kernel,
        out_shape=(rows, rows),
        in_specs=[hbm],
        out_specs=(hbm, hbm),
        scratch_shapes=[pltpu.SemaphoreType.DMA((8,))],
        compiler_params=pltpu.CompilerParams(vmem_limit_bytes=RIM_VMEM),
        cost_estimate=pl.CostEstimate(
            flops=4 * 10**9, bytes_accessed=4 * 10**6, transcendentals=0
        ),
        name="rims",
    )(sec)


def edges_kernel(ref_hbm, sec_hbm, near_ref, far_ref, mate_ref, other_ref, sems):
    odd_rows = lax.axis_index("az") & 1
    odd = lax.axis_index("rg") & 1
    own = CHIP_LEN + MARGIN
    pairs = []
    sides = []
    for to_ref, at in ((mate_ref, 1 - odd), (other_ref, odd)):
        cols = pl.ds(pl.multiple_of(at * (COLS - 128), 128), 128)
        sides.append((to_ref, cols))
        pairs += [
            (
                ref_hbm.at[:, FIRST_ROW : FIRST_ROW + CHIP_LEN, cols],
                to_ref.at[:, 0:CHIP_LEN, :],
            ),
            (sec_hbm.at[:, :, cols], to_ref.at[:, own : own + LINES, :]),
        ]
    fetch = begin(sems, *pairs)
    for to_ref, cols in sides:
        for rows_ref, low in ((near_ref, 1 - odd_rows), (far_ref, odd_rows)):
            at = pl.ds(pl.multiple_of(CHIP_LEN + low * (MARGIN + LINES), 16), MARGIN)
            for part in range(2):
                to_ref[part, at, :] = rows_ref[part, :, cols]
    for copy in fetch:
        copy.wait()


def rg_edges(ref, sec, near, far):
    cols = jax.ShapeDtypeStruct((2, CHIP_LEN + ROWS, 128), BF)
    return pl.pallas_call(
        edges_kernel,
        out_shape=(cols, cols),
        in_specs=[hbm, hbm, vmem, vmem],
        out_specs=(vmem, vmem),
        scratch_shapes=[pltpu.SemaphoreType.DMA((4,))],
        compiler_params=pltpu.CompilerParams(vmem_limit_bytes=8 * 2**20),
        cost_estimate=pl.CostEstimate(
            flops=4 * 10**9, bytes_accessed=4 * 10**6, transcendentals=0
        ),
        name="rg_edges",
    )(ref, sec, near, far)


def side_by_side(half, pairs):
    rows = []
    for pair in pairs:
        if isinstance(pair, int):
            at = slice(pair * 128, (pair + 1) * 128)
        else:
            at = pl.ds(pl.multiple_of(pair * 128, 128), 128)
        rows.append(
            jnp.concatenate([half[0:CHIP_LEN, at], half[CHIP_LEN : 2 * CHIP_LEN, at]], axis=1)
        )
    return jnp.concatenate(rows, axis=0)


def first_pass(table_ref, chips_ref, half_ref):
    fwd = table_ref[864:992, 0:128]
    for first in range(0, CHIPS * 64, 1024):
        half_ref[:, first : first + 1024] = jnp.dot(
            fwd, chips_ref[:, first : first + 1024], preferred_element_type=F32
        ).astype(BF)


def even_pair(near, here):
    lane = iota(near.shape, 1)
    return pltpu.roll(jnp.where(lane >= 112, near, here), 16, 1).astype(BF)


def odd_pair(here, far):
    lane = iota(far.shape, 1)
    return pltpu.roll(jnp.where(lane >= 48, here, far), 80, 1).astype(BF)


def reference_spectra(table_ref, spec_ref, rcols_ref, chips_ref, half_ref):
    none = jnp.zeros((2 * CHIP_LEN, 128), BF)
    rcols_ref[:, 0:128] = none
    rcols_ref[:, 128 + COLS : 256 + COLS] = none

    def cut(step, carry):
        def block(at):
            return rcols_ref[:, pl.ds(pl.multiple_of(at * 128, 128), 128)].astype(F32)

        for member in range(4):
            first = step * 4 + member
            near, here, far = block(first), block(first + 1), block(first + 2)
            to = pl.multiple_of(first * 256, 256)
            chips_ref[:, pl.ds(to, 128)] = even_pair(near, here)
            chips_ref[:, pl.ds(pl.multiple_of(to + 128, 128), 128)] = odd_pair(here, far)
        return carry

    lax.fori_loop(0, PAIRS // 8, cut, 0)
    first_pass(table_ref, chips_ref, half_ref)

    for step in range(PAIRS // GROUP):
        at = step * GROUP * CHIP_LEN
        spec_ref[at : at + GROUP * CHIP_LEN, :] = jnp.dot(
            side_by_side(half_ref, range(step * GROUP, (step + 1) * GROUP)),
            table_ref[0:256, :],
            preferred_element_type=F32,
        )


def cut_pair(off_ref, scols_ref, pair, first_block):
    lane = iota((CHIP_LEN, 128), 1)
    parts = []
    for part in range(2):
        found = []
        for side in range(2):
            chip = pair * 2 + side
            row = off_ref[0, chip] + (FIRST_ROW + MARGIN + part * ROWS)
            col = chip * SPACING + off_ref[1, chip] + 112
            block = (col >> 7) - first_block
            turn = col & 127
            near = scols_ref[block, pl.ds(row, CHIP_LEN), :]
            far = scols_ref[block + 1, pl.ds(row, CHIP_LEN), :]
            found.append(
                pltpu.roll(jnp.where(lane >= turn, near, far), (128 + side * 64 - turn) & 127, 1)
            )
        parts.append(jnp.where(lane < 64, found[0], found[1]).astype(BF))
    return parts


def correlated(spec_ref, spec_sec, table_ref, count):
    rr, ri = spec_ref[:, :128], spec_ref[:, 128:]
    sr, si = spec_sec[:, :128], spec_sec[:, 128:]
    cross = jnp.concatenate([rr * sr + ri * si, ri * sr - rr * si], axis=1).astype(BF)
    middle = jnp.dot(cross, table_ref[512:768, :], preferred_element_type=F32).astype(BF)
    columns = []
    for m in range(count):
        rows = middle[m * CHIP_LEN : (m + 1) * CHIP_LEN]
        columns.append(jnp.concatenate([rows[:, :128], rows[:, 128:]], axis=0))
    corr = jnp.dot(
        table_ref[768:864, 0:128], jnp.concatenate(columns, axis=1), preferred_element_type=F32
    )
    lag_row = (iota((LAG_COUNT, 128), 0) - LAG_COUNT // 2).astype(F32) / OVERSAMPLE
    sums = []
    for m in range(count):
        re = corr[:LAG_COUNT, m * 128 : (m + 1) * 128]
        im = corr[LAG_COUNT:, m * 128 : (m + 1) * 128]
        energy = re * re + im * im
        weight = energy * energy
        sums.append(
            (
                jnp.sum(weight, axis=0, keepdims=True),
                jnp.sum(weight * lag_row, axis=0, keepdims=True),
            )
        )
    return sums


def inner_kernel(
    off_ref,
    sec_hbm,
    near_ref,
    far_ref,
    table_hbm,
    spec_ref,
    tot_ref,
    mom_ref,
    sec_ref,
    table_ref,
    scols_ref,
    chips_ref,
    half_ref,
    sems,
):
    fetch = begin(sems, (sec_hbm, sec_ref), (table_hbm, table_ref))
    odd = lax.axis_index("az") & 1
    none = jnp.zeros((2 * ROWS, 128), F32)
    for block in (0, SCRATCH_BLOCKS - 2, SCRATCH_BLOCKS - 1):
        scols_ref[block] = none

    def widen_rims(step, carry):
        for member in range(4):
            block = step * 4 + member
            at = pl.ds(pl.multiple_of(block * 128, 128), 128)
            for part in range(2):
                for rows_ref, low in ((near_ref, 1 - odd), (far_ref, odd)):
                    first = pl.multiple_of(part * ROWS + low * (MARGIN + LINES), 8)
                    scols_ref[block + 1, pl.ds(first, MARGIN), :] = rows_ref[part, :, at].astype(
                        F32
                    )
        return carry

    lax.fori_loop(0, BLOCKS // 4, widen_rims, 0)
    for copy in fetch:
        copy.wait()

    def widen(step, carry):
        for member in range(4):
            block = step * 4 + member
            at = pl.ds(pl.multiple_of(block * 128, 128), 128)
            for part in range(2):
                own = part * ROWS + MARGIN
                scols_ref[block + 1, own : own + LINES, :] = sec_ref[part, :, at].astype(F32)
        return carry

    lax.fori_loop(0, BLOCKS // 4, widen, 0)

    def cut(step, carry):
        for member in range(8):
            pair = step * 8 + member
            to = pl.ds(pl.multiple_of(pair * 128, 128), 128)
            re, im = cut_pair(off_ref, scols_ref, pair, 0)
            chips_ref[0:CHIP_LEN, to] = re
            chips_ref[CHIP_LEN : 2 * CHIP_LEN, to] = im
        return carry

    lax.fori_loop(0, PAIRS // 8, cut, 0)
    first_pass(table_ref, chips_ref, half_ref)

    def correlate(step, carry):
        size = GROUP * CHIP_LEN
        spec_sec = jnp.dot(
            side_by_side(half_ref, [step * GROUP + m for m in range(GROUP)]),
            table_ref[256:512, :],
            preferred_element_type=F32,
        )
        spec = spec_ref[pl.ds(pl.multiple_of(step * size, size), size), :]
        for m, (total, moment) in enumerate(correlated(spec, spec_sec, table_ref, GROUP)):
            row = pl.ds(step * GROUP + m, 1)
            tot_ref[row, :] = total
            mom_ref[row, :] = moment
        return carry

    lax.fori_loop(0, PAIRS // GROUP, correlate, 0)


def inner_pairs(off, sec, near, far, table, spectra):
    sums = jax.ShapeDtypeStruct((PAIRS, 128), F32)
    return pl.pallas_call(
        inner_kernel,
        out_shape=(sums, sums),
        in_specs=[smem, hbm, vmem, vmem, hbm, vmem],
        out_specs=(vmem, vmem),
        scratch_shapes=[
            pltpu.VMEM((2, LINES, COLS), BF),
            pltpu.VMEM(TABLE, BF),
            pltpu.VMEM((SCRATCH_BLOCKS, 2 * ROWS, 128), F32),
            pltpu.VMEM((2 * CHIP_LEN, CHIPS * 64), BF),
            pltpu.VMEM((2 * CHIP_LEN, CHIPS * 64), BF),
            pltpu.SemaphoreType.DMA((2,)),
        ],
        compiler_params=pltpu.CompilerParams(vmem_limit_bytes=24 * 2**20),
        cost_estimate=pl.CostEstimate(
            flops=6 * 10**9, bytes_accessed=20 * 10**6, transcendentals=0
        ),
        name="inner_pairs",
    )(off, sec, near, far, table, spectra)


def finish_kernel(
    off_ref,
    offv_ref,
    sent_mate_ref,
    sent_other_ref,
    got_mate_ref,
    got_other_ref,
    sec_hbm,
    start_hbm,
    taps_hbm,
    table_hbm,
    tot_ref,
    mom_ref,
    sum_hbm,
    pick_hbm,
    est_ref,
    out_ref,
    sum_ref,
    pick_ref,
    near_ref,
    start_ref,
    taps_ref,
    table_ref,
    edge_ref,
    padded_ref,
    scols_ref,
    lines_ref,
    packed_ref,
    table_sem,
    sems,
    out_sems,
):
    rg = lax.axis_index("rg")
    fetch_table = begin(table_sem, (table_hbm, table_ref))
    fetch = begin(
        sems,
        *band_copies(rg, start_hbm, taps_hbm, start_ref, taps_ref),
        (sec_hbm.at[:, :, 128:256], near_ref.at[0]),
        (sec_hbm.at[:, :, COLS - 256 : COLS - 128], near_ref.at[1]),
        (sum_hbm, sum_ref),
        (pick_hbm, pick_ref),
    )
    left_ref, first_ref, last_ref, right_ref = (edge_ref.at[n] for n in range(4))

    def ordered(refs):
        for to_ref, from_ref in zip((left_ref, first_ref, last_ref, right_ref), refs):
            to_ref[...] = from_ref[...]

    @pl.when((rg & 1) == 0)
    def _():
        ordered((got_other_ref, sent_other_ref, sent_mate_ref, got_mate_ref))

    @pl.when((rg & 1) == 1)
    def _():
        ordered((got_mate_ref, sent_mate_ref, sent_other_ref, got_other_ref))

    own_rows = slice(CHIP_LEN + MARGIN, CHIP_LEN + MARGIN + LINES)
    sides = (
        (left_ref, first_ref, 0),
        (last_ref, right_ref, 3),
    )
    for near_side, far_side, at in sides:
        for part in range(2):
            base = part * ROWS
            scols_ref[at, base : base + ROWS, :] = near_side[part, CHIP_LEN:, :].astype(F32)
            scols_ref[at + 1, base : base + ROWS, :] = far_side[part, CHIP_LEN:, :].astype(F32)
        scols_ref[at + 2] = jnp.zeros((2 * ROWS, 128), F32)

    def both_parts(ref, rows):
        return jnp.concatenate([ref[0, rows, :], ref[1, rows, :]], axis=0)

    chip_rows = slice(0, CHIP_LEN)
    columns = [
        even_pair(
            both_parts(left_ref, chip_rows).astype(F32),
            both_parts(first_ref, chip_rows).astype(F32),
        ),
        odd_pair(
            both_parts(last_ref, chip_rows).astype(F32),
            both_parts(right_ref, chip_rows).astype(F32),
        ),
        jnp.concatenate(cut_pair(off_ref, scols_ref, 0, 0), axis=0),
        jnp.concatenate(cut_pair(off_ref, scols_ref, PAIRS - 1, BLOCKS - 3), axis=0),
    ]
    for copy in fetch_table:
        copy.wait()
    half = jnp.dot(
        table_ref[864:992, 0:128],
        jnp.concatenate(columns, axis=1),
        preferred_element_type=F32,
    ).astype(BF)
    spec = jnp.dot(
        side_by_side(half, (0, 1)), table_ref[0:256, :], preferred_element_type=F32
    )
    spec_sec = jnp.dot(
        side_by_side(half, (2, 3)), table_ref[256:512, :], preferred_element_type=F32
    )
    outer = correlated(spec, spec_sec, table_ref, 2)

    wide = (PAIRS, 128)
    lanes = iota(wide, 1)
    pairs = iota(wide, 0)

    def completed(ref, which):
        return jnp.where(
            pairs == 0,
            outer[0][which],
            jnp.where(pairs == PAIRS - 1, outer[1][which], ref[...]),
        )

    total = completed(tot_ref, 0)
    moment = completed(mom_ref, 1)
    lag_lane = ((lanes & 63) - LAG_COUNT // 2).astype(F32) / OVERSAMPLE
    found = []
    for side in range(2):
        mask = (lanes < 64) if side == 0 else (lanes >= 64)

        def over(values):
            return jnp.sum(jnp.where(mask, values, 0.0), axis=1, keepdims=True)

        whole = over(total) + EPS
        found.append((over(moment) / whole, over(total * lag_lane) / whole))
    own_chip = (lanes >> 1) == pairs
    even = (lanes & 1) == 0

    def spread(which):
        values = jnp.where(even, found[0][which], found[1][which])
        return jnp.sum(jnp.where(own_chip, values, 0.0), axis=0, keepdims=True)

    padded_ref[...] = jnp.zeros((8, 128), jnp.int32)
    padded_ref[0:2, 0:CHIPS] = offv_ref[...]
    offsets = padded_ref[...].astype(F32)
    est_az = offsets[0:1, :] + spread(0)
    est_rg = offsets[1:2, :] + spread(1)
    est_ref[0:1, :] = est_az
    est_ref[1:2, :] = est_rg
    angle = PHASE_RATE * est_az
    cos_all = jnp.broadcast_to(jnp.cos(angle), (8, 128))
    sin_all = jnp.broadcast_to(jnp.sin(angle), (8, 128))

    for copy in fetch:
        copy.wait()
    start_ref[...] = start_ref[...] - rg * COLS
    every = slice(0, LINES)
    edge_columns = {
        0: (
            both_parts(left_ref, own_rows),
            both_parts(first_ref, own_rows),
            both_parts(near_ref.at[0], every),
        ),
        BLOCKS - 1: (
            both_parts(near_ref.at[1], every),
            both_parts(last_ref, own_rows),
            both_parts(right_ref, own_rows),
        ),
    }

    def turned(block):
        if block in edge_columns:
            cols = edge_columns[block]
            near = jnp.concatenate(
                [half_turned(cols[0], cols[1]), half_turned(cols[1], cols[2])], axis=1
            )
            summed = jnp.dot(
                near, sinc_band(start_ref, taps_ref, block), preferred_element_type=F32
            )
        else:
            summed = sum_ref[:, block * 128 : (block + 1) * 128]
        chip = block * 4 + (iota((8, 128), 1) >> 5)
        cosine = jnp.take_along_axis(cos_all, chip, axis=1)[0:1, :]
        sine = jnp.take_along_axis(sin_all, chip, axis=1)[0:1, :]
        re, im = summed[:LINES], summed[LINES:]
        half = block // HALF
        at = slice((block - half * HALF) * 128, (block - half * HALF + 1) * 128)
        base = half * 2 * LINES
        lines_ref[base : base + LINES, at] = (re * cosine + im * sine).astype(BF)
        lines_ref[base + LINES : base + 2 * LINES, at] = (im * cosine - re * sine).astype(BF)

    copies = []
    for first in range(0, WIDTH, 256):
        at = slice(first, first + 256)
        for block in (first // 128, first // 128 + 1):
            turned(block)
            turned(block + HALF)
        packed_ref[:, at] = jnp.dot(
            pick_ref[...], lines_ref[:, at], preferred_element_type=F32
        ).astype(BF)
        copy = pltpu.make_async_copy(
            packed_ref.at[:, at], out_ref.at[:, at], out_sems.at[first // 256]
        )
        copy.start()
        copies.append(copy)
    for copy in copies:
        copy.wait()


def finish(off, *arrays):
    return pl.pallas_call(
        finish_kernel,
        out_shape=(
            jax.ShapeDtypeStruct((2, 128), F32),
            jax.ShapeDtypeStruct((OWNERS * 8, WIDTH), BF),
        ),
        in_specs=[smem] + [vmem] * 5 + [hbm] * 4 + [vmem] * 2 + [hbm] * 2,
        out_specs=(vmem, hbm),
        scratch_shapes=[
            pltpu.VMEM((2 * LINES, COLS), F32),
            pltpu.VMEM((OWNERS * 8, 4 * LINES), BF),
            pltpu.VMEM((2, 2, LINES, 128), BF),
            pltpu.VMEM((BLOCKS, 128), jnp.int32),
            pltpu.VMEM((TAP_COUNT, COLS), BF),
            pltpu.VMEM(TABLE, BF),
            pltpu.VMEM((4, 2, CHIP_LEN + ROWS, 128), BF),
            pltpu.VMEM((8, 128), jnp.int32),
            pltpu.VMEM((6, 2 * ROWS, 128), F32),
            pltpu.VMEM((4 * LINES, WIDTH), BF),
            pltpu.VMEM((OWNERS * 8, WIDTH), BF),
            pltpu.SemaphoreType.DMA((1,)),
            pltpu.SemaphoreType.DMA((6,)),
            pltpu.SemaphoreType.DMA((WIDTH // 256,)),
        ],
        compiler_params=pltpu.CompilerParams(vmem_limit_bytes=52 * 2**20),
        cost_estimate=pl.CostEstimate(
            flops=2 * 10**9, bytes_accessed=10 * 10**6, transcendentals=0
        ),
        name="finish",
    )(off, off, *arrays)


def place_kernel(pick_ref, arr_ref, out_ref):
    pick = pick_ref[...]
    for first in range(0, WIDTH, 256):
        for piece in range(PLACED):
            lines = jnp.dot(
                pick,
                arr_ref[:, piece, :, first : first + 256].reshape(128, 256),
                preferred_element_type=F32,
            ).astype(BF)
            for half in range(2):
                begin_at = piece * COLS + half * WIDTH + first
                at = slice(begin_at, begin_at + 256)
                for part in range(2):
                    base = half * 64 + part * OWNER_CAP
                    out_ref[part, :, at] = lines[base : base + OWNER_CAP, :]


def place_lines(pick, arrived):
    return pl.pallas_call(
        place_kernel,
        grid=(PIECES // PLACED,),
        out_shape=jax.ShapeDtypeStruct((2, OWNER_CAP, COLS * PIECES), BF),
        in_specs=[
            pl.BlockSpec((128, 128), lambda r: (0, 0)),
            pl.BlockSpec((TILES, PLACED, 8, WIDTH), lambda r: (0, r, 0, 0)),
        ],
        out_specs=pl.BlockSpec((2, OWNER_CAP, PLACED * COLS), lambda r: (0, 0, r)),
        compiler_params=pltpu.CompilerParams(vmem_limit_bytes=20 * 2**20),
        cost_estimate=pl.CostEstimate(
            flops=10**9, bytes_accessed=8 * 10**6, transcendentals=0
        ),
        name="place_lines",
    )(pick, arrived)


def owner_table(src_row, line_owner, me):
    tile = src_row // LINES
    owned = line_owner == me
    ids = jnp.arange(ALL_LINES, dtype=jnp.int32)
    before = owned[None, :] & (ids[None, :] < ids[:, None])
    rank = jnp.sum(before.astype(jnp.int32), axis=1)
    rank_tile = jnp.sum((before & (tile[None, :] == tile[:, None])).astype(jnp.int32), axis=1)
    outs = jnp.arange(OWNER_CAP, dtype=jnp.int32)
    hit = owned[None, :] & (rank[None, :] == outs[:, None])
    code = jnp.sum(jnp.where(hit, (tile * 2 + rank_tile + 1)[None, :], 0), axis=1) - 1
    rows = jnp.arange(128, dtype=jnp.int32)[:, None]
    cols = jnp.arange(128, dtype=jnp.int32)[None, :]
    slot = jnp.tile(code, 4)[:, None]
    pick = (
        (slot == (cols >> 3) * 2 + ((cols >> 1) & 1))
        & ((rows >> 6) == ((cols >> 2) & 1))
        & (((rows >> 5) & 1) == (cols & 1))
    )
    return pick.astype(BF)


def exchanged(axis, mate, other):
    count = lax.axis_size(axis)

    def swap(block, first):
        pairs = [(i, i + 1) for i in range(first, count - 1, 2)]
        return lax.ppermute(block, axis, pairs + [(j, i) for i, j in pairs])

    return swap(mate, 0), swap(other, 1)


def per_device(
    reference_slc, secondary_slc, chip_offsets, src_row, line_owner, band_start, band_taps
):
    az = lax.axis_index("az")
    rg = lax.axis_index("rg")
    starts = band_start.reshape(PIECES * BLOCKS, 128)
    table = kernel_table()
    near, far = exchanged("az", *rims(secondary_slc))
    summed, pick_sent, spectra = own_side(
        secondary_slc.reshape(2 * LINES, COLS),
        starts,
        band_taps,
        src_row.reshape(ALL_LINES // 128, 128),
        line_owner.reshape(ALL_LINES // 128, 128),
        reference_slc,
        table,
    )
    sent = rg_edges(reference_slc, secondary_slc, near, far)
    got = exchanged("rg", *sent)
    off = chip_offsets[:, 0, :]
    total, moment = inner_pairs(off, secondary_slc, near, far, table, spectra)
    est, packed = finish(
        off,
        *sent,
        *got,
        secondary_slc,
        starts,
        band_taps,
        table,
        total,
        moment,
        summed,
        pick_sent,
    )
    arrived = lax.all_to_all(packed, BOTH, 0, 0, tiled=True)
    pick = owner_table(src_row, line_owner, az * PIECES + rg)
    resampled = place_lines(pick, arrived.reshape(TILES, PIECES, 8, WIDTH))
    return est[:, None, :CHIPS], resampled


def solution(mesh):
    return jax.shard_map(
        per_device,
        mesh=mesh,
        in_specs=(
            P(None, "az", "rg"),
            P(None, "az", "rg"),
            P(None, "az", "rg"),
            P(),
            P(),
            P(),
            P(),
        ),
        out_specs=(P(None, "az", "rg"), P(None, BOTH, None)),
        check_vma=False,
    )
```

```python
import math

import jax
import jax.numpy as jnp
import ml_dtypes
import numpy as np
from jax import lax
from jax.experimental import pallas as pl
from jax.experimental.pallas import tpu as pltpu
from jax.sharding import PartitionSpec as P

CHIP_LEN = 64
OVERSAMPLE = 16
LAG_COUNT = 48
TAP_COUNT = 8
SPACING = 32
MARGIN = 64
PHASE_RATE = 2.0
EPS = 1e-06

TILES = 16
PIECES = 8
OWNERS = 128
LINES = 96
COLS = 3072
BLOCKS = COLS // 128
ALL_LINES = 1536
CHIPS = 96
PAIRS = CHIPS // 2
OWNER_CAP = 32
FIRST_ROW = 16
ROWS = LINES + 2 * MARGIN
HALF = BLOCKS // 2
WIDTH = HALF * 128
LINE_SPAN = 256
SCRATCH_BLOCKS = BLOCKS + 3
GROUP = 24
BAND_ROWS = 64
PLACED = 4
TABLE = (992, 256)
RIM_VMEM = 16 * 2**20
OWN_VMEM = 44 * 2**20
BOTH = ("az", "rg")
BF = jnp.bfloat16
F32 = jnp.float32


def numpy_tables():
    ids = np.arange(CHIP_LEN)
    angles = -2.0 * math.pi / CHIP_LEN * (ids[:, None] * ids[None, :] % CHIP_LEN)
    scale = 1.0 / math.sqrt(CHIP_LEN)

    def low(values):
        return values.astype(np.float32).astype(ml_dtypes.bfloat16).astype(np.float32)

    four = (low(np.cos(angles) * scale), low(np.sin(angles) * scale))
    steps = np.arange(LAG_COUNT) - LAG_COUNT // 2
    freq = np.where(ids < CHIP_LEN // 2, ids, ids - CHIP_LEN)
    turns = steps[:, None] * freq[None, :] % (OVERSAMPLE * CHIP_LEN)
    lifted = 2.0 * math.pi / (OVERSAMPLE * CHIP_LEN) * turns
    lift = (low(np.cos(lifted) * scale), low(np.sin(lifted) * scale))
    return four, lift


def kernel_table():
    four, lift = numpy_tables()

    def stacked(re, im):
        out = np.zeros((2 * re.shape[0], 256), np.float32)
        out[:, :128] = np.block([[re, -im], [im, re]])
        return out

    def paired(re, im, starts):
        out = np.zeros((2, 128, 2, 2, 64), np.float32)
        count = re.shape[0]
        for chip, first in enumerate(starts):
            rows = slice(first, first + CHIP_LEN)
            out[0, rows, 0, chip, :count] = re.T
            out[0, rows, 1, chip, :count] = im.T
            out[1, rows, 0, chip, :count] = -im.T
            out[1, rows, 1, chip, :count] = re.T
        return out.reshape(256, 256)

    whole = np.concatenate(
        [
            paired(*four, (0, 32)),
            paired(*four, (0, 64)),
            paired(*lift, (0, 64)),
            stacked(*lift),
            stacked(*four),
        ]
    )
    return jnp.asarray(whole.astype(ml_dtypes.bfloat16))


smem = pl.BlockSpec(memory_space=pltpu.SMEM)
vmem = pl.BlockSpec(memory_space=pltpu.VMEM)
hbm = pl.BlockSpec(memory_space=pltpu.HBM)


def iota(shape, dim):
    return lax.broadcasted_iota(jnp.int32, shape, dim)


def half_turned(left, right):
    lane = iota(left.shape, 1)
    return pltpu.roll(jnp.where(lane >= 64, left.astype(F32), right.astype(F32)), 64, 1).astype(BF)


def begin(sems, *pairs):
    started = [pltpu.make_async_copy(src, dst, sems.at[n]) for n, (src, dst) in enumerate(pairs)]
    for copy in started:
        copy.start()
    return started


def band_copies(rg, start_hbm, taps_hbm, start_ref, taps_ref):
    return (
        (start_hbm.at[pl.ds(pl.multiple_of(rg * BLOCKS, 8), BLOCKS), :], start_ref),
        (taps_hbm.at[:, pl.ds(pl.multiple_of(rg * COLS, 128), COLS)], taps_ref),
    )


def sinc_band(start_ref, taps_ref, block):
    start = start_ref[pl.ds(block, 1), :] - block * 128 + MARGIN
    taps = taps_ref[:, pl.ds(pl.multiple_of(block * 128, 128), 128)].astype(F32)
    chunks = []
    for first in range(0, 256, BAND_ROWS):
        offset = iota((BAND_ROWS, 128), 0) - (start - first)
        band = jnp.zeros((BAND_ROWS, 128), F32)
        for tap in range(TAP_COUNT):
            band = jnp.where(offset == tap, taps[tap : tap + 1, :], band)
        chunks.append(band.astype(BF))
    return jnp.concatenate(chunks, axis=0)


def own_kernel(
    sec_hbm,
    start_hbm,
    taps_hbm,
    src_ref,
    own_ref,
    ref_hbm,
    table_hbm,
    sum_ref,
    pick_ref,
    spec_ref,
    sec_ref,
    start_ref,
    taps_ref,
    shift_ref,
    table_ref,
    rcols_ref,
    chips_ref,
    half_ref,
    sems,
):
    az = lax.axis_index("az")
    rg = lax.axis_index("rg")
    rows = slice(FIRST_ROW, FIRST_ROW + CHIP_LEN)
    fetch = begin(
        sems,
        (sec_hbm, sec_ref),
        *band_copies(rg, start_hbm, taps_hbm, start_ref, taps_ref),
        (table_hbm, table_ref),
        *(
            (
                ref_hbm.at[part, rows, :],
                rcols_ref.at[part * CHIP_LEN : (part + 1) * CHIP_LEN, 128 : 128 + COLS],
            )
            for part in range(2)
        ),
    )

    line_block = jnp.minimum(jnp.maximum(az * LINES - 8, 0) // 128, ALL_LINES // 128 - 2)

    def spanned(ref):
        return jnp.concatenate(
            [ref[pl.ds(line_block, 1), :], ref[pl.ds(line_block + 1, 1), :]], axis=1
        )

    local = spanned(src_ref) - az * LINES
    owner = spanned(own_ref)
    here = (local >= 0) & (local < LINES)
    tagged = jnp.where(here, owner, -1).astype(F32)
    tagged_col = jnp.transpose(jnp.broadcast_to(tagged, (128, LINE_SPAN)))
    tagged_col = jnp.concatenate([tagged_col, tagged_col], axis=1)
    square = (LINE_SPAN, LINE_SPAN)
    earlier = iota(square, 0) < iota(square, 1)
    same = (tagged_col == tagged) & earlier
    rank = jnp.sum(jnp.where(same, 1.0, 0.0), axis=0, keepdims=True)
    slot = jnp.where(here, tagged * 2.0 + rank, -1.0)
    marked = jnp.where(here, local + 1, 0).astype(F32)
    marked_col = jnp.transpose(jnp.broadcast_to(marked, (128, LINE_SPAN))).astype(BF)
    for first in range(0, 1024, 256):
        ids = iota((256, LINE_SPAN), 0) + first
        wanted = ((ids >> 3) * 2 + ((ids >> 1) & 1)).astype(F32)
        hot = jnp.where(slot == wanted, 1.0, 0.0).astype(BF)
        found = jnp.dot(hot, marked_col, preferred_element_type=F32).astype(jnp.int32)
        ids = iota((256, 128), 0) + first
        base = ((ids >> 2) & 1) * (2 * LINES) + (ids & 1) * LINES - 1
        target = jnp.where(found > 0, found + base, -1)
        for block in range(3):
            lanes = iota((256, 128), 1) + block * 128
            pick_ref[first : first + 256, block * 128 : (block + 1) * 128] = jnp.where(
                lanes == target, 1.0, 0.0
            ).astype(BF)

    for copy in fetch:
        copy.wait()

    for at in range(128, COLS, 128):
        shift_ref[:, at : at + 128] = half_turned(
            sec_ref[:, at - 128 : at], sec_ref[:, at : at + 128]
        )
    start_ref[...] = start_ref[...] - rg * COLS

    def window(step, carry):
        for member in range(22):
            block = step * 22 + member + 1
            at = pl.multiple_of(block * 128, 128)
            sum_ref[:, pl.ds(at, 128)] = jnp.dot(
                shift_ref[:, pl.ds(at, 256)],
                sinc_band(start_ref, taps_ref, block),
                preferred_element_type=F32,
            )
        return carry

    lax.fori_loop(0, (BLOCKS - 2) // 22, window, 0)
    reference_spectra(table_ref, spec_ref, rcols_ref, chips_ref, half_ref)


def own_side(sec, starts, taps, src, own, ref, table):
    return pl.pallas_call(
        own_kernel,
        out_shape=(
            jax.ShapeDtypeStruct((2 * LINES, COLS), F32),
            jax.ShapeDtypeStruct((OWNERS * 8, 4 * LINES), BF),
            jax.ShapeDtypeStruct((PAIRS * CHIP_LEN, 256), F32),
        ),
        in_specs=[hbm] * 3 + [vmem] * 2 + [hbm] * 2,
        out_specs=(vmem,) * 3,
        scratch_shapes=[
            pltpu.VMEM((2 * LINES, COLS), BF),
            pltpu.VMEM((BLOCKS, 128), jnp.int32),
            pltpu.VMEM((TAP_COUNT, COLS), BF),
            pltpu.VMEM((2 * LINES, COLS), BF),
            pltpu.VMEM(TABLE, BF),
            pltpu.VMEM((2 * CHIP_LEN, SCRATCH_BLOCKS * 128), BF),
            pltpu.VMEM((2 * CHIP_LEN, CHIPS * 64), BF),
            pltpu.VMEM((2 * CHIP_LEN, CHIPS * 64), BF),
            pltpu.SemaphoreType.DMA((6,)),
        ],
        compiler_params=pltpu.CompilerParams(vmem_limit_bytes=OWN_VMEM),
        cost_estimate=pl.CostEstimate(
            flops=2 * 10**9, bytes_accessed=6 * 10**6, transcendentals=0
        ),
        name="own_side",
    )(sec, starts, taps, src, own, ref, table)


def rims_kernel(sec_hbm, mate_ref, other_ref, sems):
    odd = lax.axis_index("az") & 1
    pairs = []
    for to_ref, at in ((other_ref, odd), (mate_ref, 1 - odd)):
        first = at * (LINES - MARGIN)
        for part in range(2):
            for row in range(0, MARGIN, 32):
                pairs.append(
                    (
                        sec_hbm.at[part, pl.ds(pl.multiple_of(first + row, 16), 32), :],
                        to_ref.at[part, row : row + 32, :],
                    )
                )
    for copy in begin(sems, *pairs):
        copy.wait()


def rims(sec):
    rows = jax.ShapeDtypeStruct((2, MARGIN, COLS), BF)
    return pl.pallas_call(
        rims_kernel,
        out_shape=(rows, rows),
        in_specs=[hbm],
        out_specs=(hbm, hbm),
        scratch_shapes=[pltpu.SemaphoreType.DMA((8,))],
        compiler_params=pltpu.CompilerParams(vmem_limit_bytes=RIM_VMEM),
        cost_estimate=pl.CostEstimate(
            flops=4 * 10**9, bytes_accessed=4 * 10**6, transcendentals=0
        ),
        name="rims",
    )(sec)


def edges_kernel(ref_hbm, sec_hbm, far_ref, near_ref, mate_ref, other_ref, sems):
    odd_rows = lax.axis_index("az") & 1
    odd = lax.axis_index("rg") & 1
    own = CHIP_LEN + MARGIN
    pairs = []
    sides = []
    for to_ref, at in ((mate_ref, 1 - odd), (other_ref, odd)):
        cols = pl.ds(pl.multiple_of(at * (COLS - 128), 128), 128)
        sides.append((to_ref, cols))
        pairs += [
            (
                ref_hbm.at[:, FIRST_ROW : FIRST_ROW + CHIP_LEN, cols],
                to_ref.at[:, 0:CHIP_LEN, :],
            ),
            (sec_hbm.at[:, :, cols], to_ref.at[:, own : own + LINES, :]),
        ]
    fetch = begin(sems, *pairs)
    for to_ref, cols in sides:
        for rows_ref, low in ((near_ref, 1 - odd_rows), (far_ref, odd_rows)):
            at = pl.ds(pl.multiple_of(CHIP_LEN + low * (MARGIN + LINES), 16), MARGIN)
            for part in range(2):
                to_ref[part, at, :] = rows_ref[part, :, cols]
    for copy in fetch:
        copy.wait()


def rg_edges(ref, sec, near, far):
    cols = jax.ShapeDtypeStruct((2, CHIP_LEN + ROWS, 128), BF)
    return pl.pallas_call(
        edges_kernel,
        out_shape=(cols, cols),
        in_specs=[hbm, hbm, vmem, vmem],
        out_specs=(vmem, vmem),
        scratch_shapes=[pltpu.SemaphoreType.DMA((4,))],
        compiler_params=pltpu.CompilerParams(vmem_limit_bytes=8 * 2**20),
        cost_estimate=pl.CostEstimate(
            flops=4 * 10**9, bytes_accessed=4 * 10**6, transcendentals=0
        ),
        name="rg_edges",
    )(ref, sec, far, near)


def side_by_side(half, pairs):
    rows = []
    for pair in pairs:
        if isinstance(pair, int):
            at = slice(pair * 128, (pair + 1) * 128)
        else:
            at = pl.ds(pl.multiple_of(pair * 128, 128), 128)
        rows.append(
            jnp.concatenate([half[0:CHIP_LEN, at], half[CHIP_LEN : 2 * CHIP_LEN, at]], axis=1)
        )
    return jnp.concatenate(rows, axis=0)


def first_pass(table_ref, chips_ref, half_ref):
    fwd = table_ref[864:992, 0:128]
    for first in range(0, CHIPS * 64, 1024):
        half_ref[:, first : first + 1024] = jnp.dot(
            fwd, chips_ref[:, first : first + 1024], preferred_element_type=F32
        ).astype(BF)


def even_pair(near, here):
    lane = iota(near.shape, 1)
    return pltpu.roll(jnp.where(lane >= 112, near, here), 16, 1).astype(BF)


def odd_pair(here, far):
    lane = iota(far.shape, 1)
    return pltpu.roll(jnp.where(lane >= 48, here, far), 80, 1).astype(BF)


def reference_spectra(table_ref, spec_ref, rcols_ref, chips_ref, half_ref):
    none = jnp.zeros((2 * CHIP_LEN, 128), BF)
    rcols_ref[:, 0:128] = none
    rcols_ref[:, 128 + COLS : 256 + COLS] = none

    def cut(step, carry):
        def block(at):
            return rcols_ref[:, pl.ds(pl.multiple_of(at * 128, 128), 128)].astype(F32)

        for member in range(4):
            first = step * 4 + member
            near, here, far = block(first), block(first + 1), block(first + 2)
            to = pl.multiple_of(first * 256, 256)
            chips_ref[:, pl.ds(to, 128)] = even_pair(near, here)
            chips_ref[:, pl.ds(pl.multiple_of(to + 128, 128), 128)] = odd_pair(here, far)
        return carry

    lax.fori_loop(0, PAIRS // 8, cut, 0)
    first_pass(table_ref, chips_ref, half_ref)

    for step in range(PAIRS // GROUP):
        at = step * GROUP * CHIP_LEN
        spec_ref[at : at + GROUP * CHIP_LEN, :] = jnp.dot(
            side_by_side(half_ref, range(step * GROUP, (step + 1) * GROUP)),
            table_ref[0:256, :],
            preferred_element_type=F32,
        )


def cut_pair(off_ref, scols_ref, pair, first_block):
    lane = iota((CHIP_LEN, 128), 1)
    parts = []
    for part in range(2):
        found = []
        for side in range(2):
            chip = pair * 2 + side
            row = off_ref[0, chip] + (FIRST_ROW + MARGIN + part * ROWS)
            col = chip * SPACING + off_ref[1, chip] + 112
            block = (col >> 7) - first_block
            turn = col & 127
            near = scols_ref[block, pl.ds(row, CHIP_LEN), :]
            far = scols_ref[block + 1, pl.ds(row, CHIP_LEN), :]
            found.append(
                pltpu.roll(jnp.where(lane >= turn, near, far), (128 + side * 64 - turn) & 127, 1)
            )
        parts.append(jnp.where(lane < 64, found[0], found[1]).astype(BF))
    return parts


def correlated(spec_ref, spec_sec, table_ref, count):
    rr, ri = spec_ref[:, :128], spec_ref[:, 128:]
    sr, si = spec_sec[:, :128], spec_sec[:, 128:]
    cross = jnp.concatenate([rr * sr + ri * si, ri * sr - rr * si], axis=1).astype(BF)
    middle = jnp.dot(cross, table_ref[512:768, :], preferred_element_type=F32).astype(BF)
    columns = []
    for m in range(count):
        rows = middle[m * CHIP_LEN : (m + 1) * CHIP_LEN]
        columns.append(jnp.concatenate([rows[:, :128], rows[:, 128:]], axis=0))
    corr = jnp.dot(
        table_ref[768:864, 0:128], jnp.concatenate(columns, axis=1), preferred_element_type=F32
    )
    lag_row = (iota((LAG_COUNT, 128), 0) - LAG_COUNT // 2).astype(F32) / OVERSAMPLE
    sums = []
    for m in range(count):
        re = corr[:LAG_COUNT, m * 128 : (m + 1) * 128]
        im = corr[LAG_COUNT:, m * 128 : (m + 1) * 128]
        energy = re * re + im * im
        weight = energy * energy
        sums.append(
            (
                jnp.sum(weight, axis=0, keepdims=True),
                jnp.sum(weight * lag_row, axis=0, keepdims=True),
            )
        )
    return sums


def inner_kernel(
    off_ref,
    sec_hbm,
    far_ref,
    near_ref,
    table_hbm,
    spec_ref,
    tot_ref,
    mom_ref,
    sec_ref,
    table_ref,
    scols_ref,
    chips_ref,
    half_ref,
    sems,
):
    fetch = begin(sems, (sec_hbm, sec_ref), (table_hbm, table_ref))
    odd = lax.axis_index("az") & 1
    none = jnp.zeros((2 * ROWS, 128), F32)
    for block in (0, SCRATCH_BLOCKS - 2, SCRATCH_BLOCKS - 1):
        scols_ref[block] = none

    def widen_rims(step, carry):
        for member in range(4):
            block = step * 4 + member
            at = pl.ds(pl.multiple_of(block * 128, 128), 128)
            for part in range(2):
                for rows_ref, low in ((near_ref, 1 - odd), (far_ref, odd)):
                    first = pl.multiple_of(part * ROWS + low * (MARGIN + LINES), 8)
                    scols_ref[block + 1, pl.ds(first, MARGIN), :] = rows_ref[part, :, at].astype(
                        F32
                    )
        return carry

    lax.fori_loop(0, BLOCKS // 4, widen_rims, 0)
    for copy in fetch:
        copy.wait()

    def widen(step, carry):
        for member in range(4):
            block = step * 4 + member
            at = pl.ds(pl.multiple_of(block * 128, 128), 128)
            for part in range(2):
                own = part * ROWS + MARGIN
                scols_ref[block + 1, own : own + LINES, :] = sec_ref[part, :, at].astype(F32)
        return carry

    lax.fori_loop(0, BLOCKS // 4, widen, 0)

    def cut(step, carry):
        for member in range(8):
            pair = step * 8 + member
            to = pl.ds(pl.multiple_of(pair * 128, 128), 128)
            re, im = cut_pair(off_ref, scols_ref, pair, 0)
            chips_ref[0:CHIP_LEN, to] = re
            chips_ref[CHIP_LEN : 2 * CHIP_LEN, to] = im
        return carry

    lax.fori_loop(0, PAIRS // 8, cut, 0)
    first_pass(table_ref, chips_ref, half_ref)

    def correlate(step, carry):
        size = GROUP * CHIP_LEN
        spec_sec = jnp.dot(
            side_by_side(half_ref, [step * GROUP + m for m in range(GROUP)]),
            table_ref[256:512, :],
            preferred_element_type=F32,
        )
        spec = spec_ref[pl.ds(pl.multiple_of(step * size, size), size), :]
        for m, (total, moment) in enumerate(correlated(spec, spec_sec, table_ref, GROUP)):
            row = pl.ds(step * GROUP + m, 1)
            tot_ref[row, :] = total
            mom_ref[row, :] = moment
        return carry

    lax.fori_loop(0, PAIRS // GROUP, correlate, 0)


def inner_pairs(off, sec, near, far, table, spectra):
    sums = jax.ShapeDtypeStruct((PAIRS, 128), F32)
    return pl.pallas_call(
        inner_kernel,
        out_shape=(sums, sums),
        in_specs=[smem, hbm, vmem, vmem, hbm, vmem],
        out_specs=(vmem, vmem),
        scratch_shapes=[
            pltpu.VMEM((2, LINES, COLS), BF),
            pltpu.VMEM(TABLE, BF),
            pltpu.VMEM((SCRATCH_BLOCKS, 2 * ROWS, 128), F32),
            pltpu.VMEM((2 * CHIP_LEN, CHIPS * 64), BF),
            pltpu.VMEM((2 * CHIP_LEN, CHIPS * 64), BF),
            pltpu.SemaphoreType.DMA((2,)),
        ],
        compiler_params=pltpu.CompilerParams(vmem_limit_bytes=24 * 2**20),
        cost_estimate=pl.CostEstimate(
            flops=6 * 10**9, bytes_accessed=20 * 10**6, transcendentals=0
        ),
        name="inner_pairs",
    )(off, sec, far, near, table, spectra)


def finish_kernel(
    off_ref,
    offv_ref,
    sent_mate_ref,
    sent_other_ref,
    got_mate_ref,
    got_other_ref,
    sec_hbm,
    start_hbm,
    taps_hbm,
    table_hbm,
    tot_ref,
    mom_ref,
    sum_hbm,
    pick_hbm,
    est_ref,
    out_ref,
    sum_ref,
    pick_ref,
    near_ref,
    start_ref,
    taps_ref,
    table_ref,
    edge_ref,
    padded_ref,
    scols_ref,
    lines_ref,
    packed_ref,
    table_sem,
    sems,
    out_sems,
):
    rg = lax.axis_index("rg")
    fetch_table = begin(table_sem, (table_hbm, table_ref))
    fetch = begin(
        sems,
        *band_copies(rg, start_hbm, taps_hbm, start_ref, taps_ref),
        (sec_hbm.at[:, :, 128:256], near_ref.at[0]),
        (sec_hbm.at[:, :, COLS - 256 : COLS - 128], near_ref.at[1]),
        (sum_hbm, sum_ref),
        (pick_hbm, pick_ref),
    )
    left_ref, first_ref, last_ref, right_ref = (edge_ref.at[n] for n in range(4))

    def ordered(refs):
        for to_ref, from_ref in zip((left_ref, first_ref, last_ref, right_ref), refs):
            to_ref[...] = from_ref[...]

    @pl.when((rg & 1) == 0)
    def _():
        ordered((got_other_ref, sent_other_ref, sent_mate_ref, got_mate_ref))

    @pl.when((rg & 1) == 1)
    def _():
        ordered((got_mate_ref, sent_mate_ref, sent_other_ref, got_other_ref))

    own_rows = slice(CHIP_LEN + MARGIN, CHIP_LEN + MARGIN + LINES)
    sides = (
        (left_ref, first_ref, 0),
        (last_ref, right_ref, 3),
    )
    for near_side, far_side, at in sides:
        for part in range(2):
            base = part * ROWS
            scols_ref[at, base : base + ROWS, :] = near_side[part, CHIP_LEN:, :].astype(F32)
            scols_ref[at + 1, base : base + ROWS, :] = far_side[part, CHIP_LEN:, :].astype(F32)
        scols_ref[at + 2] = jnp.zeros((2 * ROWS, 128), F32)

    def both_parts(ref, rows):
        return jnp.concatenate([ref[0, rows, :], ref[1, rows, :]], axis=0)

    chip_rows = slice(0, CHIP_LEN)
    columns = [
        even_pair(
            both_parts(left_ref, chip_rows).astype(F32),
            both_parts(first_ref, chip_rows).astype(F32),
        ),
        odd_pair(
            both_parts(last_ref, chip_rows).astype(F32),
            both_parts(right_ref, chip_rows).astype(F32),
        ),
        jnp.concatenate(cut_pair(off_ref, scols_ref, 0, 0), axis=0),
        jnp.concatenate(cut_pair(off_ref, scols_ref, PAIRS - 1, BLOCKS - 3), axis=0),
    ]
    for copy in fetch_table:
        copy.wait()
    half = jnp.dot(
        table_ref[864:992, 0:128],
        jnp.concatenate(columns, axis=1),
        preferred_element_type=F32,
    ).astype(BF)
    spec = jnp.dot(
        side_by_side(half, (0, 1)), table_ref[0:256, :], preferred_element_type=F32
    )
    spec_sec = jnp.dot(
        side_by_side(half, (2, 3)), table_ref[256:512, :], preferred_element_type=F32
    )
    outer = correlated(spec, spec_sec, table_ref, 2)

    wide = (PAIRS, 128)
    lanes = iota(wide, 1)
    pairs = iota(wide, 0)

    def completed(ref, which):
        return jnp.where(
            pairs == 0,
            outer[0][which],
            jnp.where(pairs == PAIRS - 1, outer[1][which], ref[...]),
        )

    total = completed(tot_ref, 0)
    moment = completed(mom_ref, 1)
    lag_lane = ((lanes & 63) - LAG_COUNT // 2).astype(F32) / OVERSAMPLE
    found = []
    for side in range(2):
        mask = (lanes < 64) if side == 0 else (lanes >= 64)

        def over(values):
            return jnp.sum(jnp.where(mask, values, 0.0), axis=1, keepdims=True)

        whole = over(total) + EPS
        found.append((over(moment) / whole, over(total * lag_lane) / whole))
    own_chip = (lanes >> 1) == pairs
    even = (lanes & 1) == 0

    def spread(which):
        values = jnp.where(even, found[0][which], found[1][which])
        return jnp.sum(jnp.where(own_chip, values, 0.0), axis=0, keepdims=True)

    padded_ref[...] = jnp.zeros((8, 128), jnp.int32)
    padded_ref[0:2, 0:CHIPS] = offv_ref[...]
    offsets = padded_ref[...].astype(F32)
    est_az = offsets[0:1, :] + spread(0)
    est_rg = offsets[1:2, :] + spread(1)
    est_ref[0:1, :] = est_az
    est_ref[1:2, :] = est_rg
    angle = PHASE_RATE * est_az
    cos_all = jnp.broadcast_to(jnp.cos(angle), (8, 128))
    sin_all = jnp.broadcast_to(jnp.sin(angle), (8, 128))

    for copy in fetch:
        copy.wait()
    start_ref[...] = start_ref[...] - rg * COLS
    every = slice(0, LINES)
    edge_columns = {
        0: (
            both_parts(left_ref, own_rows),
            both_parts(first_ref, own_rows),
            both_parts(near_ref.at[0], every),
        ),
        BLOCKS - 1: (
            both_parts(near_ref.at[1], every),
            both_parts(last_ref, own_rows),
            both_parts(right_ref, own_rows),
        ),
    }

    def turned(block):
        if block in edge_columns:
            cols = edge_columns[block]
            near = jnp.concatenate(
                [half_turned(cols[0], cols[1]), half_turned(cols[1], cols[2])], axis=1
            )
            summed = jnp.dot(
                near, sinc_band(start_ref, taps_ref, block), preferred_element_type=F32
            )
        else:
            summed = sum_ref[:, block * 128 : (block + 1) * 128]
        chip = block * 4 + (iota((8, 128), 1) >> 5)
        cosine = jnp.take_along_axis(cos_all, chip, axis=1)[0:1, :]
        sine = jnp.take_along_axis(sin_all, chip, axis=1)[0:1, :]
        re, im = summed[:LINES], summed[LINES:]
        half = block // HALF
        at = slice((block - half * HALF) * 128, (block - half * HALF + 1) * 128)
        base = half * 2 * LINES
        lines_ref[base : base + LINES, at] = (re * cosine + im * sine).astype(BF)
        lines_ref[base + LINES : base + 2 * LINES, at] = (im * cosine - re * sine).astype(BF)

    copies = []
    for first in range(0, WIDTH, 256):
        at = slice(first, first + 256)
        for block in (first // 128, first // 128 + 1):
            turned(block)
            turned(block + HALF)
        packed_ref[:, at] = jnp.dot(
            pick_ref[...], lines_ref[:, at], preferred_element_type=F32
        ).astype(BF)
        copy = pltpu.make_async_copy(
            packed_ref.at[:, at], out_ref.at[:, at], out_sems.at[first // 256]
        )
        copy.start()
        copies.append(copy)
    for copy in copies:
        copy.wait()


def finish(off, *arrays):
    return pl.pallas_call(
        finish_kernel,
        out_shape=(
            jax.ShapeDtypeStruct((2, 128), F32),
            jax.ShapeDtypeStruct((OWNERS * 8, WIDTH), BF),
        ),
        in_specs=[smem] + [vmem] * 5 + [hbm] * 4 + [vmem] * 2 + [hbm] * 2,
        out_specs=(vmem, hbm),
        scratch_shapes=[
            pltpu.VMEM((2 * LINES, COLS), F32),
            pltpu.VMEM((OWNERS * 8, 4 * LINES), BF),
            pltpu.VMEM((2, 2, LINES, 128), BF),
            pltpu.VMEM((BLOCKS, 128), jnp.int32),
            pltpu.VMEM((TAP_COUNT, COLS), BF),
            pltpu.VMEM(TABLE, BF),
            pltpu.VMEM((4, 2, CHIP_LEN + ROWS, 128), BF),
            pltpu.VMEM((8, 128), jnp.int32),
            pltpu.VMEM((6, 2 * ROWS, 128), F32),
            pltpu.VMEM((4 * LINES, WIDTH), BF),
            pltpu.VMEM((OWNERS * 8, WIDTH), BF),
            pltpu.SemaphoreType.DMA((1,)),
            pltpu.SemaphoreType.DMA((6,)),
            pltpu.SemaphoreType.DMA((WIDTH // 256,)),
        ],
        compiler_params=pltpu.CompilerParams(vmem_limit_bytes=52 * 2**20),
        cost_estimate=pl.CostEstimate(
            flops=2 * 10**9, bytes_accessed=10 * 10**6, transcendentals=0
        ),
        name="finish",
    )(off, off, *arrays)


def place_kernel(pick_ref, arr_ref, out_ref):
    pick = pick_ref[...]
    for first in range(0, WIDTH, 256):
        for piece in range(PLACED):
            lines = jnp.dot(
                pick,
                arr_ref[:, piece, :, first : first + 256].reshape(128, 256),
                preferred_element_type=F32,
            ).astype(BF)
            for half in range(2):
                begin_at = piece * COLS + half * WIDTH + first
                at = slice(begin_at, begin_at + 256)
                for part in range(2):
                    base = half * 64 + part * OWNER_CAP
                    out_ref[part, :, at] = lines[base : base + OWNER_CAP, :]


def place_lines(pick, arrived):
    return pl.pallas_call(
        place_kernel,
        grid=(PIECES // PLACED,),
        out_shape=jax.ShapeDtypeStruct((2, OWNER_CAP, COLS * PIECES), BF),
        in_specs=[
            pl.BlockSpec((128, 128), lambda r: (0, 0)),
            pl.BlockSpec((TILES, PLACED, 8, WIDTH), lambda r: (0, r, 0, 0)),
        ],
        out_specs=pl.BlockSpec((2, OWNER_CAP, PLACED * COLS), lambda r: (0, 0, r)),
        compiler_params=pltpu.CompilerParams(vmem_limit_bytes=20 * 2**20),
        cost_estimate=pl.CostEstimate(
            flops=10**9, bytes_accessed=8 * 10**6, transcendentals=0
        ),
        name="place_lines",
    )(pick, arrived)


def owner_table(src_row, line_owner, me):
    tile = src_row // LINES
    owned = line_owner == me
    ids = jnp.arange(ALL_LINES, dtype=jnp.int32)
    before = owned[None, :] & (ids[None, :] < ids[:, None])
    rank = jnp.sum(before.astype(jnp.int32), axis=1)
    rank_tile = jnp.sum((before & (tile[None, :] == tile[:, None])).astype(jnp.int32), axis=1)
    outs = jnp.arange(OWNER_CAP, dtype=jnp.int32)
    hit = owned[None, :] & (rank[None, :] == outs[:, None])
    code = jnp.sum(jnp.where(hit, (tile * 2 + rank_tile + 1)[None, :], 0), axis=1) - 1
    rows = jnp.arange(128, dtype=jnp.int32)[:, None]
    cols = jnp.arange(128, dtype=jnp.int32)[None, :]
    slot = jnp.tile(code, 4)[:, None]
    pick = (
        (slot == (cols >> 3) * 2 + ((cols >> 1) & 1))
        & ((rows >> 6) == ((cols >> 2) & 1))
        & (((rows >> 5) & 1) == (cols & 1))
    )
    return pick.astype(BF)


def exchanged(axis, mate, other):
    count = lax.axis_size(axis)

    def swap(block, first):
        pairs = [(i, i + 1) for i in range(first, count - 1, 2)]
        return lax.ppermute(block, axis, pairs + [(j, i) for i, j in pairs])

    from_other = swap(other, 1)
    return swap(mate, 0), from_other


def per_device(
    reference_slc, secondary_slc, chip_offsets, src_row, line_owner, band_start, band_taps
):
    az = lax.axis_index("az")
    rg = lax.axis_index("rg")
    starts = band_start.reshape(PIECES * BLOCKS, 128)
    table = kernel_table()
    near, far = exchanged("az", *rims(secondary_slc))
    summed, pick_sent, spectra = own_side(
        secondary_slc.reshape(2 * LINES, COLS),
        starts,
        band_taps,
        src_row.reshape(ALL_LINES // 128, 128),
        line_owner.reshape(ALL_LINES // 128, 128),
        reference_slc,
        table,
    )
    sent = rg_edges(reference_slc, secondary_slc, near, far)
    got = exchanged("rg", *sent)
    off = chip_offsets[:, 0, :]
    total, moment = inner_pairs(off, secondary_slc, near, far, table, spectra)
    est, packed = finish(
        off,
        *sent,
        *got,
        secondary_slc,
        starts,
        band_taps,
        table,
        total,
        moment,
        summed,
        pick_sent,
    )
    arrived = lax.all_to_all(packed, BOTH, 0, 0, tiled=True)
    pick = owner_table(src_row, line_owner, az * PIECES + rg)
    resampled = place_lines(pick, arrived.reshape(TILES, PIECES, 8, WIDTH))
    return est[:, None, :CHIPS], resampled


def solution(mesh):
    return jax.shard_map(
        per_device,
        mesh=mesh,
        in_specs=(
            P(None, "az", "rg"),
            P(None, "az", "rg"),
            P(None, "az", "rg"),
            P(),
            P(),
            P(),
            P(),
        ),
        out_specs=(P(None, "az", "rg"), P(None, BOTH, None)),
        check_vma=False,
    )
```

```python
import math

import jax
import jax.numpy as jnp
import ml_dtypes
import numpy as np
from jax import lax
from jax.experimental import pallas as pl
from jax.experimental.pallas import tpu as pltpu
from jax.sharding import PartitionSpec as P

CHIP_LEN = 64
OVERSAMPLE = 16
LAG_COUNT = 48
TAP_COUNT = 8
SPACING = 32
MARGIN = 64
PHASE_RATE = 2.0
EPS = 1e-06

TILES = 16
PIECES = 8
OWNERS = 128
LINES = 96
COLS = 3072
BLOCKS = COLS // 128
ALL_LINES = 1536
CHIPS = 96
PAIRS = CHIPS // 2
OWNER_CAP = 32
FIRST_ROW = 16
ROWS = LINES + 2 * MARGIN
HALF = BLOCKS // 2
WIDTH = HALF * 128
LINE_SPAN = 256
SCRATCH_BLOCKS = BLOCKS + 3
GROUP = 48
BAND_ROWS = 64
PLACED = 4
TABLE = (992, 256)
RIM_VMEM = 16 * 2**20
OWN_VMEM = 44 * 2**20
BOTH = ("az", "rg")
BF = jnp.bfloat16
F32 = jnp.float32


def numpy_tables():
    ids = np.arange(CHIP_LEN)
    angles = -2.0 * math.pi / CHIP_LEN * (ids[:, None] * ids[None, :] % CHIP_LEN)
    scale = 1.0 / math.sqrt(CHIP_LEN)

    def low(values):
        return values.astype(np.float32).astype(ml_dtypes.bfloat16).astype(np.float32)

    four = (low(np.cos(angles) * scale), low(np.sin(angles) * scale))
    steps = np.arange(LAG_COUNT) - LAG_COUNT // 2
    freq = np.where(ids < CHIP_LEN // 2, ids, ids - CHIP_LEN)
    turns = steps[:, None] * freq[None, :] % (OVERSAMPLE * CHIP_LEN)
    lifted = 2.0 * math.pi / (OVERSAMPLE * CHIP_LEN) * turns
    lift = (low(np.cos(lifted) * scale), low(np.sin(lifted) * scale))
    return four, lift


def kernel_table():
    four, lift = numpy_tables()

    def stacked(re, im):
        out = np.zeros((2 * re.shape[0], 256), np.float32)
        out[:, :128] = np.block([[re, -im], [im, re]])
        return out

    def paired(re, im, starts):
        out = np.zeros((2, 128, 2, 2, 64), np.float32)
        count = re.shape[0]
        for chip, first in enumerate(starts):
            rows = slice(first, first + CHIP_LEN)
            out[0, rows, 0, chip, :count] = re.T
            out[0, rows, 1, chip, :count] = im.T
            out[1, rows, 0, chip, :count] = -im.T
            out[1, rows, 1, chip, :count] = re.T
        return out.reshape(256, 256)

    whole = np.concatenate(
        [
            paired(*four, (0, 32)),
            paired(*four, (0, 64)),
            paired(*lift, (0, 64)),
            stacked(*lift),
            stacked(*four),
        ]
    )
    return jnp.asarray(whole.astype(ml_dtypes.bfloat16))


smem = pl.BlockSpec(memory_space=pltpu.SMEM)
vmem = pl.BlockSpec(memory_space=pltpu.VMEM)
hbm = pl.BlockSpec(memory_space=pltpu.HBM)


def iota(shape, dim):
    return lax.broadcasted_iota(jnp.int32, shape, dim)


def half_turned(left, right):
    lane = iota(left.shape, 1)
    return pltpu.roll(jnp.where(lane >= 64, left.astype(F32), right.astype(F32)), 64, 1).astype(BF)


def begin(sems, *pairs):
    started = [pltpu.make_async_copy(src, dst, sems.at[n]) for n, (src, dst) in enumerate(pairs)]
    for copy in started:
        copy.start()
    return started


def band_copies(rg, start_hbm, taps_hbm, start_ref, taps_ref):
    return (
        (start_hbm.at[pl.ds(pl.multiple_of(rg * BLOCKS, 8), BLOCKS), :], start_ref),
        (taps_hbm.at[:, pl.ds(pl.multiple_of(rg * COLS, 128), COLS)], taps_ref),
    )


def sinc_band(start_ref, taps_ref, block):
    start = start_ref[pl.ds(block, 1), :] - block * 128 + MARGIN
    taps = taps_ref[:, pl.ds(pl.multiple_of(block * 128, 128), 128)].astype(F32)
    chunks = []
    for first in range(0, 256, BAND_ROWS):
        offset = iota((BAND_ROWS, 128), 0) - (start - first)
        band = jnp.zeros((BAND_ROWS, 128), F32)
        for tap in range(TAP_COUNT):
            band = jnp.where(offset == tap, taps[tap : tap + 1, :], band)
        chunks.append(band.astype(BF))
    return jnp.concatenate(chunks, axis=0)


def own_kernel(
    sec_hbm,
    start_hbm,
    taps_hbm,
    src_ref,
    own_ref,
    ref_hbm,
    table_hbm,
    sum_ref,
    pick_ref,
    spec_ref,
    sec_ref,
    start_ref,
    taps_ref,
    shift_ref,
    table_ref,
    rcols_ref,
    chips_ref,
    half_ref,
    sems,
):
    az = lax.axis_index("az")
    rg = lax.axis_index("rg")
    rows = slice(FIRST_ROW, FIRST_ROW + CHIP_LEN)
    fetch = begin(
        sems,
        (sec_hbm, sec_ref),
        *band_copies(rg, start_hbm, taps_hbm, start_ref, taps_ref),
        (table_hbm, table_ref),
        *(
            (
                ref_hbm.at[part, rows, :],
                rcols_ref.at[part * CHIP_LEN : (part + 1) * CHIP_LEN, 128 : 128 + COLS],
            )
            for part in range(2)
        ),
    )

    line_block = jnp.minimum(jnp.maximum(az * LINES - 8, 0) // 128, ALL_LINES // 128 - 2)

    def spanned(ref):
        return jnp.concatenate(
            [ref[pl.ds(line_block, 1), :], ref[pl.ds(line_block + 1, 1), :]], axis=1
        )

    local = spanned(src_ref) - az * LINES
    owner = spanned(own_ref)
    here = (local >= 0) & (local < LINES)
    tagged = jnp.where(here, owner, -1).astype(F32)
    tagged_col = jnp.transpose(jnp.broadcast_to(tagged, (128, LINE_SPAN)))
    tagged_col = jnp.concatenate([tagged_col, tagged_col], axis=1)
    square = (LINE_SPAN, LINE_SPAN)
    earlier = iota(square, 0) < iota(square, 1)
    same = (tagged_col == tagged) & earlier
    rank = jnp.sum(jnp.where(same, 1.0, 0.0), axis=0, keepdims=True)
    slot = jnp.where(here, tagged * 2.0 + rank, -1.0)
    marked = jnp.where(here, local + 1, 0).astype(F32)
    marked_col = jnp.transpose(jnp.broadcast_to(marked, (128, LINE_SPAN))).astype(BF)
    for first in range(0, 1024, 256):
        ids = iota((256, LINE_SPAN), 0) + first
        wanted = ((ids >> 3) * 2 + ((ids >> 1) & 1)).astype(F32)
        hot = jnp.where(slot == wanted, 1.0, 0.0).astype(BF)
        found = jnp.dot(hot, marked_col, preferred_element_type=F32).astype(jnp.int32)
        ids = iota((256, 128), 0) + first
        base = ((ids >> 2) & 1) * (2 * LINES) + (ids & 1) * LINES - 1
        target = jnp.where(found > 0, found + base, -1)
        for block in range(3):
            lanes = iota((256, 128), 1) + block * 128
            pick_ref[first : first + 256, block * 128 : (block + 1) * 128] = jnp.where(
                lanes == target, 1.0, 0.0
            ).astype(BF)

    for copy in fetch:
        copy.wait()

    for at in range(128, COLS, 128):
        shift_ref[:, at : at + 128] = half_turned(
            sec_ref[:, at - 128 : at], sec_ref[:, at : at + 128]
        )
    start_ref[...] = start_ref[...] - rg * COLS

    def window(step, carry):
        for member in range(22):
            block = step * 22 + member + 1
            at = pl.multiple_of(block * 128, 128)
            sum_ref[:, pl.ds(at, 128)] = jnp.dot(
                shift_ref[:, pl.ds(at, 256)],
                sinc_band(start_ref, taps_ref, block),
                preferred_element_type=F32,
            )
        return carry

    lax.fori_loop(0, (BLOCKS - 2) // 22, window, 0)
    reference_spectra(table_ref, spec_ref, rcols_ref, chips_ref, half_ref)


def own_side(sec, starts, taps, src, own, ref, table):
    return pl.pallas_call(
        own_kernel,
        out_shape=(
            jax.ShapeDtypeStruct((2 * LINES, COLS), F32),
            jax.ShapeDtypeStruct((OWNERS * 8, 4 * LINES), BF),
            jax.ShapeDtypeStruct((PAIRS * CHIP_LEN, 256), F32),
        ),
        in_specs=[hbm] * 3 + [vmem] * 2 + [hbm] * 2,
        out_specs=(vmem,) * 3,
        scratch_shapes=[
            pltpu.VMEM((2 * LINES, COLS), BF),
            pltpu.VMEM((BLOCKS, 128), jnp.int32),
            pltpu.VMEM((TAP_COUNT, COLS), BF),
            pltpu.VMEM((2 * LINES, COLS), BF),
            pltpu.VMEM(TABLE, BF),
            pltpu.VMEM((2 * CHIP_LEN, SCRATCH_BLOCKS * 128), BF),
            pltpu.VMEM((2 * CHIP_LEN, CHIPS * 64), BF),
            pltpu.VMEM((2 * CHIP_LEN, CHIPS * 64), BF),
            pltpu.SemaphoreType.DMA((6,)),
        ],
        compiler_params=pltpu.CompilerParams(vmem_limit_bytes=OWN_VMEM),
        cost_estimate=pl.CostEstimate(
            flops=2 * 10**9, bytes_accessed=6 * 10**6, transcendentals=0
        ),
        name="own_side",
    )(sec, starts, taps, src, own, ref, table)


def rims_kernel(sec_hbm, mate_ref, other_ref, sems):
    odd = lax.axis_index("az") & 1
    pairs = []
    for to_ref, at in ((other_ref, odd), (mate_ref, 1 - odd)):
        first = at * (LINES - MARGIN)
        for part in range(2):
            for row in range(0, MARGIN, 32):
                pairs.append(
                    (
                        sec_hbm.at[part, pl.ds(pl.multiple_of(first + row, 16), 32), :],
                        to_ref.at[part, row : row + 32, :],
                    )
                )
    for copy in begin(sems, *pairs):
        copy.wait()


def rims(sec):
    rows = jax.ShapeDtypeStruct((2, MARGIN, COLS), BF)
    return pl.pallas_call(
        rims_kernel,
        out_shape=(rows, rows),
        in_specs=[hbm],
        out_specs=(hbm, hbm),
        scratch_shapes=[pltpu.SemaphoreType.DMA((8,))],
        compiler_params=pltpu.CompilerParams(vmem_limit_bytes=RIM_VMEM),
        cost_estimate=pl.CostEstimate(
            flops=4 * 10**9, bytes_accessed=4 * 10**6, transcendentals=0
        ),
        name="rims",
    )(sec)


def edges_kernel(ref_hbm, sec_hbm, far_ref, near_ref, mate_ref, other_ref, sems):
    odd_rows = lax.axis_index("az") & 1
    odd = lax.axis_index("rg") & 1
    own = CHIP_LEN + MARGIN
    pairs = []
    sides = []
    for to_ref, at in ((mate_ref, 1 - odd), (other_ref, odd)):
        cols = pl.ds(pl.multiple_of(at * (COLS - 128), 128), 128)
        sides.append((to_ref, cols))
        pairs += [
            (
                ref_hbm.at[:, FIRST_ROW : FIRST_ROW + CHIP_LEN, cols],
                to_ref.at[:, 0:CHIP_LEN, :],
            ),
            (sec_hbm.at[:, :, cols], to_ref.at[:, own : own + LINES, :]),
        ]
    fetch = begin(sems, *pairs)
    for to_ref, cols in sides:
        for rows_ref, low in ((near_ref, 1 - odd_rows), (far_ref, odd_rows)):
            at = pl.ds(pl.multiple_of(CHIP_LEN + low * (MARGIN + LINES), 16), MARGIN)
            for part in range(2):
                to_ref[part, at, :] = rows_ref[part, :, cols]
    for copy in fetch:
        copy.wait()


def rg_edges(ref, sec, near, far):
    cols = jax.ShapeDtypeStruct((2, CHIP_LEN + ROWS, 128), BF)
    return pl.pallas_call(
        edges_kernel,
        out_shape=(cols, cols),
        in_specs=[hbm, hbm, vmem, vmem],
        out_specs=(vmem, vmem),
        scratch_shapes=[pltpu.SemaphoreType.DMA((4,))],
        compiler_params=pltpu.CompilerParams(vmem_limit_bytes=8 * 2**20),
        cost_estimate=pl.CostEstimate(
            flops=4 * 10**9, bytes_accessed=4 * 10**6, transcendentals=0
        ),
        name="rg_edges",
    )(ref, sec, far, near)


def side_by_side(half, pairs):
    rows = []
    for pair in pairs:
        if isinstance(pair, int):
            at = slice(pair * 128, (pair + 1) * 128)
        else:
            at = pl.ds(pl.multiple_of(pair * 128, 128), 128)
        rows.append(
            jnp.concatenate([half[0:CHIP_LEN, at], half[CHIP_LEN : 2 * CHIP_LEN, at]], axis=1)
        )
    return jnp.concatenate(rows, axis=0)


def first_pass(table_ref, chips_ref, half_ref):
    fwd = table_ref[864:992, 0:128]
    for first in range(0, CHIPS * 64, 1024):
        half_ref[:, first : first + 1024] = jnp.dot(
            fwd, chips_ref[:, first : first + 1024], preferred_element_type=F32
        ).astype(BF)


def even_pair(near, here):
    lane = iota(near.shape, 1)
    return pltpu.roll(jnp.where(lane >= 112, near, here), 16, 1).astype(BF)


def odd_pair(here, far):
    lane = iota(far.shape, 1)
    return pltpu.roll(jnp.where(lane >= 48, here, far), 80, 1).astype(BF)


def reference_spectra(table_ref, spec_ref, rcols_ref, chips_ref, half_ref):
    none = jnp.zeros((2 * CHIP_LEN, 128), BF)
    rcols_ref[:, 0:128] = none
    rcols_ref[:, 128 + COLS : 256 + COLS] = none

    def cut(step, carry):
        def block(at):
            return rcols_ref[:, pl.ds(pl.multiple_of(at * 128, 128), 128)].astype(F32)

        for member in range(12):
            first = step * 12 + member
            near, here, far = block(first), block(first + 1), block(first + 2)
            to = pl.multiple_of(first * 256, 256)
            chips_ref[:, pl.ds(to, 128)] = even_pair(near, here)
            chips_ref[:, pl.ds(pl.multiple_of(to + 128, 128), 128)] = odd_pair(here, far)
        return carry

    lax.fori_loop(0, PAIRS // 24, cut, 0)
    first_pass(table_ref, chips_ref, half_ref)

    for step in range(PAIRS // GROUP):
        at = step * GROUP * CHIP_LEN
        spec_ref[at : at + GROUP * CHIP_LEN, :] = jnp.dot(
            side_by_side(half_ref, range(step * GROUP, (step + 1) * GROUP)),
            table_ref[0:256, :],
            preferred_element_type=F32,
        )


def cut_pair(off_ref, scols_ref, pair, first_block):
    lane = iota((CHIP_LEN, 128), 1)
    parts = []
    for part in range(2):
        found = []
        for side in range(2):
            chip = pair * 2 + side
            row = off_ref[0, chip] + (FIRST_ROW + MARGIN + part * ROWS)
            col = chip * SPACING + off_ref[1, chip] + 112
            block = (col >> 7) - first_block
            turn = col & 127
            near = scols_ref[block, pl.ds(row, CHIP_LEN), :]
            far = scols_ref[block + 1, pl.ds(row, CHIP_LEN), :]
            found.append(
                pltpu.roll(jnp.where(lane >= turn, near, far), (128 + side * 64 - turn) & 127, 1)
            )
        parts.append(jnp.where(lane < 64, found[0], found[1]).astype(BF))
    return parts


def correlated(spec_ref, spec_sec, table_ref, count):
    rr, ri = spec_ref[:, :128], spec_ref[:, 128:]
    sr, si = spec_sec[:, :128], spec_sec[:, 128:]
    cross = jnp.concatenate([rr * sr + ri * si, ri * sr - rr * si], axis=1).astype(BF)
    middle = jnp.dot(cross, table_ref[512:768, :], preferred_element_type=F32).astype(BF)
    columns = []
    for m in range(count):
        rows = middle[m * CHIP_LEN : (m + 1) * CHIP_LEN]
        columns.append(jnp.concatenate([rows[:, :128], rows[:, 128:]], axis=0))
    corr = jnp.dot(
        table_ref[768:864, 0:128], jnp.concatenate(columns, axis=1), preferred_element_type=F32
    )
    lag_row = (iota((LAG_COUNT, 128), 0) - LAG_COUNT // 2).astype(F32) / OVERSAMPLE
    sums = []
    for m in range(count):
        re = corr[:LAG_COUNT, m * 128 : (m + 1) * 128]
        im = corr[LAG_COUNT:, m * 128 : (m + 1) * 128]
        energy = re * re + im * im
        weight = energy * energy
        sums.append(
            (
                jnp.sum(weight, axis=0, keepdims=True),
                jnp.sum(weight * lag_row, axis=0, keepdims=True),
            )
        )
    return sums


def inner_kernel(
    off_ref,
    sec_hbm,
    far_ref,
    near_ref,
    table_hbm,
    spec_ref,
    tot_ref,
    mom_ref,
    sec_ref,
    table_ref,
    scols_ref,
    chips_ref,
    half_ref,
    sems,
):
    fetch = begin(sems, (sec_hbm, sec_ref), (table_hbm, table_ref))
    odd = lax.axis_index("az") & 1
    none = jnp.zeros((2 * ROWS, 128), F32)
    for block in (0, SCRATCH_BLOCKS - 2, SCRATCH_BLOCKS - 1):
        scols_ref[block] = none

    def widen_rims(step, carry):
        for member in range(12):
            block = step * 12 + member
            at = pl.ds(pl.multiple_of(block * 128, 128), 128)
            for part in range(2):
                for rows_ref, low in ((near_ref, 1 - odd), (far_ref, odd)):
                    first = pl.multiple_of(part * ROWS + low * (MARGIN + LINES), 8)
                    scols_ref[block + 1, pl.ds(first, MARGIN), :] = rows_ref[part, :, at].astype(
                        F32
                    )
        return carry

    lax.fori_loop(0, BLOCKS // 12, widen_rims, 0)
    for copy in fetch:
        copy.wait()

    def widen(step, carry):
        for member in range(12):
            block = step * 12 + member
            at = pl.ds(pl.multiple_of(block * 128, 128), 128)
            for part in range(2):
                own = part * ROWS + MARGIN
                scols_ref[block + 1, own : own + LINES, :] = sec_ref[part, :, at].astype(F32)
        return carry

    lax.fori_loop(0, BLOCKS // 12, widen, 0)

    def cut(step, carry):
        for member in range(16):
            pair = step * 16 + member
            to = pl.ds(pl.multiple_of(pair * 128, 128), 128)
            re, im = cut_pair(off_ref, scols_ref, pair, 0)
            chips_ref[0:CHIP_LEN, to] = re
            chips_ref[CHIP_LEN : 2 * CHIP_LEN, to] = im
        return carry

    lax.fori_loop(0, PAIRS // 16, cut, 0)
    first_pass(table_ref, chips_ref, half_ref)

    def correlate(step, carry):
        size = GROUP * CHIP_LEN
        spec_sec = jnp.dot(
            side_by_side(half_ref, [step * GROUP + m for m in range(GROUP)]),
            table_ref[256:512, :],
            preferred_element_type=F32,
        )
        spec = spec_ref[pl.ds(pl.multiple_of(step * size, size), size), :]
        for m, (total, moment) in enumerate(correlated(spec, spec_sec, table_ref, GROUP)):
            row = pl.ds(step * GROUP + m, 1)
            tot_ref[row, :] = total
            mom_ref[row, :] = moment
        return carry

    lax.fori_loop(0, PAIRS // GROUP, correlate, 0)


def inner_pairs(off, sec, near, far, table, spectra):
    sums = jax.ShapeDtypeStruct((PAIRS, 128), F32)
    return pl.pallas_call(
        inner_kernel,
        out_shape=(sums, sums),
        in_specs=[smem, hbm, vmem, vmem, hbm, vmem],
        out_specs=(vmem, vmem),
        scratch_shapes=[
            pltpu.VMEM((2, LINES, COLS), BF),
            pltpu.VMEM(TABLE, BF),
            pltpu.VMEM((SCRATCH_BLOCKS, 2 * ROWS, 128), F32),
            pltpu.VMEM((2 * CHIP_LEN, CHIPS * 64), BF),
            pltpu.VMEM((2 * CHIP_LEN, CHIPS * 64), BF),
            pltpu.SemaphoreType.DMA((2,)),
        ],
        compiler_params=pltpu.CompilerParams(vmem_limit_bytes=24 * 2**20),
        cost_estimate=pl.CostEstimate(
            flops=6 * 10**9, bytes_accessed=20 * 10**6, transcendentals=0
        ),
        name="inner_pairs",
    )(off, sec, far, near, table, spectra)


def finish_kernel(
    off_ref,
    offv_ref,
    sent_mate_ref,
    sent_other_ref,
    got_mate_ref,
    got_other_ref,
    sec_hbm,
    start_hbm,
    taps_hbm,
    table_hbm,
    tot_ref,
    mom_ref,
    sum_hbm,
    pick_hbm,
    est_ref,
    out_ref,
    sum_ref,
    pick_ref,
    near_ref,
    start_ref,
    taps_ref,
    table_ref,
    edge_ref,
    padded_ref,
    scols_ref,
    lines_ref,
    packed_ref,
    table_sem,
    sems,
    out_sems,
):
    rg = lax.axis_index("rg")
    fetch_table = begin(table_sem, (table_hbm, table_ref))
    fetch = begin(
        sems,
        *band_copies(rg, start_hbm, taps_hbm, start_ref, taps_ref),
        (sec_hbm.at[:, :, 128:256], near_ref.at[0]),
        (sec_hbm.at[:, :, COLS - 256 : COLS - 128], near_ref.at[1]),
        (sum_hbm, sum_ref),
        (pick_hbm, pick_ref),
    )
    left_ref, first_ref, last_ref, right_ref = (edge_ref.at[n] for n in range(4))

    def ordered(refs):
        for to_ref, from_ref in zip((left_ref, first_ref, last_ref, right_ref), refs):
            to_ref[...] = from_ref[...]

    @pl.when((rg & 1) == 0)
    def _():
        ordered((got_other_ref, sent_other_ref, sent_mate_ref, got_mate_ref))

    @pl.when((rg & 1) == 1)
    def _():
        ordered((got_mate_ref, sent_mate_ref, sent_other_ref, got_other_ref))

    own_rows = slice(CHIP_LEN + MARGIN, CHIP_LEN + MARGIN + LINES)
    sides = (
        (left_ref, first_ref, 0),
        (last_ref, right_ref, 3),
    )
    for near_side, far_side, at in sides:
        for part in range(2):
            base = part * ROWS
            scols_ref[at, base : base + ROWS, :] = near_side[part, CHIP_LEN:, :].astype(F32)
            scols_ref[at + 1, base : base + ROWS, :] = far_side[part, CHIP_LEN:, :].astype(F32)
        scols_ref[at + 2] = jnp.zeros((2 * ROWS, 128), F32)

    def both_parts(ref, rows):
        return jnp.concatenate([ref[0, rows, :], ref[1, rows, :]], axis=0)

    chip_rows = slice(0, CHIP_LEN)
    columns = [
        even_pair(
            both_parts(left_ref, chip_rows).astype(F32),
            both_parts(first_ref, chip_rows).astype(F32),
        ),
        odd_pair(
            both_parts(last_ref, chip_rows).astype(F32),
            both_parts(right_ref, chip_rows).astype(F32),
        ),
        jnp.concatenate(cut_pair(off_ref, scols_ref, 0, 0), axis=0),
        jnp.concatenate(cut_pair(off_ref, scols_ref, PAIRS - 1, BLOCKS - 3), axis=0),
    ]
    for copy in fetch_table:
        copy.wait()
    half = jnp.dot(
        table_ref[864:992, 0:128],
        jnp.concatenate(columns, axis=1),
        preferred_element_type=F32,
    ).astype(BF)
    spec = jnp.dot(
        side_by_side(half, (0, 1)), table_ref[0:256, :], preferred_element_type=F32
    )
    spec_sec = jnp.dot(
        side_by_side(half, (2, 3)), table_ref[256:512, :], preferred_element_type=F32
    )
    outer = correlated(spec, spec_sec, table_ref, 2)

    wide = (PAIRS, 128)
    lanes = iota(wide, 1)
    pairs = iota(wide, 0)

    def completed(ref, which):
        return jnp.where(
            pairs == 0,
            outer[0][which],
            jnp.where(pairs == PAIRS - 1, outer[1][which], ref[...]),
        )

    total = completed(tot_ref, 0)
    moment = completed(mom_ref, 1)
    lag_lane = ((lanes & 63) - LAG_COUNT // 2).astype(F32) / OVERSAMPLE
    found = []
    for side in range(2):
        mask = (lanes < 64) if side == 0 else (lanes >= 64)

        def over(values):
            return jnp.sum(jnp.where(mask, values, 0.0), axis=1, keepdims=True)

        whole = over(total) + EPS
        found.append((over(moment) / whole, over(total * lag_lane) / whole))
    own_chip = (lanes >> 1) == pairs
    even = (lanes & 1) == 0

    def spread(which):
        values = jnp.where(even, found[0][which], found[1][which])
        return jnp.sum(jnp.where(own_chip, values, 0.0), axis=0, keepdims=True)

    padded_ref[...] = jnp.zeros((8, 128), jnp.int32)
    padded_ref[0:2, 0:CHIPS] = offv_ref[...]
    offsets = padded_ref[...].astype(F32)
    est_az = offsets[0:1, :] + spread(0)
    est_rg = offsets[1:2, :] + spread(1)
    est_ref[0:1, :] = est_az
    est_ref[1:2, :] = est_rg
    angle = PHASE_RATE * est_az
    cos_all = jnp.broadcast_to(jnp.cos(angle), (8, 128))
    sin_all = jnp.broadcast_to(jnp.sin(angle), (8, 128))

    for copy in fetch:
        copy.wait()
    start_ref[...] = start_ref[...] - rg * COLS
    every = slice(0, LINES)
    edge_columns = {
        0: (
            both_parts(left_ref, own_rows),
            both_parts(first_ref, own_rows),
            both_parts(near_ref.at[0], every),
        ),
        BLOCKS - 1: (
            both_parts(near_ref.at[1], every),
            both_parts(last_ref, own_rows),
            both_parts(right_ref, own_rows),
        ),
    }

    def turned(block):
        if block in edge_columns:
            cols = edge_columns[block]
            near = jnp.concatenate(
                [half_turned(cols[0], cols[1]), half_turned(cols[1], cols[2])], axis=1
            )
            summed = jnp.dot(
                near, sinc_band(start_ref, taps_ref, block), preferred_element_type=F32
            )
        else:
            summed = sum_ref[:, block * 128 : (block + 1) * 128]
        chip = block * 4 + (iota((8, 128), 1) >> 5)
        cosine = jnp.take_along_axis(cos_all, chip, axis=1)[0:1, :]
        sine = jnp.take_along_axis(sin_all, chip, axis=1)[0:1, :]
        re, im = summed[:LINES], summed[LINES:]
        half = block // HALF
        at = slice((block - half * HALF) * 128, (block - half * HALF + 1) * 128)
        base = half * 2 * LINES
        lines_ref[base : base + LINES, at] = (re * cosine + im * sine).astype(BF)
        lines_ref[base + LINES : base + 2 * LINES, at] = (im * cosine - re * sine).astype(BF)

    copies = []
    for first in range(0, WIDTH, 256):
        at = slice(first, first + 256)
        for block in (first // 128, first // 128 + 1):
            turned(block)
            turned(block + HALF)
        packed_ref[:, at] = jnp.dot(
            pick_ref[...], lines_ref[:, at], preferred_element_type=F32
        ).astype(BF)
        copy = pltpu.make_async_copy(
            packed_ref.at[:, at], out_ref.at[:, at], out_sems.at[first // 256]
        )
        copy.start()
        copies.append(copy)
    for copy in copies:
        copy.wait()


def finish(off, *arrays):
    return pl.pallas_call(
        finish_kernel,
        out_shape=(
            jax.ShapeDtypeStruct((2, 128), F32),
            jax.ShapeDtypeStruct((OWNERS * 8, WIDTH), BF),
        ),
        in_specs=[smem] + [vmem] * 5 + [hbm] * 4 + [vmem] * 2 + [hbm] * 2,
        out_specs=(vmem, hbm),
        scratch_shapes=[
            pltpu.VMEM((2 * LINES, COLS), F32),
            pltpu.VMEM((OWNERS * 8, 4 * LINES), BF),
            pltpu.VMEM((2, 2, LINES, 128), BF),
            pltpu.VMEM((BLOCKS, 128), jnp.int32),
            pltpu.VMEM((TAP_COUNT, COLS), BF),
            pltpu.VMEM(TABLE, BF),
            pltpu.VMEM((4, 2, CHIP_LEN + ROWS, 128), BF),
            pltpu.VMEM((8, 128), jnp.int32),
            pltpu.VMEM((6, 2 * ROWS, 128), F32),
            pltpu.VMEM((4 * LINES, WIDTH), BF),
            pltpu.VMEM((OWNERS * 8, WIDTH), BF),
            pltpu.SemaphoreType.DMA((1,)),
            pltpu.SemaphoreType.DMA((6,)),
            pltpu.SemaphoreType.DMA((WIDTH // 256,)),
        ],
        compiler_params=pltpu.CompilerParams(vmem_limit_bytes=52 * 2**20),
        cost_estimate=pl.CostEstimate(
            flops=2 * 10**9, bytes_accessed=10 * 10**6, transcendentals=0
        ),
        name="finish",
    )(off, off, *arrays)


def place_kernel(pick_ref, arr_ref, out_ref):
    pick = pick_ref[...]
    for first in range(0, WIDTH, 256):
        for piece in range(PLACED):
            lines = jnp.dot(
                pick,
                arr_ref[:, piece, :, first : first + 256].reshape(128, 256),
                preferred_element_type=F32,
            ).astype(BF)
            for half in range(2):
                begin_at = piece * COLS + half * WIDTH + first
                at = slice(begin_at, begin_at + 256)
                for part in range(2):
                    base = half * 64 + part * OWNER_CAP
                    out_ref[part, :, at] = lines[base : base + OWNER_CAP, :]


def place_lines(pick, arrived):
    return pl.pallas_call(
        place_kernel,
        grid=(PIECES // PLACED,),
        out_shape=jax.ShapeDtypeStruct((2, OWNER_CAP, COLS * PIECES), BF),
        in_specs=[
            pl.BlockSpec((128, 128), lambda r: (0, 0)),
            pl.BlockSpec((TILES, PLACED, 8, WIDTH), lambda r: (0, r, 0, 0)),
        ],
        out_specs=pl.BlockSpec((2, OWNER_CAP, PLACED * COLS), lambda r: (0, 0, r)),
        compiler_params=pltpu.CompilerParams(vmem_limit_bytes=20 * 2**20),
        cost_estimate=pl.CostEstimate(
            flops=10**9, bytes_accessed=8 * 10**6, transcendentals=0
        ),
        name="place_lines",
    )(pick, arrived)


def owner_table(src_row, line_owner, me):
    tile = src_row // LINES
    owned = line_owner == me
    ids = jnp.arange(ALL_LINES, dtype=jnp.int32)
    before = owned[None, :] & (ids[None, :] < ids[:, None])
    rank = jnp.sum(before.astype(jnp.int32), axis=1)
    rank_tile = jnp.sum((before & (tile[None, :] == tile[:, None])).astype(jnp.int32), axis=1)
    outs = jnp.arange(OWNER_CAP, dtype=jnp.int32)
    hit = owned[None, :] & (rank[None, :] == outs[:, None])
    code = jnp.sum(jnp.where(hit, (tile * 2 + rank_tile + 1)[None, :], 0), axis=1) - 1
    rows = jnp.arange(128, dtype=jnp.int32)[:, None]
    cols = jnp.arange(128, dtype=jnp.int32)[None, :]
    slot = jnp.tile(code, 4)[:, None]
    pick = (
        (slot == (cols >> 3) * 2 + ((cols >> 1) & 1))
        & ((rows >> 6) == ((cols >> 2) & 1))
        & (((rows >> 5) & 1) == (cols & 1))
    )
    return pick.astype(BF)


def exchanged(axis, mate, other):
    count = lax.axis_size(axis)

    def swap(block, first):
        pairs = [(i, i + 1) for i in range(first, count - 1, 2)]
        return lax.ppermute(block, axis, pairs + [(j, i) for i, j in pairs])

    from_other = swap(other, 1)
    return swap(mate, 0), from_other


def per_device(
    reference_slc, secondary_slc, chip_offsets, src_row, line_owner, band_start, band_taps
):
    az = lax.axis_index("az")
    rg = lax.axis_index("rg")
    starts = band_start.reshape(PIECES * BLOCKS, 128)
    table = kernel_table()
    near, far = exchanged("az", *rims(secondary_slc))
    summed, pick_sent, spectra = own_side(
        secondary_slc.reshape(2 * LINES, COLS),
        starts,
        band_taps,
        src_row.reshape(ALL_LINES // 128, 128),
        line_owner.reshape(ALL_LINES // 128, 128),
        reference_slc,
        table,
    )
    sent = rg_edges(reference_slc, secondary_slc, near, far)
    got = exchanged("rg", *sent)
    off = chip_offsets[:, 0, :]
    total, moment = inner_pairs(off, secondary_slc, near, far, table, spectra)
    est, packed = finish(
        off,
        *sent,
        *got,
        secondary_slc,
        starts,
        band_taps,
        table,
        total,
        moment,
        summed,
        pick_sent,
    )
    arrived = lax.all_to_all(packed, BOTH, 0, 0, tiled=True)
    pick = owner_table(src_row, line_owner, az * PIECES + rg)
    resampled = place_lines(pick, arrived.reshape(TILES, PIECES, 8, WIDTH))
    return est[:, None, :CHIPS], resampled


def solution(mesh):
    return jax.shard_map(
        per_device,
        mesh=mesh,
        in_specs=(
            P(None, "az", "rg"),
            P(None, "az", "rg"),
            P(None, "az", "rg"),
            P(),
            P(),
            P(),
            P(),
        ),
        out_specs=(P(None, "az", "rg"), P(None, BOTH, None)),
        check_vma=False,
    )
```

```python
import math

import jax
import jax.numpy as jnp
import ml_dtypes
import numpy as np
from jax import lax
from jax.experimental import pallas as pl
from jax.experimental.pallas import tpu as pltpu
from jax.sharding import PartitionSpec as P

CHIP_LEN = 64
OVERSAMPLE = 16
LAG_COUNT = 48
TAP_COUNT = 8
SPACING = 32
MARGIN = 64
PHASE_RATE = 2.0
EPS = 1e-06

TILES = 16
PIECES = 8
OWNERS = 128
LINES = 96
COLS = 3072
BLOCKS = COLS // 128
ALL_LINES = 1536
CHIPS = 96
PAIRS = CHIPS // 2
OWNER_CAP = 32
FIRST_ROW = 16
ROWS = LINES + 2 * MARGIN
HALF = BLOCKS // 2
WIDTH = HALF * 128
LINE_SPAN = 256
SCRATCH_BLOCKS = BLOCKS + 3
GROUP = 48
BAND_ROWS = 64
PLACED = 4
TABLE = (992, 256)
RIM_VMEM = 16 * 2**20
OWN_VMEM = 44 * 2**20
BOTH = ("az", "rg")
BF = jnp.bfloat16
F32 = jnp.float32


def numpy_tables():
    ids = np.arange(CHIP_LEN)
    angles = -2.0 * math.pi / CHIP_LEN * (ids[:, None] * ids[None, :] % CHIP_LEN)
    scale = 1.0 / math.sqrt(CHIP_LEN)

    def low(values):
        return values.astype(np.float32).astype(ml_dtypes.bfloat16).astype(np.float32)

    four = (low(np.cos(angles) * scale), low(np.sin(angles) * scale))
    steps = np.arange(LAG_COUNT) - LAG_COUNT // 2
    freq = np.where(ids < CHIP_LEN // 2, ids, ids - CHIP_LEN)
    turns = steps[:, None] * freq[None, :] % (OVERSAMPLE * CHIP_LEN)
    lifted = 2.0 * math.pi / (OVERSAMPLE * CHIP_LEN) * turns
    lift = (low(np.cos(lifted) * scale), low(np.sin(lifted) * scale))
    return four, lift


def kernel_table():
    four, lift = numpy_tables()

    def stacked(re, im):
        out = np.zeros((2 * re.shape[0], 256), np.float32)
        out[:, :128] = np.block([[re, -im], [im, re]])
        return out

    def paired(re, im, starts):
        out = np.zeros((2, 128, 2, 2, 64), np.float32)
        count = re.shape[0]
        for chip, first in enumerate(starts):
            rows = slice(first, first + CHIP_LEN)
            out[0, rows, 0, chip, :count] = re.T
            out[0, rows, 1, chip, :count] = im.T
            out[1, rows, 0, chip, :count] = -im.T
            out[1, rows, 1, chip, :count] = re.T
        return out.reshape(256, 256)

    whole = np.concatenate(
        [
            paired(*four, (0, 32)),
            paired(*four, (0, 64)),
            paired(*lift, (0, 64)),
            stacked(*lift),
            stacked(*four),
        ]
    )
    return jnp.asarray(whole.astype(ml_dtypes.bfloat16))


smem = pl.BlockSpec(memory_space=pltpu.SMEM)
vmem = pl.BlockSpec(memory_space=pltpu.VMEM)
hbm = pl.BlockSpec(memory_space=pltpu.HBM)


def iota(shape, dim):
    return lax.broadcasted_iota(jnp.int32, shape, dim)


def half_turned(left, right):
    lane = iota(left.shape, 1)
    return pltpu.roll(jnp.where(lane >= 64, left.astype(F32), right.astype(F32)), 64, 1).astype(BF)


def begin(sems, *pairs):
    started = [pltpu.make_async_copy(src, dst, sems.at[n]) for n, (src, dst) in enumerate(pairs)]
    for copy in started:
        copy.start()
    return started


def band_copies(rg, start_hbm, taps_hbm, start_ref, taps_ref):
    return (
        (start_hbm.at[pl.ds(pl.multiple_of(rg * BLOCKS, 8), BLOCKS), :], start_ref),
        (taps_hbm.at[:, pl.ds(pl.multiple_of(rg * COLS, 128), COLS)], taps_ref),
    )


def sinc_band(start_ref, taps_ref, block):
    start = start_ref[pl.ds(block, 1), :] - block * 128 + MARGIN
    taps = taps_ref[:, pl.ds(pl.multiple_of(block * 128, 128), 128)].astype(F32)
    chunks = []
    for first in range(0, 256, BAND_ROWS):
        offset = iota((BAND_ROWS, 128), 0) - (start - first)
        band = jnp.zeros((BAND_ROWS, 128), F32)
        for tap in range(TAP_COUNT):
            band = jnp.where(offset == tap, taps[tap : tap + 1, :], band)
        chunks.append(band.astype(BF))
    return jnp.concatenate(chunks, axis=0)


def own_kernel(
    sec_hbm,
    start_hbm,
    taps_hbm,
    src_ref,
    own_ref,
    ref_hbm,
    table_hbm,
    sum_ref,
    pick_ref,
    spec_ref,
    sec_ref,
    start_ref,
    taps_ref,
    shift_ref,
    table_ref,
    rcols_ref,
    chips_ref,
    half_ref,
    sems,
):
    az = lax.axis_index("az")
    rg = lax.axis_index("rg")
    rows = slice(FIRST_ROW, FIRST_ROW + CHIP_LEN)
    fetch = begin(
        sems,
        (sec_hbm, sec_ref),
        *band_copies(rg, start_hbm, taps_hbm, start_ref, taps_ref),
        (table_hbm, table_ref),
        *(
            (
                ref_hbm.at[part, rows, :],
                rcols_ref.at[part * CHIP_LEN : (part + 1) * CHIP_LEN, 128 : 128 + COLS],
            )
            for part in range(2)
        ),
    )

    line_block = jnp.minimum(jnp.maximum(az * LINES - 8, 0) // 128, ALL_LINES // 128 - 2)

    def spanned(ref):
        return jnp.concatenate(
            [ref[pl.ds(line_block, 1), :], ref[pl.ds(line_block + 1, 1), :]], axis=1
        )

    local = spanned(src_ref) - az * LINES
    owner = spanned(own_ref)
    here = (local >= 0) & (local < LINES)
    tagged = jnp.where(here, owner, -1).astype(F32)
    tagged_col = jnp.transpose(jnp.broadcast_to(tagged, (128, LINE_SPAN)))
    tagged_col = jnp.concatenate([tagged_col, tagged_col], axis=1)
    square = (LINE_SPAN, LINE_SPAN)
    earlier = iota(square, 0) < iota(square, 1)
    same = (tagged_col == tagged) & earlier
    rank = jnp.sum(jnp.where(same, 1.0, 0.0), axis=0, keepdims=True)
    slot = jnp.where(here, tagged * 2.0 + rank, -1.0)
    marked = jnp.where(here, local + 1, 0).astype(F32)
    marked_col = jnp.transpose(jnp.broadcast_to(marked, (128, LINE_SPAN))).astype(BF)
    for first in range(0, 1024, 256):
        ids = iota((256, LINE_SPAN), 0) + first
        wanted = ((ids >> 3) * 2 + ((ids >> 1) & 1)).astype(F32)
        hot = jnp.where(slot == wanted, 1.0, 0.0).astype(BF)
        found = jnp.dot(hot, marked_col, preferred_element_type=F32).astype(jnp.int32)
        ids = iota((256, 128), 0) + first
        base = ((ids >> 2) & 1) * (2 * LINES) + (ids & 1) * LINES - 1
        target = jnp.where(found > 0, found + base, -1)
        for block in range(3):
            lanes = iota((256, 128), 1) + block * 128
            pick_ref[first : first + 256, block * 128 : (block + 1) * 128] = jnp.where(
                lanes == target, 1.0, 0.0
            ).astype(BF)

    for copy in fetch:
        copy.wait()

    for at in range(128, COLS, 128):
        shift_ref[:, at : at + 128] = half_turned(
            sec_ref[:, at - 128 : at], sec_ref[:, at : at + 128]
        )
    start_ref[...] = start_ref[...] - rg * COLS

    def window(step, carry):
        for member in range(22):
            block = step * 22 + member + 1
            at = pl.multiple_of(block * 128, 128)
            sum_ref[:, pl.ds(at, 128)] = jnp.dot(
                shift_ref[:, pl.ds(at, 256)],
                sinc_band(start_ref, taps_ref, block),
                preferred_element_type=F32,
            )
        return carry

    lax.fori_loop(0, (BLOCKS - 2) // 22, window, 0)
    reference_spectra(table_ref, spec_ref, rcols_ref, chips_ref, half_ref)


def own_side(sec, starts, taps, src, own, ref, table):
    return pl.pallas_call(
        own_kernel,
        out_shape=(
            jax.ShapeDtypeStruct((2 * LINES, COLS), F32),
            jax.ShapeDtypeStruct((OWNERS * 8, 4 * LINES), BF),
            jax.ShapeDtypeStruct((PAIRS * CHIP_LEN, 256), F32),
        ),
        in_specs=[hbm] * 3 + [vmem] * 2 + [hbm] * 2,
        out_specs=(vmem,) * 3,
        scratch_shapes=[
            pltpu.VMEM((2 * LINES, COLS), BF),
            pltpu.VMEM((BLOCKS, 128), jnp.int32),
            pltpu.VMEM((TAP_COUNT, COLS), BF),
            pltpu.VMEM((2 * LINES, COLS), BF),
            pltpu.VMEM(TABLE, BF),
            pltpu.VMEM((2 * CHIP_LEN, SCRATCH_BLOCKS * 128), BF),
            pltpu.VMEM((2 * CHIP_LEN, CHIPS * 64), BF),
            pltpu.VMEM((2 * CHIP_LEN, CHIPS * 64), BF),
            pltpu.SemaphoreType.DMA((6,)),
        ],
        compiler_params=pltpu.CompilerParams(vmem_limit_bytes=OWN_VMEM),
        cost_estimate=pl.CostEstimate(
            flops=2 * 10**9, bytes_accessed=6 * 10**6, transcendentals=0
        ),
        name="own_side",
    )(sec, starts, taps, src, own, ref, table)


def rims_kernel(sec_ref, mate_ref, other_ref):
    odd = lax.axis_index("az") & 1
    for to_ref, at in ((other_ref, odd), (mate_ref, 1 - odd)):
        rows = pl.ds(pl.multiple_of(at * (LINES - MARGIN), 32), MARGIN)
        for part in range(2):
            to_ref[part] = sec_ref[part, rows, :]


def rims(sec):
    rows = jax.ShapeDtypeStruct((2, MARGIN, COLS), BF)
    return pl.pallas_call(
        rims_kernel,
        out_shape=(rows, rows),
        in_specs=[vmem],
        out_specs=(vmem, vmem),
        compiler_params=pltpu.CompilerParams(vmem_limit_bytes=RIM_VMEM),
        cost_estimate=pl.CostEstimate(
            flops=4 * 10**9, bytes_accessed=4 * 10**6, transcendentals=0
        ),
        name="rims",
    )(sec)


def edges_kernel(ref_hbm, sec_hbm, far_ref, near_ref, mate_ref, other_ref, sems):
    odd_rows = lax.axis_index("az") & 1
    odd = lax.axis_index("rg") & 1
    own = CHIP_LEN + MARGIN
    pairs = []
    sides = []
    for to_ref, at in ((mate_ref, 1 - odd), (other_ref, odd)):
        cols = pl.ds(pl.multiple_of(at * (COLS - 128), 128), 128)
        sides.append((to_ref, cols))
        pairs += [
            (
                ref_hbm.at[:, FIRST_ROW : FIRST_ROW + CHIP_LEN, cols],
                to_ref.at[:, 0:CHIP_LEN, :],
            ),
            (sec_hbm.at[:, :, cols], to_ref.at[:, own : own + LINES, :]),
        ]
    fetch = begin(sems, *pairs)
    for to_ref, cols in sides:
        for rows_ref, low in ((near_ref, 1 - odd_rows), (far_ref, odd_rows)):
            at = pl.ds(pl.multiple_of(CHIP_LEN + low * (MARGIN + LINES), 16), MARGIN)
            for part in range(2):
                to_ref[part, at, :] = rows_ref[part, :, cols]
    for copy in fetch:
        copy.wait()


def rg_edges(ref, sec, near, far):
    cols = jax.ShapeDtypeStruct((2, CHIP_LEN + ROWS, 128), BF)
    return pl.pallas_call(
        edges_kernel,
        out_shape=(cols, cols),
        in_specs=[hbm, hbm, vmem, vmem],
        out_specs=(vmem, vmem),
        scratch_shapes=[pltpu.SemaphoreType.DMA((4,))],
        compiler_params=pltpu.CompilerParams(vmem_limit_bytes=8 * 2**20),
        cost_estimate=pl.CostEstimate(
            flops=4 * 10**9, bytes_accessed=4 * 10**6, transcendentals=0
        ),
        name="rg_edges",
    )(ref, sec, far, near)


def side_by_side(half, pairs):
    rows = []
    for pair in pairs:
        if isinstance(pair, int):
            at = slice(pair * 128, (pair + 1) * 128)
        else:
            at = pl.ds(pl.multiple_of(pair * 128, 128), 128)
        rows.append(
            jnp.concatenate([half[0:CHIP_LEN, at], half[CHIP_LEN : 2 * CHIP_LEN, at]], axis=1)
        )
    return jnp.concatenate(rows, axis=0)


def first_pass(table_ref, chips_ref, half_ref):
    fwd = table_ref[864:992, 0:128]
    for first in range(0, CHIPS * 64, 1024):
        half_ref[:, first : first + 1024] = jnp.dot(
            fwd, chips_ref[:, first : first + 1024], preferred_element_type=F32
        ).astype(BF)


def even_pair(near, here):
    lane = iota(near.shape, 1)
    return pltpu.roll(jnp.where(lane >= 112, near, here), 16, 1).astype(BF)


def odd_pair(here, far):
    lane = iota(far.shape, 1)
    return pltpu.roll(jnp.where(lane >= 48, here, far), 80, 1).astype(BF)


def reference_spectra(table_ref, spec_ref, rcols_ref, chips_ref, half_ref):
    none = jnp.zeros((2 * CHIP_LEN, 128), BF)
    rcols_ref[:, 0:128] = none
    rcols_ref[:, 128 + COLS : 256 + COLS] = none

    def cut(step, carry):
        def block(at):
            return rcols_ref[:, pl.ds(pl.multiple_of(at * 128, 128), 128)].astype(F32)

        for member in range(12):
            first = step * 12 + member
            near, here, far = block(first), block(first + 1), block(first + 2)
            to = pl.multiple_of(first * 256, 256)
            chips_ref[:, pl.ds(to, 128)] = even_pair(near, here)
            chips_ref[:, pl.ds(pl.multiple_of(to + 128, 128), 128)] = odd_pair(here, far)
        return carry

    lax.fori_loop(0, PAIRS // 24, cut, 0)
    first_pass(table_ref, chips_ref, half_ref)

    for step in range(PAIRS // GROUP):
        at = step * GROUP * CHIP_LEN
        spec_ref[at : at + GROUP * CHIP_LEN, :] = jnp.dot(
            side_by_side(half_ref, range(step * GROUP, (step + 1) * GROUP)),
            table_ref[0:256, :],
            preferred_element_type=F32,
        )


def cut_pair(off_ref, scols_ref, pair, first_block):
    lane = iota((CHIP_LEN, 128), 1)
    parts = []
    for part in range(2):
        found = []
        for side in range(2):
            chip = pair * 2 + side
            row = off_ref[0, chip] + (FIRST_ROW + MARGIN + part * ROWS)
            col = chip * SPACING + off_ref[1, chip] + 112
            block = (col >> 7) - first_block
            turn = col & 127
            near = scols_ref[block, pl.ds(row, CHIP_LEN), :]
            far = scols_ref[block + 1, pl.ds(row, CHIP_LEN), :]
            found.append(
                pltpu.roll(jnp.where(lane >= turn, near, far), (128 + side * 64 - turn) & 127, 1)
            )
        parts.append(jnp.where(lane < 64, found[0], found[1]).astype(BF))
    return parts


def correlated(spec_ref, spec_sec, table_ref, count):
    rr, ri = spec_ref[:, :128], spec_ref[:, 128:]
    sr, si = spec_sec[:, :128], spec_sec[:, 128:]
    cross = jnp.concatenate([rr * sr + ri * si, ri * sr - rr * si], axis=1).astype(BF)
    middle = jnp.dot(cross, table_ref[512:768, :], preferred_element_type=F32).astype(BF)
    columns = []
    for m in range(count):
        rows = middle[m * CHIP_LEN : (m + 1) * CHIP_LEN]
        columns.append(jnp.concatenate([rows[:, :128], rows[:, 128:]], axis=0))
    corr = jnp.dot(
        table_ref[768:864, 0:128], jnp.concatenate(columns, axis=1), preferred_element_type=F32
    )
    lag_row = (iota((LAG_COUNT, 128), 0) - LAG_COUNT // 2).astype(F32) / OVERSAMPLE
    sums = []
    for m in range(count):
        re = corr[:LAG_COUNT, m * 128 : (m + 1) * 128]
        im = corr[LAG_COUNT:, m * 128 : (m + 1) * 128]
        energy = re * re + im * im
        weight = energy * energy
        sums.append(
            (
                jnp.sum(weight, axis=0, keepdims=True),
                jnp.sum(weight * lag_row, axis=0, keepdims=True),
            )
        )
    return sums


def inner_kernel(
    off_ref,
    sec_hbm,
    far_ref,
    near_ref,
    table_hbm,
    spec_ref,
    tot_ref,
    mom_ref,
    sec_ref,
    table_ref,
    scols_ref,
    chips_ref,
    half_ref,
    sems,
):
    fetch = begin(sems, (sec_hbm, sec_ref), (table_hbm, table_ref))
    odd = lax.axis_index("az") & 1
    none = jnp.zeros((2 * ROWS, 128), F32)
    for block in (0, SCRATCH_BLOCKS - 2, SCRATCH_BLOCKS - 1):
        scols_ref[block] = none

    def widen_rims(step, carry):
        for member in range(12):
            block = step * 12 + member
            at = pl.ds(pl.multiple_of(block * 128, 128), 128)
            for part in range(2):
                for rows_ref, low in ((near_ref, 1 - odd), (far_ref, odd)):
                    first = pl.multiple_of(part * ROWS + low * (MARGIN + LINES), 8)
                    scols_ref[block + 1, pl.ds(first, MARGIN), :] = rows_ref[part, :, at].astype(
                        F32
                    )
        return carry

    lax.fori_loop(0, BLOCKS // 12, widen_rims, 0)
    for copy in fetch:
        copy.wait()

    def widen(step, carry):
        for member in range(12):
            block = step * 12 + member
            at = pl.ds(pl.multiple_of(block * 128, 128), 128)
            for part in range(2):
                own = part * ROWS + MARGIN
                scols_ref[block + 1, own : own + LINES, :] = sec_ref[part, :, at].astype(F32)
        return carry

    lax.fori_loop(0, BLOCKS // 12, widen, 0)

    def cut(step, carry):
        for member in range(16):
            pair = step * 16 + member
            to = pl.ds(pl.multiple_of(pair * 128, 128), 128)
            re, im = cut_pair(off_ref, scols_ref, pair, 0)
            chips_ref[0:CHIP_LEN, to] = re
            chips_ref[CHIP_LEN : 2 * CHIP_LEN, to] = im
        return carry

    lax.fori_loop(0, PAIRS // 16, cut, 0)
    first_pass(table_ref, chips_ref, half_ref)

    def correlate(step, carry):
        size = GROUP * CHIP_LEN
        spec_sec = jnp.dot(
            side_by_side(half_ref, [step * GROUP + m for m in range(GROUP)]),
            table_ref[256:512, :],
            preferred_element_type=F32,
        )
        spec = spec_ref[pl.ds(pl.multiple_of(step * size, size), size), :]
        for m, (total, moment) in enumerate(correlated(spec, spec_sec, table_ref, GROUP)):
            row = pl.ds(step * GROUP + m, 1)
            tot_ref[row, :] = total
            mom_ref[row, :] = moment
        return carry

    lax.fori_loop(0, PAIRS // GROUP, correlate, 0)


def inner_pairs(off, sec, near, far, table, spectra):
    sums = jax.ShapeDtypeStruct((PAIRS, 128), F32)
    return pl.pallas_call(
        inner_kernel,
        out_shape=(sums, sums),
        in_specs=[smem, hbm, vmem, vmem, hbm, vmem],
        out_specs=(vmem, vmem),
        scratch_shapes=[
            pltpu.VMEM((2, LINES, COLS), BF),
            pltpu.VMEM(TABLE, BF),
            pltpu.VMEM((SCRATCH_BLOCKS, 2 * ROWS, 128), F32),
            pltpu.VMEM((2 * CHIP_LEN, CHIPS * 64), BF),
            pltpu.VMEM((2 * CHIP_LEN, CHIPS * 64), BF),
            pltpu.SemaphoreType.DMA((2,)),
        ],
        compiler_params=pltpu.CompilerParams(vmem_limit_bytes=24 * 2**20),
        cost_estimate=pl.CostEstimate(
            flops=6 * 10**9, bytes_accessed=20 * 10**6, transcendentals=0
        ),
        name="inner_pairs",
    )(off, sec, far, near, table, spectra)


def finish_kernel(
    off_ref,
    offv_ref,
    sent_mate_ref,
    sent_other_ref,
    got_mate_ref,
    got_other_ref,
    sec_hbm,
    start_hbm,
    taps_hbm,
    table_hbm,
    tot_ref,
    mom_ref,
    sum_hbm,
    pick_hbm,
    est_ref,
    out_ref,
    sum_ref,
    pick_ref,
    near_ref,
    start_ref,
    taps_ref,
    table_ref,
    edge_ref,
    padded_ref,
    scols_ref,
    lines_ref,
    packed_ref,
    table_sem,
    sems,
    out_sems,
):
    rg = lax.axis_index("rg")
    fetch_table = begin(table_sem, (table_hbm, table_ref))
    fetch = begin(
        sems,
        *band_copies(rg, start_hbm, taps_hbm, start_ref, taps_ref),
        (sec_hbm.at[:, :, 128:256], near_ref.at[0]),
        (sec_hbm.at[:, :, COLS - 256 : COLS - 128], near_ref.at[1]),
        (sum_hbm, sum_ref),
        (pick_hbm, pick_ref),
    )
    left_ref, first_ref, last_ref, right_ref = (edge_ref.at[n] for n in range(4))

    def ordered(refs):
        for to_ref, from_ref in zip((left_ref, first_ref, last_ref, right_ref), refs):
            to_ref[...] = from_ref[...]

    @pl.when((rg & 1) == 0)
    def _():
        ordered((got_other_ref, sent_other_ref, sent_mate_ref, got_mate_ref))

    @pl.when((rg & 1) == 1)
    def _():
        ordered((got_mate_ref, sent_mate_ref, sent_other_ref, got_other_ref))

    own_rows = slice(CHIP_LEN + MARGIN, CHIP_LEN + MARGIN + LINES)
    sides = (
        (left_ref, first_ref, 0),
        (last_ref, right_ref, 3),
    )
    for near_side, far_side, at in sides:
        for part in range(2):
            base = part * ROWS
            scols_ref[at, base : base + ROWS, :] = near_side[part, CHIP_LEN:, :].astype(F32)
            scols_ref[at + 1, base : base + ROWS, :] = far_side[part, CHIP_LEN:, :].astype(F32)
        scols_ref[at + 2] = jnp.zeros((2 * ROWS, 128), F32)

    def both_parts(ref, rows):
        return jnp.concatenate([ref[0, rows, :], ref[1, rows, :]], axis=0)

    chip_rows = slice(0, CHIP_LEN)
    columns = [
        even_pair(
            both_parts(left_ref, chip_rows).astype(F32),
            both_parts(first_ref, chip_rows).astype(F32),
        ),
        odd_pair(
            both_parts(last_ref, chip_rows).astype(F32),
            both_parts(right_ref, chip_rows).astype(F32),
        ),
        jnp.concatenate(cut_pair(off_ref, scols_ref, 0, 0), axis=0),
        jnp.concatenate(cut_pair(off_ref, scols_ref, PAIRS - 1, BLOCKS - 3), axis=0),
    ]
    for copy in fetch_table:
        copy.wait()
    half = jnp.dot(
        table_ref[864:992, 0:128],
        jnp.concatenate(columns, axis=1),
        preferred_element_type=F32,
    ).astype(BF)
    spec = jnp.dot(
        side_by_side(half, (0, 1)), table_ref[0:256, :], preferred_element_type=F32
    )
    spec_sec = jnp.dot(
        side_by_side(half, (2, 3)), table_ref[256:512, :], preferred_element_type=F32
    )
    outer = correlated(spec, spec_sec, table_ref, 2)

    wide = (PAIRS, 128)
    lanes = iota(wide, 1)
    pairs = iota(wide, 0)

    def completed(ref, which):
        return jnp.where(
            pairs == 0,
            outer[0][which],
            jnp.where(pairs == PAIRS - 1, outer[1][which], ref[...]),
        )

    total = completed(tot_ref, 0)
    moment = completed(mom_ref, 1)
    lag_lane = ((lanes & 63) - LAG_COUNT // 2).astype(F32) / OVERSAMPLE
    found = []
    for side in range(2):
        mask = (lanes < 64) if side == 0 else (lanes >= 64)

        def over(values):
            return jnp.sum(jnp.where(mask, values, 0.0), axis=1, keepdims=True)

        whole = over(total) + EPS
        found.append((over(moment) / whole, over(total * lag_lane) / whole))
    own_chip = (lanes >> 1) == pairs
    even = (lanes & 1) == 0

    def spread(which):
        values = jnp.where(even, found[0][which], found[1][which])
        return jnp.sum(jnp.where(own_chip, values, 0.0), axis=0, keepdims=True)

    padded_ref[...] = jnp.zeros((8, 128), jnp.int32)
    padded_ref[0:2, 0:CHIPS] = offv_ref[...]
    offsets = padded_ref[...].astype(F32)
    est_az = offsets[0:1, :] + spread(0)
    est_rg = offsets[1:2, :] + spread(1)
    est_ref[0:1, :] = est_az
    est_ref[1:2, :] = est_rg
    angle = PHASE_RATE * est_az
    cos_all = jnp.broadcast_to(jnp.cos(angle), (8, 128))
    sin_all = jnp.broadcast_to(jnp.sin(angle), (8, 128))

    for copy in fetch:
        copy.wait()
    start_ref[...] = start_ref[...] - rg * COLS
    every = slice(0, LINES)
    edge_columns = {
        0: (
            both_parts(left_ref, own_rows),
            both_parts(first_ref, own_rows),
            both_parts(near_ref.at[0], every),
        ),
        BLOCKS - 1: (
            both_parts(near_ref.at[1], every),
            both_parts(last_ref, own_rows),
            both_parts(right_ref, own_rows),
        ),
    }

    def turned(block):
        if block in edge_columns:
            cols = edge_columns[block]
            near = jnp.concatenate(
                [half_turned(cols[0], cols[1]), half_turned(cols[1], cols[2])], axis=1
            )
            summed = jnp.dot(
                near, sinc_band(start_ref, taps_ref, block), preferred_element_type=F32
            )
        else:
            summed = sum_ref[:, block * 128 : (block + 1) * 128]
        chip = block * 4 + (iota((8, 128), 1) >> 5)
        cosine = jnp.take_along_axis(cos_all, chip, axis=1)[0:1, :]
        sine = jnp.take_along_axis(sin_all, chip, axis=1)[0:1, :]
        re, im = summed[:LINES], summed[LINES:]
        half = block // HALF
        at = slice((block - half * HALF) * 128, (block - half * HALF + 1) * 128)
        base = half * 2 * LINES
        lines_ref[base : base + LINES, at] = (re * cosine + im * sine).astype(BF)
        lines_ref[base + LINES : base + 2 * LINES, at] = (im * cosine - re * sine).astype(BF)

    copies = []
    for first in range(0, WIDTH, 256):
        at = slice(first, first + 256)
        for block in (first // 128, first // 128 + 1):
            turned(block)
            turned(block + HALF)
        packed_ref[:, at] = jnp.dot(
            pick_ref[...], lines_ref[:, at], preferred_element_type=F32
        ).astype(BF)
        copy = pltpu.make_async_copy(
            packed_ref.at[:, at], out_ref.at[:, at], out_sems.at[first // 256]
        )
        copy.start()
        copies.append(copy)
    for copy in copies:
        copy.wait()


def finish(off, *arrays):
    return pl.pallas_call(
        finish_kernel,
        out_shape=(
            jax.ShapeDtypeStruct((2, 128), F32),
            jax.ShapeDtypeStruct((OWNERS * 8, WIDTH), BF),
        ),
        in_specs=[smem] + [vmem] * 5 + [hbm] * 4 + [vmem] * 2 + [hbm] * 2,
        out_specs=(vmem, hbm),
        scratch_shapes=[
            pltpu.VMEM((2 * LINES, COLS), F32),
            pltpu.VMEM((OWNERS * 8, 4 * LINES), BF),
            pltpu.VMEM((2, 2, LINES, 128), BF),
            pltpu.VMEM((BLOCKS, 128), jnp.int32),
            pltpu.VMEM((TAP_COUNT, COLS), BF),
            pltpu.VMEM(TABLE, BF),
            pltpu.VMEM((4, 2, CHIP_LEN + ROWS, 128), BF),
            pltpu.VMEM((8, 128), jnp.int32),
            pltpu.VMEM((6, 2 * ROWS, 128), F32),
            pltpu.VMEM((4 * LINES, WIDTH), BF),
            pltpu.VMEM((OWNERS * 8, WIDTH), BF),
            pltpu.SemaphoreType.DMA((1,)),
            pltpu.SemaphoreType.DMA((6,)),
            pltpu.SemaphoreType.DMA((WIDTH // 256,)),
        ],
        compiler_params=pltpu.CompilerParams(vmem_limit_bytes=52 * 2**20),
        cost_estimate=pl.CostEstimate(
            flops=2 * 10**9, bytes_accessed=10 * 10**6, transcendentals=0
        ),
        name="finish",
    )(off, off, *arrays)


def place_kernel(pick_ref, arr_ref, out_ref):
    pick = pick_ref[...]
    for first in range(0, WIDTH, 256):
        for piece in range(PLACED):
            lines = jnp.dot(
                pick,
                arr_ref[:, piece, :, first : first + 256].reshape(128, 256),
                preferred_element_type=F32,
            ).astype(BF)
            for half in range(2):
                begin_at = piece * COLS + half * WIDTH + first
                at = slice(begin_at, begin_at + 256)
                for part in range(2):
                    base = half * 64 + part * OWNER_CAP
                    out_ref[part, :, at] = lines[base : base + OWNER_CAP, :]


def place_lines(pick, arrived):
    return pl.pallas_call(
        place_kernel,
        grid=(PIECES // PLACED,),
        out_shape=jax.ShapeDtypeStruct((2, OWNER_CAP, COLS * PIECES), BF),
        in_specs=[
            pl.BlockSpec((128, 128), lambda r: (0, 0)),
            pl.BlockSpec((TILES, PLACED, 8, WIDTH), lambda r: (0, r, 0, 0)),
        ],
        out_specs=pl.BlockSpec((2, OWNER_CAP, PLACED * COLS), lambda r: (0, 0, r)),
        compiler_params=pltpu.CompilerParams(vmem_limit_bytes=20 * 2**20),
        cost_estimate=pl.CostEstimate(
            flops=10**9, bytes_accessed=8 * 10**6, transcendentals=0
        ),
        name="place_lines",
    )(pick, arrived)


def owner_table(src_row, line_owner, me):
    tile = src_row // LINES
    owned = line_owner == me
    ids = jnp.arange(ALL_LINES, dtype=jnp.int32)
    before = owned[None, :] & (ids[None, :] < ids[:, None])
    rank = jnp.sum(before.astype(jnp.int32), axis=1)
    rank_tile = jnp.sum((before & (tile[None, :] == tile[:, None])).astype(jnp.int32), axis=1)
    outs = jnp.arange(OWNER_CAP, dtype=jnp.int32)
    hit = owned[None, :] & (rank[None, :] == outs[:, None])
    code = jnp.sum(jnp.where(hit, (tile * 2 + rank_tile + 1)[None, :], 0), axis=1) - 1
    rows = jnp.arange(128, dtype=jnp.int32)[:, None]
    cols = jnp.arange(128, dtype=jnp.int32)[None, :]
    slot = jnp.tile(code, 4)[:, None]
    pick = (
        (slot == (cols >> 3) * 2 + ((cols >> 1) & 1))
        & ((rows >> 6) == ((cols >> 2) & 1))
        & (((rows >> 5) & 1) == (cols & 1))
    )
    return pick.astype(BF)


def exchanged(axis, mate, other):
    count = lax.axis_size(axis)

    def swap(block, first):
        pairs = [(i, i + 1) for i in range(first, count - 1, 2)]
        return lax.ppermute(block, axis, pairs + [(j, i) for i, j in pairs])

    from_other = swap(other, 1)
    return swap(mate, 0), from_other


def per_device(
    reference_slc, secondary_slc, chip_offsets, src_row, line_owner, band_start, band_taps
):
    az = lax.axis_index("az")
    rg = lax.axis_index("rg")
    starts = band_start.reshape(PIECES * BLOCKS, 128)
    table = kernel_table()
    near, far = exchanged("az", *rims(secondary_slc))
    summed, pick_sent, spectra = own_side(
        secondary_slc.reshape(2 * LINES, COLS),
        starts,
        band_taps,
        src_row.reshape(ALL_LINES // 128, 128),
        line_owner.reshape(ALL_LINES // 128, 128),
        reference_slc,
        table,
    )
    sent = rg_edges(reference_slc, secondary_slc, near, far)
    got = exchanged("rg", *sent)
    off = chip_offsets[:, 0, :]
    total, moment = inner_pairs(off, secondary_slc, near, far, table, spectra)
    est, packed = finish(
        off,
        *sent,
        *got,
        secondary_slc,
        starts,
        band_taps,
        table,
        total,
        moment,
        summed,
        pick_sent,
    )
    arrived = lax.all_to_all(packed, BOTH, 0, 0, tiled=True)
    pick = owner_table(src_row, line_owner, az * PIECES + rg)
    resampled = place_lines(pick, arrived.reshape(TILES, PIECES, 8, WIDTH))
    return est[:, None, :CHIPS], resampled


def solution(mesh):
    return jax.shard_map(
        per_device,
        mesh=mesh,
        in_specs=(
            P(None, "az", "rg"),
            P(None, "az", "rg"),
            P(None, "az", "rg"),
            P(),
            P(),
            P(),
            P(),
        ),
        out_specs=(P(None, "az", "rg"), P(None, BOTH, None)),
        check_vma=False,
    )
```
